256 devices in a mesh: head: 8 (over y_lo, x), tok: 32 (over z, y_hi, core).
Axes of the slice: x: 4, y: 4 (y_hi: 2, y_lo: 2; y = y_hi * 2 + y_lo), z: 8, core: 2. Of those that a mesh axis runs over, the one named last changes fastest.
Arguments:
- queries: bfloat16 [16384, 5120], P(('tok', 'head')), may hold values from -72 to 72, as said below
- keys_in: bfloat16 [16384, 5120], P(('tok', 'head')), may hold values from -12 to 12, as said below
- values: bfloat16 [16384, 5120], P(('tok', 'head')), may hold values from -8 to 8, as said below
- grad_out: bfloat16 [16384, 5120], P(('tok', 'head')), may hold values from -192 to 192
- fine_gate: bfloat16 [16384, 40], P(('tok', 'head')), may hold values from 0.25 to 1
- coarse_gate: bfloat16 [16384, 40], P(('tok', 'head')), may hold values from 0.25 to 1
- tile_of_cube: int32 [256], replicated, may hold values from 0 to 255, as said below
- select: int32 [256, 16], replicated, may hold values from 0 to 255, as said below
Outputs:
- grad_queries: bfloat16 [16384, 5120], P(('tok', 'head'))
- grad_keys: bfloat16 [16384, 5120], P(('tok', 'head'))
- grad_values: bfloat16 [16384, 5120], P(('tok', 'head'))
The draws below stay inside these ranges and needn't reach their ends.
Inputs may be any that keep to these rules, and one draw needn't show every extreme that they name: `tile_of_cube`: A permutation: every cube has its own tile. `select`: each row lists 16 distinct cubes. Over the query cubes whose tiles lie in one block of 8 consecutive tiles, the distinct listed cubes whose tiles lie in any one block number 1 to 2; some block reaches 2 from every block. `queries`: of order one, up to 72 in magnitude. `keys_in`: of order one. `values`: of order one.
All inputs are finite; a program needn't handle non-finite values.
Results may differ from the reference program's by a relative error of at most 0.014.
Values may be sent and summed in bfloat16 or wider, within the bound.
A program may use at most 192 MiB of HBM per device.

```python
import math
import jax
import jax.numpy as jnp
from jax import lax

HEADS = 40
HDIM = 128
CUBE = 64
TOPK = 16
CUBES_DEV = 8
CUBES = 256
TOKENS = 16384
LOW = 1
CAP = 2


def layout(key):
    key = jax.random.fold_in(key, 5)
    parts = jax.random.split(key, 5)
    blocks = CUBES // CUBES_DEV
    cube_of_tile = jax.random.permutation(parts[0], CUBES).astype(jnp.int32)
    counts = LOW + jax.random.randint(parts[1], (blocks, blocks), 0, CAP - LOW + 1)
    full_row = jax.random.randint(parts[2], (), 0, blocks)
    counts = jnp.where(jnp.arange(blocks)[:, None] == full_row, CAP, counts)
    ranking = jax.random.randint(parts[3], (blocks, blocks, CUBES_DEV), 0, 2 ** 20) * CUBES_DEV + jnp.arange(CUBES_DEV)
    picked_local = jnp.argsort(ranking, axis=-1)[:, :, :CAP]
    usable = jnp.arange(CAP)[None, None, :] < counts[:, :, None]
    needed = (jnp.arange(blocks)[None, :, None] * CUBES_DEV + picked_local).reshape(blocks, blocks * CAP)
    usable = usable.reshape(blocks, blocks * CAP)
    shuffle = jax.random.randint(parts[4], (blocks, blocks * CAP), 0, 2 ** 20) * (blocks * CAP) + jnp.arange(blocks * CAP)
    priority = jnp.where(usable, shuffle + 2 ** 27, shuffle)
    ordering = jnp.argsort(-priority, axis=-1)
    listed = jnp.take_along_axis(needed, ordering, axis=-1)
    live = jnp.sum(usable.astype(jnp.int32), axis=-1)
    spots = jnp.arange(CUBES_DEV)[:, None] * TOPK + jnp.arange(TOPK)[None, :]
    spots = spots[None, :, :] % live[:, None, None]
    widened = jnp.broadcast_to(listed[:, None, :], (blocks, CUBES_DEV, blocks * CAP))
    chosen = jnp.take_along_axis(widened, spots, axis=-1).reshape(CUBES, TOPK).astype(jnp.int32)
    tile_of_cube = jnp.argsort(cube_of_tile).astype(jnp.int32)
    select = jnp.zeros((CUBES, TOPK), jnp.int32).at[cube_of_tile].set(cube_of_tile[chosen])
    return (tile_of_cube, select, chosen)


def marks(key):
    key = jax.random.fold_in(key, 9)
    first = jax.random.fold_in(key, 0)
    aligned = jax.random.randint(first, (CUBES,), 0, 16) == 0
    return aligned


def smooth_rough(key, salt):
    key = jax.random.fold_in(key, salt)
    first, second = jax.random.split(key)
    common = jax.random.truncated_normal(first, -4.0, 4.0, (CUBES, 1, HEADS * HDIM), jnp.float32)
    rough = jax.random.truncated_normal(second, -4.0, 4.0, (CUBES, CUBE, HEADS * HDIM), jnp.float32)
    return (common, rough)


def key_field(key):
    common, rough = smooth_rough(key, 13)
    field = common + rough
    evens = field[:, 0::2, :]
    odds = field[:, 1::2, :]
    return jnp.stack([evens, odds], axis=2).reshape(CUBES, CUBE, HEADS * HDIM)


def draw_tile_of_cube(key, part):
    shared = layout(key)
    return shared[0]


def draw_select(key, part):
    shared = layout(key)
    return shared[1]


def draw_keys_in(key, part):
    field = key_field(key)
    return field.reshape(TOKENS, HEADS * HDIM).astype(jnp.bfloat16)


def draw_queries(key, part):
    aligned = marks(key)
    common, rough = smooth_rough(key, 29)
    drawn = common + rough
    mixed = jnp.where(aligned[:, None, None], drawn, drawn)
    return mixed.reshape(TOKENS, HEADS * HDIM).astype(jnp.bfloat16)


def draw_values(key, part):
    common, rough = smooth_rough(key, 41)
    return (common + rough).reshape(TOKENS, HEADS * HDIM).astype(jnp.bfloat16)


def steps_of(rng, dims, cuts, low, high):
    level, own = 1.0, jax.random.fold_in(rng, 6)
    for axis_at, shards_of in cuts:
        steps = jnp.exp(jax.random.uniform(jax.random.fold_in(own, axis_at), (shards_of,), jnp.float32, low / len(cuts), high / len(cuts)))
        level = level * jnp.repeat(steps, dims[axis_at] // shards_of).reshape([-1 if axis == axis_at else 1 for axis in range(len(dims))])
    return level


def normal_values(key, shape, spread, reach, cuts=(), kind=jnp.bfloat16):
    level = steps_of(key, shape, cuts, -0.22, 0.18) if cuts else 1.0
    values = jax.random.normal(key, shape, jnp.float32) * spread * level
    return jnp.minimum(jnp.maximum(values, -reach), reach).astype(kind)


def setup_inputs(seed: int = 0) -> dict:
    streams_of = jax.random.split(jax.random.key(seed), 9)
    queries = draw_queries(jax.random.fold_in(streams_of[8], 71), 0)
    keys_in = draw_keys_in(jax.random.fold_in(streams_of[8], 71), 0)
    values = draw_values(jax.random.fold_in(streams_of[8], 71), 0)
    grad_out = normal_values(streams_of[3], (TOKENS, HEADS * HDIM), 32.0, 192.0, ((0, 256),))
    fine_gate = jnp.clip(0.25 + 0.75 * jax.random.uniform(streams_of[4], (TOKENS, HEADS), jnp.float32) ** steps_of(streams_of[4], (TOKENS, HEADS), ((0, 256),), -0.2, 0.2), 0.25, 1.0).astype(jnp.bfloat16)
    coarse_gate = jnp.clip(0.25 + 0.75 * jax.random.uniform(streams_of[5], (TOKENS, HEADS), jnp.float32) ** steps_of(streams_of[5], (TOKENS, HEADS), ((0, 256),), -0.2, 0.2), 0.25, 1.0).astype(jnp.bfloat16)
    tile_of_cube = draw_tile_of_cube(jax.random.fold_in(streams_of[8], 71), 0)
    select = draw_select(jax.random.fold_in(streams_of[8], 71), 0)
    return dict(queries=queries, keys_in=keys_in, values=values, grad_out=grad_out, fine_gate=fine_gate, coarse_gate=coarse_gate, tile_of_cube=tile_of_cube, select=select)


def rounded(array):
    return lax.optimization_barrier(array.astype(jnp.bfloat16))

def back_attention(query_rows, key_rows, value_rows, grad_rows, factor):
    query_wide = query_rows.astype(jnp.float32)
    key_wide = key_rows.astype(jnp.float32)
    value_wide = value_rows.astype(jnp.float32)
    grad_wide = grad_rows.astype(jnp.float32)
    scores = jnp.einsum('tqd,tkd->tqk', query_wide, key_wide) * factor
    probs = jax.nn.softmax(scores, axis=-1)
    probs_low = rounded(probs).astype(jnp.float32)
    dprobs = jnp.einsum('tqd,tkd->tqk', grad_wide, value_wide)
    inner = lax.optimization_barrier(jnp.sum(probs * dprobs, axis=-1, keepdims=True))
    dscores = rounded(probs * (dprobs - inner)).astype(jnp.float32)
    grad_query = jnp.einsum('tqk,tkd->tqd', dscores, key_wide) * factor
    grad_key = jnp.einsum('tqk,tqd->tkd', dscores, query_wide) * factor
    grad_value = jnp.einsum('tqk,tqd->tkd', probs_low, grad_wide)
    return (grad_query, grad_key, grad_value)

def collect(terms, chosen):
    blocks = CUBES // CUBES_DEV
    parts = terms.reshape(blocks, CUBES_DEV * TOPK, CUBE * HDIM)
    owners = chosen.reshape(blocks, CUBES_DEV * TOPK).astype(jnp.int32)

    def add_block(total, members):
        part, owner = members
        summed = jax.ops.segment_sum(part, owner, num_segments=CUBES)
        return (total + rounded(summed).astype(jnp.float32), None)
    total, _ = lax.scan(add_block, jnp.zeros((CUBES, CUBE * HDIM), jnp.float32), (parts, owners))
    return total.reshape(CUBES, CUBE, HDIM)

def reference(queries, keys_in, values, grad_out, fine_gate, coarse_gate, tile_of_cube, select):
    factor = 1.0 / math.sqrt(HDIM)
    positions = jnp.arange(CUBES, dtype=jnp.int32)
    cube_of_tile = jnp.zeros((CUBES,), jnp.int32).at[tile_of_cube.astype(jnp.int32)].set(positions)
    chosen = tile_of_cube[select[cube_of_tile]].astype(jnp.int32)

    def by_head(array):
        return array.reshape(CUBES, CUBE, HEADS, HDIM).transpose(2, 0, 1, 3)

    def gate_by_head(array):
        return array.reshape(CUBES, CUBE, HEADS).transpose(2, 0, 1)

    def one_head(members):
        query_h, key_h, value_h, grad_h, fine_h, coarse_h = members
        grad_wide = grad_h.astype(jnp.float32)
        fine_grad = rounded(fine_h.astype(jnp.float32)[:, :, None] * grad_wide)
        picked_keys = key_h[chosen].reshape(CUBES, TOPK * CUBE, HDIM)
        picked_values = value_h[chosen].reshape(CUBES, TOPK * CUBE, HDIM)
        fine_dq, key_terms, value_terms = back_attention(query_h, picked_keys, picked_values, fine_grad, factor)
        fine_dk = collect(key_terms, chosen)
        fine_dv = collect(value_terms, chosen)
        pooled_q = rounded(lax.optimization_barrier(jnp.mean(query_h.astype(jnp.float32), axis=1)))
        pooled_k = rounded(lax.optimization_barrier(jnp.mean(key_h.astype(jnp.float32), axis=1)))
        pooled_v = rounded(lax.optimization_barrier(jnp.mean(value_h.astype(jnp.float32), axis=1)))
        pooled_g = rounded(lax.optimization_barrier(jnp.sum(coarse_h.astype(jnp.float32)[:, :, None] * grad_wide, axis=1)))
        coarse_dq, coarse_dk, coarse_dv = back_attention(pooled_q[None], pooled_k[None], pooled_v[None], pooled_g[None], factor)
        grad_query = (fine_dq + coarse_dq[0][:, None, :] / CUBE).astype(jnp.bfloat16)
        grad_key = (fine_dk + coarse_dk[0][:, None, :] / CUBE).astype(jnp.bfloat16)
        grad_value = (fine_dv + coarse_dv[0][:, None, :] / CUBE).astype(jnp.bfloat16)
        return (grad_query, grad_key, grad_value)
    results = lax.map(one_head, (by_head(queries), by_head(keys_in), by_head(values), by_head(grad_out), gate_by_head(fine_gate), gate_by_head(coarse_gate)))

    def by_token(array):
        return array.transpose(1, 2, 0, 3).reshape(TOKENS, HEADS * HDIM)
    return (by_token(results[0]), by_token(results[1]), by_token(results[2]))
```

```python
import functools
import math

import jax
import jax.numpy as jnp
from jax import lax
from jax.experimental import pallas as pl
from jax.experimental.pallas import tpu as pltpu
from jax.sharding import PartitionSpec as P

MESH = pl.DeviceIdType.MESH
BF16 = jnp.bfloat16
F32 = jnp.float32

CUBE = 64
HDIM = 128
PLANES = 8
CHIPS = 16
HEADS_PLANE = 5
COPIES = 3
WORKERS = HEADS_PLANE * COPIES
WIDTH = HEADS_PLANE * HDIM
QGROUPS = 6
TOPK = 16
SLOTS = 2 * CHIPS * PLANES
UNITS = QGROUPS * PLANES
HALF = CUBE // 2
STAGES = 8
ATTEND_VMEM = 30 * 2**20
HOME_VMEM = 20 * 2**20


def where_am_i():
    tok = lax.axis_index("tok")
    head = lax.axis_index("head")
    plane = tok // 4
    chip = (tok // 2) % 2 * 8 + head
    core = tok % 2
    return plane, chip, core


def head_of(chip):
    return jnp.minimum(chip // COPIES, HEADS_PLANE - 1)


def device_of(plane, chip, core):
    return {"tok": plane * 4 + chip // 8 * 2 + core, "head": chip % 8}


def remote(src, dst, send, recv, device):
    return pltpu.make_async_remote_copy(
        src_ref=src, dst_ref=dst, send_sem=send, recv_sem=recv, device_id=device, device_id_type=MESH
    )


def take_bytes(ref, sem):
    pltpu.make_async_copy(ref, ref, sem).wait()


def greet(plane, chip, core):
    barrier = pltpu.get_barrier_semaphore()

    def along_z(d, _):
        pl.semaphore_signal(
            barrier, inc=1, device_id=device_of((plane + d) % PLANES, chip, core), device_id_type=MESH
        )
        return 0

    def in_plane(d, _):
        pl.semaphore_signal(
            barrier, inc=1, device_id=device_of(plane, (chip + d) % CHIPS, core), device_id_type=MESH
        )
        return 0

    lax.fori_loop(1, PLANES, along_z, 0)
    lax.fori_loop(1, CHIPS, in_plane, 0)
    pl.semaphore_signal(
        barrier, inc=1, device_id=device_of(plane, chip, 1 - core), device_id_type=MESH
    )
    pl.semaphore_wait(barrier, PLANES - 1 + CHIPS - 1 + 1)


def columns(group, width=WIDTH):
    return pl.ds(pl.multiple_of(group * width, 128), width)


def rows_of(half):
    return pl.ds(half * HALF, HALF)


def bring_kernel(
    k_in, v_in, q_in, g_hbm, fgate, cgate,
    kh, vh, qh, fh, ph,
    kz, vz, qz, fz, pz, fg, pg, g_in,
    gsem, zsend, zrecv, psend, krecv, qrecv, fsend, frecv,
):
    plane, chip, core = where_am_i()
    load_grad = pltpu.make_async_copy(g_hbm, g_in, gsem)
    load_grad.start()
    greet(plane, chip, core)

    def start_along_z(stage, source, landing):
        def step(d, _):
            target = (plane + d) % PLANES
            remote(
                source(target), landing(plane), zsend.at[stage], zrecv.at[stage],
                device_of(target, chip, core),
            ).start()
            return 0

        lax.fori_loop(1, PLANES, step, 0)
        pltpu.make_async_copy(source(plane), landing(plane), zrecv.at[stage]).start()

    sources = (
        lambda t, rows: k_in.at[rows, columns(t)],
        lambda t, rows: v_in.at[rows, columns(t)],
        lambda t, rows: q_in.at[rows, columns(t)],
        lambda t, rows: fg.at[t, rows],
    )
    slabs = (kz, vz, qz, fz)
    outs = (kh, vh, qh, fh)

    def start_stage(stage):
        number, rows = stage // 2, rows_of(stage % 2)
        start_along_z(
            stage, lambda t: sources[number](t, rows), lambda t: slabs[number].at[t, rows]
        )

    start_stage(0)
    start_stage(1)
    load_grad.wait()

    def gates(group, _):
        row = lax.broadcasted_iota(jnp.int32, (fgate.shape[0], WIDTH), 0)
        col = lax.broadcasted_iota(jnp.int32, (fgate.shape[0], WIDTH), 1)
        spread = jnp.where(
            row == group * HEADS_PLANE + lax.shift_right_logical(col, 7), 1.0, 0.0
        ).astype(BF16)
        grad = g_in[:, columns(group)].astype(F32)
        fine = tn(fgate[...], spread)
        fg[group] = (fine * grad).astype(BF16)
        coarse = tn(cgate[...], spread)
        pooled = jnp.sum(coarse * grad, axis=0, keepdims=True)
        rows = [pooled[:, j * HDIM:(j + 1) * HDIM] for j in range(HEADS_PLANE)]
        rows.append(jnp.zeros((16 - HEADS_PLANE, HDIM), F32))
        pg[group] = jnp.concatenate(rows, axis=0).astype(BF16)
        return 0

    lax.fori_loop(0, PLANES, gates, 0)

    def share_keys(number, rows):
        landed, out = slabs[number], outs[number]

        def step(d, _):
            target = (chip + d) % CHIPS

            @pl.when(target < WORKERS)
            def _():
                remote(
                    landed.at[:, rows, columns(head_of(target), HDIM)],
                    out.at[core * CHIPS + chip, :, rows],
                    psend.at[number], krecv.at[number, chip], device_of(plane, target, core),
                ).start()

            return 0

        lax.fori_loop(1, CHIPS, step, 0)

        @pl.when(chip < WORKERS)
        def _():
            pltpu.make_async_copy(
                landed.at[:, rows, columns(head_of(chip), HDIM)],
                out.at[core * CHIPS + chip, :, rows],
                krecv.at[number, chip],
            ).start()

    def share_queries(number, pick, place):
        def step(j, _):
            target = j * COPIES + chip % COPIES

            @pl.when(target != chip)
            def _():
                remote(
                    pick(j), place(chip // COPIES), psend.at[number],
                    qrecv.at[number - 2], device_of(plane, target, core),
                ).start()

            @pl.when(target == chip)
            def _():
                pltpu.make_async_copy(
                    pick(j), place(chip // COPIES), qrecv.at[number - 2]
                ).start()

            return 0

        lax.fori_loop(0, HEADS_PLANE, step, 0)

    for stage in range(STAGES):
        number, rows = stage // 2, rows_of(stage % 2)
        take_bytes(slabs[number].at[:, rows], zrecv.at[stage])
        if stage + 2 < STAGES:
            start_stage(stage + 2)
        if stage + 2 == STAGES:
            start_along_z(STAGES, lambda t: pg.at[t], lambda t: pz.at[t])
        if number < 2:
            share_keys(number, rows)
        else:
            share_queries(
                number,
                lambda j, number=number, rows=rows: slabs[number].at[:, rows, columns(j, HDIM)],
                lambda i, number=number, rows=rows: outs[number].at[i, :, rows],
            )
    take_bytes(pz, zrecv.at[STAGES])
    share_queries(4, lambda j: pz, lambda i: ph.at[i])

    sibling = device_of(plane, chip, 1 - core)

    @pl.when(chip < WORKERS)
    def _():
        for number, out in ((0, kh), (1, vh)):
            def forward(d, _, number=number, out=out):
                origin = (chip + CHIPS - d) % CHIPS
                block = out.at[core * CHIPS + origin]
                take_bytes(block, krecv.at[number, origin])
                remote(block, block, fsend.at[number], frecv.at[number], sibling).start()
                return 0

            lax.fori_loop(0, CHIPS, forward, 0)

        @pl.when(chip % COPIES == 0)
        def _():
            for number, out in enumerate((qh, fh, ph)):
                take_bytes(out, qrecv.at[number])

        @pl.when(chip % COPIES != 0)
        def _():
            for number, out in enumerate((qh, fh, ph)):
                take_bytes(out.at[pl.ds(0, QGROUPS - 1)], qrecv.at[number])

        for number, out in ((0, kh), (1, vh)):
            theirs = out.at[pl.ds((1 - core) * CHIPS, CHIPS)]
            take_bytes(theirs, frecv.at[number])
            take_bytes(theirs, fsend.at[number])

    for stage in range(STAGES):
        landed = slabs[stage // 2].at[pl.ds(0, PLANES - 1), rows_of(stage % 2)]
        take_bytes(landed, zsend.at[stage])
    take_bytes(pz.at[pl.ds(0, PLANES - 1)], zsend.at[STAGES])

    @pl.when(chip < WORKERS)
    def _():
        for number, out in ((0, kh), (1, vh)):
            take_bytes(out.at[pl.ds(0, WORKERS - 1)], psend.at[number])
        for number, out in ((2, qh), (3, fh), (4, ph)):
            take_bytes(out.at[pl.ds(0, HEADS_PLANE - 1)], psend.at[number])

    @pl.when(chip >= WORKERS)
    def _():
        for number, out in ((0, kh), (1, vh)):
            take_bytes(out.at[pl.ds(0, WORKERS)], psend.at[number])
        for number, out in ((2, qh), (3, fh), (4, ph)):
            take_bytes(out.at[pl.ds(0, HEADS_PLANE)], psend.at[number])


def bring(keys_in, values, queries, grad_out, fine_gate, coarse_gate):
    keys_shape = jax.ShapeDtypeStruct((2 * CHIPS, PLANES, CUBE, HDIM), BF16)
    query_shape = jax.ShapeDtypeStruct((QGROUPS, PLANES, CUBE, HDIM), BF16)
    pooled_shape = jax.ShapeDtypeStruct((QGROUPS, PLANES, 16, HDIM), BF16)
    anywhere = pl.BlockSpec(memory_space=pl.ANY)
    in_hbm = pl.BlockSpec(memory_space=pltpu.HBM)
    in_vmem = pl.BlockSpec(memory_space=pltpu.VMEM)
    slab = pltpu.VMEM((PLANES, CUBE, WIDTH), BF16)
    small = pltpu.VMEM((PLANES, 16, HDIM), BF16)
    return pl.pallas_call(
        bring_kernel,
        name="bring",
        out_shape=(keys_shape, keys_shape, query_shape, query_shape, pooled_shape),
        in_specs=[in_hbm] * 4 + [in_vmem] * 2,
        out_specs=[anywhere] * 5,
        scratch_shapes=[
            slab, slab, slab, slab, small, slab, small,
            pltpu.VMEM(grad_out.shape, BF16),
            pltpu.SemaphoreType.DMA,
            pltpu.SemaphoreType.DMA((STAGES + 1,)),
            pltpu.SemaphoreType.DMA((STAGES + 1,)),
            pltpu.SemaphoreType.DMA((5,)),
            pltpu.SemaphoreType.DMA((2, CHIPS)),
            pltpu.SemaphoreType.DMA((3,)),
            pltpu.SemaphoreType.DMA((2,)),
            pltpu.SemaphoreType.DMA((2,)),
        ],
        compiler_params=pltpu.CompilerParams(
            collective_id=0, has_side_effects=True, vmem_limit_bytes=16 * 2**20
        ),
    )(keys_in, values, queries, grad_out, fine_gate.T, coarse_gate.T)


def nt(a, b):
    return lax.dot_general(a, b, (((1,), (1,)), ((), ())), preferred_element_type=F32)


def tn(a, b):
    return lax.dot_general(a, b, (((0,), (0,)), ((), ())), preferred_element_type=F32)


def nn(a, b):
    return jnp.dot(a, b, preferred_element_type=F32)


def attend_kernel(
    toc, sel, q, fg, pg, k, v,
    dq, dk, dv,
    ak, av, pk, pv, pq, cdq, part, cot, soc,
):
    _, chip, core = where_am_i()
    head, replica = chip // COPIES, chip % COPIES
    groups = jnp.where(replica == 0, QGROUPS, QGROUPS - 1)
    groups = jnp.where(chip < WORKERS, groups, 0)
    units = groups * PLANES
    factor = 1.0 / math.sqrt(HDIM)
    log2e = math.log2(math.e)

    def invert(cube, _):
        tile = toc[cube]
        cot[tile] = cube
        soc[cube] = (
            lax.shift_left(lax.shift_right_logical(tile, 3) & 1, 7)
            + lax.shift_left(lax.shift_right_logical(tile, 4) & 1, 6)
            + lax.shift_left(tile & 7, 3)
            + lax.shift_right_logical(tile, 5)
        )
        return 0

    lax.fori_loop(0, SLOTS, invert, 0, unroll=8)

    def pool(source, groups, into):
        def gather(group, _):
            block = source[pl.ds(pl.multiple_of(group * 8, 8), 8)].astype(F32)
            halves = jnp.sum(block.reshape(8, 8, 8, HDIM), axis=1)
            part[pl.ds(pl.multiple_of(group * 64, 64), 64), :] = halves.reshape(64, HDIM)
            return 0

        lax.fori_loop(0, groups, gather, 0, unroll=2)
        count = into.shape[0]
        total = part[pl.ds(0, count, stride=8), :]
        for row in range(1, 8):
            total += part[pl.ds(row, count, stride=8), :]
        into[...] = total * (1.0 / CUBE)

    pool(k, SLOTS // 8, pk)
    pool(v, SLOTS // 8, pv)
    pool(q, UNITS // 8, pq)
    unit_at = lax.broadcasted_iota(jnp.int32, (UNITS, 16, HDIM), 0)
    row_at = lax.broadcasted_iota(jnp.int32, (UNITS, 16, HDIM), 1)
    pooled_g = jnp.sum(
        jnp.where((unit_at < units) & (row_at == head), pg[...].astype(F32), 0.0), axis=1
    ).astype(BF16)
    live = lax.broadcasted_iota(jnp.int32, (UNITS, HDIM), 0) < units
    pooled_q = jnp.where(live, pq[...], 0.0).astype(BF16)
    pooled_k = pk[...].astype(BF16)
    pooled_v = pv[...].astype(BF16)
    scores = nt(pooled_q, pooled_k) * factor
    weights = jnp.exp(scores - jnp.max(scores, axis=1, keepdims=True))
    probs = weights / jnp.sum(weights, axis=1, keepdims=True)
    dprobs = nt(pooled_g, pooled_v)
    inner = jnp.sum(probs * dprobs, axis=1, keepdims=True)
    dscores = (probs * (dprobs - inner)).astype(BF16)
    cdq[...] = nn(dscores, pooled_k) * (factor / CUBE)
    pk[...] = tn(dscores, pooled_q) * (1.0 / CUBE)
    pv[...] = tn(probs.astype(BF16), pooled_g) * (1.0 / CUBE)

    def fill(slot, _):
        ak[slot] = jnp.broadcast_to(pk[pl.ds(slot, 1), :], (CUBE, HDIM))
        av[slot] = jnp.broadcast_to(pv[pl.ds(slot, 1), :], (CUBE, HDIM))
        return 0

    lax.fori_loop(0, SLOTS, fill, 0, unroll=4)

    def listed(n):
        origin = n // PLANES * COPIES + replica
        tile = ((n % PLANES * 4) + origin // 8 * 2 + core) * 8 + origin % 8
        cube = cot[tile]
        slots = [soc[sel[r, cube]] for r in range(TOPK)]
        return [slots[c * 4:c * 4 + 4] for c in range(4)]

    def tiles_of(ref, quarter):
        return jnp.concatenate([ref[s] for s in quarter], axis=0)

    def softmax_terms(n, quarters):
        score = [nt(q[n], tiles_of(k, quarter)) for quarter in quarters]
        dprob = [nt(fg[n], tiles_of(v, quarter)) for quarter in quarters]
        top = functools.reduce(jnp.maximum, score)
        top = jnp.max(top, axis=1, keepdims=True)
        weight = [jnp.exp2((s - top) * (factor * log2e)) for s in score]
        total = jnp.sum(functools.reduce(jnp.add, weight), axis=1, keepdims=True)
        inverse = 1.0 / total
        mixed = functools.reduce(jnp.add, [w * d for w, d in zip(weight, dprob)])
        center = jnp.sum(mixed, axis=1, keepdims=True) * inverse
        probs = [w * inverse for w in weight]
        dscore = [(p * (d - center)).astype(BF16) for p, d in zip(probs, dprob)]
        return [p.astype(BF16) for p in probs], dscore

    def spread_terms(n, quarters, probs, dscore):
        query, grad = q[n], fg[n]
        dquery = jnp.zeros((CUBE, HDIM), F32)
        for c, quarter in enumerate(quarters):
            dquery += nn(dscore[c], tiles_of(k, quarter))
            key_terms = tn(dscore[c], query)
            value_terms = tn(probs[c], grad)
            for i, s in enumerate(quarter):
                ak[s] += key_terms[i * CUBE:(i + 1) * CUBE]
                av[s] += value_terms[i * CUBE:(i + 1) * CUBE]
        dq[n] = (dquery * factor + cdq[pl.ds(n, 1), :]).astype(BF16)

    def pair(m, _):
        numbers = [2 * m, 2 * m + 1]
        lists = [listed(n) for n in numbers]
        terms = [softmax_terms(n, quarters) for n, quarters in zip(numbers, lists)]
        for n, quarters, (probs, dscore) in zip(numbers, lists, terms):
            spread_terms(n, quarters, probs, dscore)
        return 0

    lax.fori_loop(0, units // 2, pair, 0)

    def finish(group, _):
        rows = pl.ds(pl.multiple_of(group * 4, 4), 4)
        dk[rows] = (ak[rows] * factor).astype(BF16)
        dv[rows] = av[rows].astype(BF16)
        return 0

    lax.fori_loop(0, SLOTS // 4, finish, 0)


def attend(tile_of_cube, select, qh, fh, ph, kh, vh):
    smem = pl.BlockSpec(memory_space=pltpu.SMEM)
    vmem = pl.BlockSpec(memory_space=pltpu.VMEM)
    query_shape = jax.ShapeDtypeStruct((UNITS, CUBE, HDIM), BF16)
    keys_shape = jax.ShapeDtypeStruct((SLOTS, CUBE, HDIM), BF16)
    return pl.pallas_call(
        attend_kernel,
        name="attend",
        out_shape=(query_shape, keys_shape, keys_shape),
        in_specs=[smem] * 2 + [vmem] * 5,
        out_specs=[vmem] * 3,
        scratch_shapes=[
            pltpu.VMEM((SLOTS, CUBE, HDIM), F32),
            pltpu.VMEM((SLOTS, CUBE, HDIM), F32),
            pltpu.VMEM((SLOTS, HDIM), F32),
            pltpu.VMEM((SLOTS, HDIM), F32),
            pltpu.VMEM((UNITS, HDIM), F32),
            pltpu.VMEM((UNITS, HDIM), F32),
            pltpu.VMEM((SLOTS * 8, HDIM), F32),
            pltpu.SMEM((SLOTS,), jnp.int32),
            pltpu.SMEM((SLOTS,), jnp.int32),
        ],
        compiler_params=pltpu.CompilerParams(vmem_limit_bytes=ATTEND_VMEM),
    )(
        tile_of_cube, select.T,
        qh.reshape(UNITS, CUBE, HDIM), fh.reshape(UNITS, CUBE, HDIM),
        ph.reshape(UNITS, 16, HDIM), kh.reshape(SLOTS, CUBE, HDIM), vh.reshape(SLOTS, CUBE, HDIM),
    )


def home_kernel(
    dq, dk, dv,
    oq, ok, ov,
    own_k, own_v, sib_k, sib_v, land_q, land_k, land_v, sum_k, sum_v,
    ssend, srecv, psend, precv, zsend, zrecv,
):
    plane, chip, core = where_am_i()
    head, replica = head_of(chip), chip % COPIES
    works = chip < WORKERS
    greet(plane, chip, core)
    sibling = device_of(plane, chip, 1 - core)
    sources, owns, sibs = (dk, dv), (own_k, own_v), (sib_k, sib_v)
    lands, sums, outs = (land_k, land_v), (sum_k, sum_v), (ok, ov)
    spread = columns(head, HDIM)
    mine = columns(plane)

    @pl.when(works)
    def _():
        for number in range(2):
            def give(d, _, number=number):
                target = (chip + d) % CHIPS
                remote(
                    sources[number].at[(1 - core) * CHIPS + target], sibs[number].at[target],
                    ssend.at[number], srecv.at[number, target], sibling,
                ).start()
                return 0

            lax.fori_loop(0, CHIPS, give, 0)

        def send_query(i, _):
            wanted = i * COPIES + replica
            target = jnp.minimum(wanted, CHIPS - 1)

            @pl.when((wanted < CHIPS) & (target != chip))
            def _():
                remote(
                    dq.at[i], land_q.at[:, :, spread], psend.at[2], precv.at[4],
                    device_of(plane, target, core),
                ).start()

            @pl.when(wanted == chip)
            def _():
                pltpu.make_async_copy(dq.at[i], land_q.at[:, :, spread], precv.at[4]).start()

            return 0

        lax.fori_loop(0, QGROUPS, send_query, 0)

    def settle(number, half):
        rows = rows_of(half)
        source, own, sib, land = sources[number], owns[number], sibs[number], lands[number]

        def step(d, _):
            target = (chip + d) % CHIPS
            if half == 0:
                take_bytes(sib.at[target], srecv.at[number, target])
            own[target, :, rows] = (
                source[core * CHIPS + target, :, rows].astype(F32)
                + sib[target, :, rows].astype(F32)
            ).astype(BF16)
            arrived = precv.at[number * 2 + half]

            @pl.when(target != chip)
            def _():
                remote(
                    own.at[target, :, rows], land.at[replica, :, rows, spread], psend.at[number],
                    arrived, device_of(plane, target, core),
                ).start()

            @pl.when(target == chip)
            def _():
                pltpu.make_async_copy(
                    own.at[target, :, rows], land.at[replica, :, rows, spread], arrived
                ).start()

            return 0

        @pl.when(works)
        def _():
            lax.fori_loop(0, CHIPS, step, 0)

    def send_home(number, block, out, target):
        @pl.when(target != plane)
        def _():
            remote(
                block, out, zsend.at[number], zrecv.at[number], device_of(target, chip, core)
            ).start()

        @pl.when(target == plane)
        def _():
            pltpu.make_async_copy(block, out, zrecv.at[number]).start()

    def queries_home():
        take_bytes(land_q, precv.at[4])

        def step(d, _):
            target = (plane + d) % PLANES
            send_home(2, land_q.at[target], oq.at[:, mine], target)
            return 0

        lax.fori_loop(0, PLANES, step, 0)

    def keys_home(number, half):
        rows = rows_of(half)
        land, total, out = lands[number], sums[number], outs[number]
        take_bytes(land.at[:, :, rows], precv.at[number * 2 + half])

        def step(d, _):
            target = (plane + d) % PLANES
            summed = land[0, target, rows].astype(F32)
            for r in range(1, COPIES):
                summed += land[r, target, rows].astype(F32)
            total[target, rows] = summed.astype(BF16)
            send_home(number, total.at[target, rows], out.at[rows, mine], target)
            return 0

        lax.fori_loop(0, PLANES, step, 0)

    settle(0, 0)
    settle(0, 1)
    queries_home()
    keys_home(0, 0)
    settle(1, 0)
    keys_home(0, 1)
    settle(1, 1)
    keys_home(1, 0)
    keys_home(1, 1)

    for number, out in enumerate((ok, ov, oq)):
        take_bytes(out, zrecv.at[number])
        take_bytes(land_q.at[pl.ds(0, PLANES - 1)], zsend.at[number])

    @pl.when(works)
    def _():
        for number in range(2):
            take_bytes(sibs[number], ssend.at[number])
            take_bytes(owns[number].at[pl.ds(0, CHIPS - 1)], psend.at[number])

        @pl.when(replica == 0)
        def _():
            take_bytes(dq.at[pl.ds(0, QGROUPS - 1)], psend.at[2])

        @pl.when(replica != 0)
        def _():
            take_bytes(dq.at[pl.ds(0, QGROUPS - 2)], psend.at[2])


def home(dq, dk, dv, rows, width):
    anywhere = pl.BlockSpec(memory_space=pl.ANY)
    in_vmem = pl.BlockSpec(memory_space=pltpu.VMEM)
    out_shape = jax.ShapeDtypeStruct((rows, width), BF16)
    half = pltpu.VMEM((CHIPS, PLANES, CUBE, HDIM), BF16)
    slab = pltpu.VMEM((PLANES, CUBE, WIDTH), BF16)
    slabs = pltpu.VMEM((COPIES, PLANES, CUBE, WIDTH), BF16)
    return pl.pallas_call(
        home_kernel,
        name="home",
        out_shape=(out_shape,) * 3,
        in_specs=[anywhere, in_vmem, in_vmem],
        out_specs=[anywhere] * 3,
        scratch_shapes=[
            half, half, half, half, slab, slabs, slabs, slab, slab,
            pltpu.SemaphoreType.DMA((2,)),
            pltpu.SemaphoreType.DMA((2, CHIPS)),
            pltpu.SemaphoreType.DMA((3,)),
            pltpu.SemaphoreType.DMA((5,)),
            pltpu.SemaphoreType.DMA((3,)),
            pltpu.SemaphoreType.DMA((3,)),
        ],
        compiler_params=pltpu.CompilerParams(
            collective_id=1, has_side_effects=True, vmem_limit_bytes=HOME_VMEM
        ),
    )(
        dq.reshape(QGROUPS, PLANES, CUBE, HDIM),
        dk.reshape(2 * CHIPS, PLANES, CUBE, HDIM),
        dv.reshape(2 * CHIPS, PLANES, CUBE, HDIM),
    )


def on_device(queries, keys_in, values, grad_out, fine_gate, coarse_gate, tile_of_cube, select):
    kh, vh, qh, fh, ph = bring(keys_in, values, queries, grad_out, fine_gate, coarse_gate)
    dq, dk, dv = attend(tile_of_cube, select, qh, fh, ph, kh, vh)
    return home(dq, dk, dv, *queries.shape)


def solution(mesh):
    split = P(("tok", "head"), None)
    return jax.shard_map(
        on_device,
        mesh=mesh,
        in_specs=(split,) * 6 + (P(), P()),
        out_specs=(split,) * 3,
        check_vma=False,
    )
```

```python
import functools
import math

import jax
import jax.numpy as jnp
from jax import lax
from jax.experimental import pallas as pl
from jax.experimental.pallas import tpu as pltpu
from jax.sharding import PartitionSpec as P

MESH = pl.DeviceIdType.MESH
BF16 = jnp.bfloat16
F32 = jnp.float32

CUBE = 64
HDIM = 128
PLANES = 8
CHIPS = 16
HEADS_PLANE = 5
COPIES = 3
WORKERS = HEADS_PLANE * COPIES
WIDTH = HEADS_PLANE * HDIM
QGROUPS = 6
TOPK = 16
SLOTS = 2 * CHIPS * PLANES
UNITS = QGROUPS * PLANES
HALF = CUBE // 2
STAGES = 8
ATTEND_VMEM = 30 * 2**20
HOME_VMEM = 20 * 2**20
BRING_VMEM = 16 * 2**20


def where_am_i():
    tok = lax.axis_index("tok")
    head = lax.axis_index("head")
    plane = tok // 4
    chip = (tok // 2) % 2 * 8 + head
    core = tok % 2
    return plane, chip, core


def head_of(chip):
    return jnp.minimum(chip // COPIES, HEADS_PLANE - 1)


def device_of(plane, chip, core):
    return {"tok": plane * 4 + chip // 8 * 2 + core, "head": chip % 8}


def remote(src, dst, send, recv, device):
    return pltpu.make_async_remote_copy(
        src_ref=src, dst_ref=dst, send_sem=send, recv_sem=recv, device_id=device, device_id_type=MESH
    )


def take_bytes(ref, sem):
    pltpu.make_async_copy(ref, ref, sem).wait()


def greet(plane, chip, core):
    barrier = pltpu.get_barrier_semaphore()

    def along_z(d, _):
        pl.semaphore_signal(
            barrier, inc=1, device_id=device_of((plane + d) % PLANES, chip, core), device_id_type=MESH
        )
        return 0

    def in_plane(d, _):
        pl.semaphore_signal(
            barrier, inc=1, device_id=device_of(plane, (chip + d) % CHIPS, core), device_id_type=MESH
        )
        return 0

    lax.fori_loop(1, PLANES, along_z, 0)
    lax.fori_loop(1, CHIPS, in_plane, 0)
    pl.semaphore_signal(
        barrier, inc=1, device_id=device_of(plane, chip, 1 - core), device_id_type=MESH
    )
    pl.semaphore_wait(barrier, PLANES - 1 + CHIPS - 1 + 1)


def columns(group, width=WIDTH):
    return pl.ds(pl.multiple_of(group * width, 128), width)


def rows_of(half):
    return pl.ds(half * HALF, HALF)


def bring_kernel(
    k_in, v_in, q_in, g_in, fgate, cgate,
    kh, vh, qh, fh, ph,
    packed, kz, vz, qz, fz, pz, pg,
    zsend, zrecv, psend, krecv, qrecv, fsend, frecv,
):
    plane, chip, core = where_am_i()
    greet(plane, chip, core)

    def start_along_z(stage, source, landing):
        def step(d, _):
            target = (plane + d) % PLANES
            remote(
                source(target), landing(plane), zsend.at[stage], zrecv.at[stage],
                device_of(target, chip, core),
            ).start()
            return 0

        lax.fori_loop(1, PLANES, step, 0)
        pltpu.make_async_copy(source(plane), landing(plane), zrecv.at[stage]).start()

    slabs = (kz, vz, qz, fz)
    outs = (kh, vh, qh, fh)

    def start_stage(stage):
        number, rows = stage // 2, rows_of(stage % 2)
        start_along_z(
            stage,
            lambda t: packed.at[number, t, :, rows],
            lambda t: slabs[number].at[:, t, rows],
        )

    def pack(number, source):
        def step(group, _):
            for j in range(HEADS_PLANE):
                packed[number, group, j] = source[:, columns(group * HEADS_PLANE + j, HDIM)]
            return 0

        lax.fori_loop(0, PLANES, step, 0)

    pack(0, k_in)
    start_stage(0)
    start_stage(1)
    pack(1, v_in)
    pack(2, q_in)

    def gates(group, _):
        row = lax.broadcasted_iota(jnp.int32, (fgate.shape[0], WIDTH), 0)
        col = lax.broadcasted_iota(jnp.int32, (fgate.shape[0], WIDTH), 1)
        spread = jnp.where(
            row == group * HEADS_PLANE + lax.shift_right_logical(col, 7), 1.0, 0.0
        ).astype(BF16)
        grad = g_in[:, columns(group)].astype(F32)
        fine = (tn(fgate[...], spread) * grad).astype(BF16)
        coarse = tn(cgate[...], spread)
        pooled = jnp.sum(coarse * grad, axis=0, keepdims=True)
        rows = []
        for j in range(HEADS_PLANE):
            packed[3, group, j] = fine[:, j * HDIM:(j + 1) * HDIM]
            rows.append(pooled[:, j * HDIM:(j + 1) * HDIM])
        rows.append(jnp.zeros((16 - HEADS_PLANE, HDIM), F32))
        pg[group] = jnp.concatenate(rows, axis=0).astype(BF16)
        return 0

    lax.fori_loop(0, PLANES, gates, 0)

    def share_keys(number, rows):
        landed, out = slabs[number], outs[number]

        def step(d, _):
            target = (chip + d) % CHIPS

            @pl.when(target < WORKERS)
            def _():
                remote(
                    landed.at[head_of(target), :, rows],
                    out.at[core * CHIPS + chip, :, rows],
                    psend.at[number], krecv.at[number, chip], device_of(plane, target, core),
                ).start()

            return 0

        lax.fori_loop(1, CHIPS, step, 0)

        @pl.when(chip < WORKERS)
        def _():
            pltpu.make_async_copy(
                landed.at[head_of(chip), :, rows],
                out.at[core * CHIPS + chip, :, rows],
                krecv.at[number, chip],
            ).start()

    def share_queries(number, pick, place):
        def step(j, _):
            target = j * COPIES + chip % COPIES

            @pl.when(target != chip)
            def _():
                remote(
                    pick(j), place(chip // COPIES), psend.at[number],
                    qrecv.at[number - 2], device_of(plane, target, core),
                ).start()

            @pl.when(target == chip)
            def _():
                pltpu.make_async_copy(
                    pick(j), place(chip // COPIES), qrecv.at[number - 2]
                ).start()

            return 0

        lax.fori_loop(0, HEADS_PLANE, step, 0)

    for stage in range(STAGES):
        number, rows = stage // 2, rows_of(stage % 2)
        take_bytes(slabs[number].at[:, :, rows], zrecv.at[stage])
        if stage + 2 < STAGES:
            start_stage(stage + 2)
        if stage + 2 == STAGES:
            start_along_z(STAGES, lambda t: pg.at[t], lambda t: pz.at[t])
        if number < 2:
            share_keys(number, rows)
        else:
            share_queries(
                number,
                lambda j, number=number, rows=rows: slabs[number].at[j, :, rows],
                lambda i, number=number, rows=rows: outs[number].at[i, :, rows],
            )
    take_bytes(pz, zrecv.at[STAGES])
    share_queries(4, lambda j: pz, lambda i: ph.at[i])

    sibling = device_of(plane, chip, 1 - core)

    @pl.when(chip < WORKERS)
    def _():
        for number, out in ((0, kh), (1, vh)):
            def forward(d, _, number=number, out=out):
                origin = (chip + CHIPS - d) % CHIPS
                block = out.at[core * CHIPS + origin]
                take_bytes(block, krecv.at[number, origin])
                remote(block, block, fsend.at[number], frecv.at[number], sibling).start()
                return 0

            lax.fori_loop(0, CHIPS, forward, 0)

        @pl.when(chip % COPIES == 0)
        def _():
            for number, out in enumerate((qh, fh, ph)):
                take_bytes(out, qrecv.at[number])

        @pl.when(chip % COPIES != 0)
        def _():
            for number, out in enumerate((qh, fh, ph)):
                take_bytes(out.at[pl.ds(0, QGROUPS - 1)], qrecv.at[number])

        for number, out in ((0, kh), (1, vh)):
            theirs = out.at[pl.ds((1 - core) * CHIPS, CHIPS)]
            take_bytes(theirs, frecv.at[number])
            take_bytes(theirs, fsend.at[number])

    for stage in range(STAGES):
        landed = slabs[stage // 2].at[:, pl.ds(0, PLANES - 1), rows_of(stage % 2)]
        take_bytes(landed, zsend.at[stage])
    take_bytes(pz.at[pl.ds(0, PLANES - 1)], zsend.at[STAGES])

    @pl.when(chip < WORKERS)
    def _():
        for number, out in ((0, kh), (1, vh)):
            take_bytes(out.at[pl.ds(0, WORKERS - 1)], psend.at[number])
        for number, out in ((2, qh), (3, fh), (4, ph)):
            take_bytes(out.at[pl.ds(0, HEADS_PLANE - 1)], psend.at[number])

    @pl.when(chip >= WORKERS)
    def _():
        for number, out in ((0, kh), (1, vh)):
            take_bytes(out.at[pl.ds(0, WORKERS)], psend.at[number])
        for number, out in ((2, qh), (3, fh), (4, ph)):
            take_bytes(out.at[pl.ds(0, HEADS_PLANE)], psend.at[number])


def bring(keys_in, values, queries, grad_out, fine_gate, coarse_gate):
    keys_shape = jax.ShapeDtypeStruct((2 * CHIPS, PLANES, CUBE, HDIM), BF16)
    query_shape = jax.ShapeDtypeStruct((QGROUPS, PLANES, CUBE, HDIM), BF16)
    pooled_shape = jax.ShapeDtypeStruct((QGROUPS, PLANES, 16, HDIM), BF16)
    anywhere = pl.BlockSpec(memory_space=pl.ANY)
    in_vmem = pl.BlockSpec(memory_space=pltpu.VMEM)
    slab = pltpu.VMEM((HEADS_PLANE, PLANES, CUBE, HDIM), BF16)
    small = pltpu.VMEM((PLANES, 16, HDIM), BF16)
    return pl.pallas_call(
        bring_kernel,
        name="bring",
        out_shape=(keys_shape, keys_shape, query_shape, query_shape, pooled_shape),
        in_specs=[in_vmem] * 6,
        out_specs=[anywhere] * 5,
        scratch_shapes=[
            pltpu.VMEM((4, PLANES, HEADS_PLANE, CUBE, HDIM), BF16),
            slab, slab, slab, slab, small, small,
            pltpu.SemaphoreType.DMA((STAGES + 1,)),
            pltpu.SemaphoreType.DMA((STAGES + 1,)),
            pltpu.SemaphoreType.DMA((5,)),
            pltpu.SemaphoreType.DMA((2, CHIPS)),
            pltpu.SemaphoreType.DMA((3,)),
            pltpu.SemaphoreType.DMA((2,)),
            pltpu.SemaphoreType.DMA((2,)),
        ],
        compiler_params=pltpu.CompilerParams(
            collective_id=0, has_side_effects=True, vmem_limit_bytes=BRING_VMEM
        ),
    )(keys_in, values, queries, grad_out, fine_gate.T, coarse_gate.T)


def nt(a, b):
    return lax.dot_general(a, b, (((1,), (1,)), ((), ())), preferred_element_type=F32)


def tn(a, b):
    return lax.dot_general(a, b, (((0,), (0,)), ((), ())), preferred_element_type=F32)


def nn(a, b):
    return jnp.dot(a, b, preferred_element_type=F32)


def attend_kernel(
    toc, sel, q, fg, pg, k, v,
    dq, dk, dv,
    ak, av, pk, pv, pq, cdq, part, cot, soc,
):
    _, chip, core = where_am_i()
    head, replica = chip // COPIES, chip % COPIES
    groups = jnp.where(replica == 0, QGROUPS, QGROUPS - 1)
    groups = jnp.where(chip < WORKERS, groups, 0)
    units = groups * PLANES
    factor = 1.0 / math.sqrt(HDIM)
    log2e = math.log2(math.e)

    def invert(cube, _):
        tile = toc[cube]
        cot[tile] = cube
        soc[cube] = (
            lax.shift_left(lax.shift_right_logical(tile, 3) & 1, 7)
            + lax.shift_left(lax.shift_right_logical(tile, 4) & 1, 6)
            + lax.shift_left(tile & 7, 3)
            + lax.shift_right_logical(tile, 5)
        )
        return 0

    lax.fori_loop(0, SLOTS, invert, 0, unroll=8)

    def pool(source, groups, into):
        def gather(group, _):
            block = source[pl.ds(pl.multiple_of(group * 8, 8), 8)].astype(F32)
            halves = jnp.sum(block.reshape(8, 8, 8, HDIM), axis=1)
            part[pl.ds(pl.multiple_of(group * 64, 64), 64), :] = halves.reshape(64, HDIM)
            return 0

        lax.fori_loop(0, groups, gather, 0, unroll=2)
        count = into.shape[0]
        total = part[pl.ds(0, count, stride=8), :]
        for row in range(1, 8):
            total += part[pl.ds(row, count, stride=8), :]
        into[...] = total * (1.0 / CUBE)

    pool(k, SLOTS // 8, pk)
    pool(v, SLOTS // 8, pv)
    pool(q, UNITS // 8, pq)
    unit_at = lax.broadcasted_iota(jnp.int32, (UNITS, 16, HDIM), 0)
    row_at = lax.broadcasted_iota(jnp.int32, (UNITS, 16, HDIM), 1)
    pooled_g = jnp.sum(
        jnp.where((unit_at < units) & (row_at == head), pg[...].astype(F32), 0.0), axis=1
    ).astype(BF16)
    live = lax.broadcasted_iota(jnp.int32, (UNITS, HDIM), 0) < units
    pooled_q = jnp.where(live, pq[...], 0.0).astype(BF16)
    pooled_k = pk[...].astype(BF16)
    pooled_v = pv[...].astype(BF16)
    scores = nt(pooled_q, pooled_k) * factor
    weights = jnp.exp(scores - jnp.max(scores, axis=1, keepdims=True))
    probs = weights / jnp.sum(weights, axis=1, keepdims=True)
    dprobs = nt(pooled_g, pooled_v)
    inner = jnp.sum(probs * dprobs, axis=1, keepdims=True)
    dscores = (probs * (dprobs - inner)).astype(BF16)
    cdq[...] = nn(dscores, pooled_k) * (factor / CUBE)
    pk[...] = tn(dscores, pooled_q) * (1.0 / CUBE)
    pv[...] = tn(probs.astype(BF16), pooled_g) * (1.0 / CUBE)

    def fill(slot, _):
        ak[slot] = jnp.broadcast_to(pk[pl.ds(slot, 1), :], (CUBE, HDIM))
        av[slot] = jnp.broadcast_to(pv[pl.ds(slot, 1), :], (CUBE, HDIM))
        return 0

    lax.fori_loop(0, SLOTS, fill, 0, unroll=4)

    def listed(n):
        origin = n // PLANES * COPIES + replica
        tile = ((n % PLANES * 4) + origin // 8 * 2 + core) * 8 + origin % 8
        cube = cot[tile]
        slots = [soc[sel[r, cube]] for r in range(TOPK)]
        return [slots[c * 4:c * 4 + 4] for c in range(4)]

    def tiles_of(ref, quarter):
        return jnp.concatenate([ref[s] for s in quarter], axis=0)

    def softmax_terms(n, quarters):
        score = [nt(q[n], tiles_of(k, quarter)) for quarter in quarters]
        dprob = [nt(fg[n], tiles_of(v, quarter)) for quarter in quarters]
        top = functools.reduce(jnp.maximum, score)
        top = jnp.max(top, axis=1, keepdims=True)
        weight = [jnp.exp2((s - top) * (factor * log2e)) for s in score]
        total = jnp.sum(functools.reduce(jnp.add, weight), axis=1, keepdims=True)
        inverse = 1.0 / total
        mixed = functools.reduce(jnp.add, [w * d for w, d in zip(weight, dprob)])
        center = jnp.sum(mixed, axis=1, keepdims=True) * inverse
        probs = [w * inverse for w in weight]
        dscore = [(p * (d - center)).astype(BF16) for p, d in zip(probs, dprob)]
        return [p.astype(BF16) for p in probs], dscore

    def spread_terms(n, quarters, probs, dscore):
        query, grad = q[n], fg[n]
        dquery = jnp.zeros((CUBE, HDIM), F32)
        for c, quarter in enumerate(quarters):
            dquery += nn(dscore[c], tiles_of(k, quarter))
            key_terms = tn(dscore[c], query)
            value_terms = tn(probs[c], grad)
            for i, s in enumerate(quarter):
                ak[s] += key_terms[i * CUBE:(i + 1) * CUBE]
                av[s] += value_terms[i * CUBE:(i + 1) * CUBE]
        dq[n] = (dquery * factor + cdq[pl.ds(n, 1), :]).astype(BF16)

    def pair(m, _):
        numbers = [2 * m, 2 * m + 1]
        lists = [listed(n) for n in numbers]
        terms = [softmax_terms(n, quarters) for n, quarters in zip(numbers, lists)]
        for n, quarters, (probs, dscore) in zip(numbers, lists, terms):
            spread_terms(n, quarters, probs, dscore)
        return 0

    lax.fori_loop(0, units // 2, pair, 0)

    def finish(group, _):
        rows = pl.ds(pl.multiple_of(group * 4, 4), 4)
        dk[rows] = (ak[rows] * factor).astype(BF16)
        dv[rows] = av[rows].astype(BF16)
        return 0

    lax.fori_loop(0, SLOTS // 4, finish, 0)


def attend(tile_of_cube, select, qh, fh, ph, kh, vh):
    smem = pl.BlockSpec(memory_space=pltpu.SMEM)
    vmem = pl.BlockSpec(memory_space=pltpu.VMEM)
    query_shape = jax.ShapeDtypeStruct((UNITS, CUBE, HDIM), BF16)
    keys_shape = jax.ShapeDtypeStruct((SLOTS, CUBE, HDIM), BF16)
    return pl.pallas_call(
        attend_kernel,
        name="attend",
        out_shape=(query_shape, keys_shape, keys_shape),
        in_specs=[smem] * 2 + [vmem] * 5,
        out_specs=[vmem] * 3,
        scratch_shapes=[
            pltpu.VMEM((SLOTS, CUBE, HDIM), F32),
            pltpu.VMEM((SLOTS, CUBE, HDIM), F32),
            pltpu.VMEM((SLOTS, HDIM), F32),
            pltpu.VMEM((SLOTS, HDIM), F32),
            pltpu.VMEM((UNITS, HDIM), F32),
            pltpu.VMEM((UNITS, HDIM), F32),
            pltpu.VMEM((SLOTS * 8, HDIM), F32),
            pltpu.SMEM((SLOTS,), jnp.int32),
            pltpu.SMEM((SLOTS,), jnp.int32),
        ],
        compiler_params=pltpu.CompilerParams(vmem_limit_bytes=ATTEND_VMEM),
    )(
        tile_of_cube, select.T,
        qh.reshape(UNITS, CUBE, HDIM), fh.reshape(UNITS, CUBE, HDIM),
        ph.reshape(UNITS, 16, HDIM), kh.reshape(SLOTS, CUBE, HDIM), vh.reshape(SLOTS, CUBE, HDIM),
    )


def home_kernel(
    dq, dk, dv,
    oq, ok, ov,
    own_k, own_v, sib_k, sib_v, land_q, land_k, land_v, sum_k, sum_v, sum_q,
    ssend, srecv, psend, precv, zsend, zrecv,
):
    plane, chip, core = where_am_i()
    head, replica = head_of(chip), chip % COPIES
    works = chip < WORKERS
    greet(plane, chip, core)
    sibling = device_of(plane, chip, 1 - core)
    sources, owns, sibs = (dk, dv), (own_k, own_v), (sib_k, sib_v)
    lands, sums, outs = (land_k, land_v), (sum_k, sum_v), (ok, ov)
    mine = columns(plane)

    @pl.when(works)
    def _():
        for number in range(2):
            def give(d, _, number=number):
                target = (chip + d) % CHIPS
                remote(
                    sources[number].at[(1 - core) * CHIPS + target], sibs[number].at[target],
                    ssend.at[number], srecv.at[number, target], sibling,
                ).start()
                return 0

            lax.fori_loop(0, CHIPS, give, 0)

        def send_query(i, _):
            wanted = i * COPIES + replica
            target = jnp.minimum(wanted, CHIPS - 1)

            @pl.when((wanted < CHIPS) & (target != chip))
            def _():
                remote(
                    dq.at[i], land_q.at[head], psend.at[2], precv.at[4],
                    device_of(plane, target, core),
                ).start()

            @pl.when(wanted == chip)
            def _():
                pltpu.make_async_copy(dq.at[i], land_q.at[head], precv.at[4]).start()

            return 0

        lax.fori_loop(0, QGROUPS, send_query, 0)

    def settle(number, half):
        rows = rows_of(half)
        source, own, sib, land = sources[number], owns[number], sibs[number], lands[number]

        def step(d, _):
            target = (chip + d) % CHIPS
            if half == 0:
                take_bytes(sib.at[target], srecv.at[number, target])
            own[target, :, rows] = (
                source[core * CHIPS + target, :, rows].astype(F32)
                + sib[target, :, rows].astype(F32)
            ).astype(BF16)
            arrived = precv.at[number * 2 + half]

            @pl.when(target != chip)
            def _():
                remote(
                    own.at[target, :, rows], land.at[replica, head, :, rows], psend.at[number],
                    arrived, device_of(plane, target, core),
                ).start()

            @pl.when(target == chip)
            def _():
                pltpu.make_async_copy(
                    own.at[target, :, rows], land.at[replica, head, :, rows], arrived
                ).start()

            return 0

        @pl.when(works)
        def _():
            lax.fori_loop(0, CHIPS, step, 0)

    def send_home(number, block, out, target):
        @pl.when(target != plane)
        def _():
            remote(
                block, out, zsend.at[number], zrecv.at[number], device_of(target, chip, core)
            ).start()

        @pl.when(target == plane)
        def _():
            pltpu.make_async_copy(block, out, zrecv.at[number]).start()

    def queries_home():
        take_bytes(land_q, precv.at[4])

        def step(d, _):
            target = (plane + d) % PLANES
            for j in range(HEADS_PLANE):
                sum_q[target, :, j * HDIM:(j + 1) * HDIM] = land_q[j, target]
            send_home(2, sum_q.at[target], oq.at[:, mine], target)
            return 0

        lax.fori_loop(0, PLANES, step, 0)

    def keys_home(number, half):
        rows = rows_of(half)
        land, total, out = lands[number], sums[number], outs[number]
        take_bytes(land.at[:, :, :, rows], precv.at[number * 2 + half])

        def step(d, _):
            target = (plane + d) % PLANES
            for j in range(HEADS_PLANE):
                summed = land[0, j, target, rows].astype(F32)
                for r in range(1, COPIES):
                    summed += land[r, j, target, rows].astype(F32)
                total[target, rows, j * HDIM:(j + 1) * HDIM] = summed.astype(BF16)
            send_home(number, total.at[target, rows], out.at[rows, mine], target)
            return 0

        lax.fori_loop(0, PLANES, step, 0)

    settle(0, 0)
    settle(0, 1)
    queries_home()
    keys_home(0, 0)
    settle(1, 0)
    keys_home(0, 1)
    settle(1, 1)
    keys_home(1, 0)
    keys_home(1, 1)

    for number, out in enumerate((ok, ov, oq)):
        take_bytes(out, zrecv.at[number])
        take_bytes(sum_q.at[pl.ds(0, PLANES - 1)], zsend.at[number])

    @pl.when(works)
    def _():
        for number in range(2):
            take_bytes(sibs[number], ssend.at[number])
            take_bytes(owns[number].at[pl.ds(0, CHIPS - 1)], psend.at[number])

        @pl.when(replica == 0)
        def _():
            take_bytes(dq.at[pl.ds(0, QGROUPS - 1)], psend.at[2])

        @pl.when(replica != 0)
        def _():
            take_bytes(dq.at[pl.ds(0, QGROUPS - 2)], psend.at[2])


def home(dq, dk, dv, rows, width):
    anywhere = pl.BlockSpec(memory_space=pl.ANY)
    in_vmem = pl.BlockSpec(memory_space=pltpu.VMEM)
    out_shape = jax.ShapeDtypeStruct((rows, width), BF16)
    half = pltpu.VMEM((CHIPS, PLANES, CUBE, HDIM), BF16)
    slab = pltpu.VMEM((PLANES, CUBE, WIDTH), BF16)
    by_head = pltpu.VMEM((HEADS_PLANE, PLANES, CUBE, HDIM), BF16)
    copies = pltpu.VMEM((COPIES, HEADS_PLANE, PLANES, CUBE, HDIM), BF16)
    return pl.pallas_call(
        home_kernel,
        name="home",
        out_shape=(out_shape,) * 3,
        in_specs=[anywhere, in_vmem, in_vmem],
        out_specs=[anywhere] * 3,
        scratch_shapes=[
            half, half, half, half, by_head, copies, copies, slab, slab, slab,
            pltpu.SemaphoreType.DMA((2,)),
            pltpu.SemaphoreType.DMA((2, CHIPS)),
            pltpu.SemaphoreType.DMA((3,)),
            pltpu.SemaphoreType.DMA((5,)),
            pltpu.SemaphoreType.DMA((3,)),
            pltpu.SemaphoreType.DMA((3,)),
        ],
        compiler_params=pltpu.CompilerParams(
            collective_id=1, has_side_effects=True, vmem_limit_bytes=HOME_VMEM
        ),
    )(
        dq.reshape(QGROUPS, PLANES, CUBE, HDIM),
        dk.reshape(2 * CHIPS, PLANES, CUBE, HDIM),
        dv.reshape(2 * CHIPS, PLANES, CUBE, HDIM),
    )


def on_device(queries, keys_in, values, grad_out, fine_gate, coarse_gate, tile_of_cube, select):
    kh, vh, qh, fh, ph = bring(keys_in, values, queries, grad_out, fine_gate, coarse_gate)
    dq, dk, dv = attend(tile_of_cube, select, qh, fh, ph, kh, vh)
    return home(dq, dk, dv, *queries.shape)


def solution(mesh):
    split = P(("tok", "head"), None)
    return jax.shard_map(
        on_device,
        mesh=mesh,
        in_specs=(split,) * 6 + (P(), P()),
        out_specs=(split,) * 3,
        check_vma=False,
    )
```

```python
import functools
import math

import jax
import jax.numpy as jnp
from jax import lax
from jax.experimental import pallas as pl
from jax.experimental.pallas import tpu as pltpu
from jax.sharding import PartitionSpec as P

MESH = pl.DeviceIdType.MESH
BF16 = jnp.bfloat16
F32 = jnp.float32

CUBE = 64
HDIM = 128
PLANES = 8
CHIPS = 16
SIDE = 4
HEADS_PLANE = 5
COPIES = 3
WORKERS = HEADS_PLANE * COPIES
WIDTH = HEADS_PLANE * HDIM
QGROUPS = 6
TOPK = 16
SLOTS = 2 * CHIPS * PLANES
UNITS = QGROUPS * PLANES
HALF = CUBE // 2
STAGES = 8
HOPS = ((), (), ((0, 0),), ((0, 1),), ((0, 2), (1, 0)), ((0, 3), (1, 1)), ((1, 2),), ((1, 3),))
ALL = slice(None)
EXTRA = ((0, 4), (4, 2), (6, 2))
ATTEND_VMEM = 30 * 2**20
HOME_VMEM = 26 * 2**20
BRING_VMEM = 16 * 2**20


def where_am_i():
    tok = lax.axis_index("tok")
    head = lax.axis_index("head")
    plane = tok // 4
    chip = (tok // 2) % 2 * 8 + head
    core = tok % 2
    return plane, chip, core


def place_of(chip):
    x, y = chip % SIDE, chip // SIDE
    in_row = x < COPIES
    return x, y, in_row, jnp.where(in_row, x, y), jnp.where(in_row, y, HEADS_PLANE - 1)


def on_line(x, y, at):
    return jnp.where(x < COPIES, y * SIDE + at, at * SIDE + COPIES)


def source_of(group, x, y):
    in_row = jnp.where(group < SIDE, group * SIDE + x, x * SIDE + COPIES)
    in_column = jnp.where(group < SIDE, y * SIDE + group, COPIES * SIDE + y)
    return jnp.where(group < SIDE + 1, jnp.where(x < COPIES, in_row, in_column), WORKERS)


def device_of(plane, chip, core):
    return {"tok": plane * 4 + chip // 8 * 2 + core, "head": chip % 8}


def remote(src, dst, send, recv, device):
    return pltpu.make_async_remote_copy(
        src_ref=src, dst_ref=dst, send_sem=send, recv_sem=recv, device_id=device, device_id_type=MESH
    )


def take_bytes(ref, sem):
    pltpu.make_async_copy(ref, ref, sem).wait()


def greet(plane, chip, core):
    barrier = pltpu.get_barrier_semaphore()

    def along_z(d, _):
        pl.semaphore_signal(
            barrier, inc=1, device_id=device_of((plane + d) % PLANES, chip, core), device_id_type=MESH
        )
        return 0

    def in_plane(d, _):
        pl.semaphore_signal(
            barrier, inc=1, device_id=device_of(plane, (chip + d) % CHIPS, core), device_id_type=MESH
        )
        return 0

    lax.fori_loop(1, PLANES, along_z, 0)
    lax.fori_loop(1, CHIPS, in_plane, 0)
    pl.semaphore_signal(
        barrier, inc=1, device_id=device_of(plane, chip, 1 - core), device_id_type=MESH
    )
    pl.semaphore_wait(barrier, PLANES - 1 + CHIPS - 1 + 1)


def columns(group, width=WIDTH):
    return pl.ds(pl.multiple_of(group * width, 128), width)


def rows_of(half):
    return pl.ds(half * HALF, HALF)


def bring_kernel(
    k_in, v_in, q_in, g_in, fgate, cgate,
    kh, vh, qh, fh, ph,
    packed, kz, vz, qz, fz, pz, pg,
    zsend, zrecv, ysend, lsend, psend, krecv, qrecv, xrecv, fsend, frecv,
):
    plane, chip, core = where_am_i()
    greet(plane, chip, core)

    def start_along_z(stage, source, landing):
        def step(d, _):
            target = (plane + d) % PLANES
            remote(
                source(target), landing(plane), zsend.at[stage], zrecv.at[stage],
                device_of(target, chip, core),
            ).start()
            return 0

        lax.fori_loop(1, PLANES, step, 0)
        pltpu.make_async_copy(source(plane), landing(plane), zrecv.at[stage]).start()

    x, y, in_row, spot, _ = place_of(chip)
    works = chip < WORKERS
    slabs = (kz, vz, qz, fz)
    outs = (kh, vh, qh, fh)

    def start_stage(stage):
        number, rows = stage // 2, rows_of(stage % 2)
        start_along_z(
            stage,
            lambda t: packed.at[number, t, :, rows],
            lambda t: slabs[number].at[:, t, rows],
        )

    def pack(number, source):
        def step(group, _):
            for j in range(HEADS_PLANE):
                packed[number, group, j] = source[:, columns(group * HEADS_PLANE + j, HDIM)]
            return 0

        lax.fori_loop(0, PLANES, step, 0)

    pack(0, k_in)
    start_stage(0)
    start_stage(1)
    pack(1, v_in)
    pack(2, q_in)

    def gates(group, _):
        row = lax.broadcasted_iota(jnp.int32, (fgate.shape[0], WIDTH), 0)
        col = lax.broadcasted_iota(jnp.int32, (fgate.shape[0], WIDTH), 1)
        spread = jnp.where(
            row == group * HEADS_PLANE + lax.shift_right_logical(col, 7), 1.0, 0.0
        ).astype(BF16)
        grad = g_in[:, columns(group)].astype(F32)
        fine = (tn(fgate[...], spread) * grad).astype(BF16)
        coarse = tn(cgate[...], spread)
        pooled = jnp.sum(coarse * grad, axis=0, keepdims=True)
        rows = []
        for j in range(HEADS_PLANE):
            packed[3, group, j] = fine[:, j * HDIM:(j + 1) * HDIM]
            rows.append(pooled[:, j * HDIM:(j + 1) * HDIM])
        rows.append(jnp.zeros((16 - HEADS_PLANE, HDIM), F32))
        pg[group] = jnp.concatenate(rows, axis=0).astype(BF16)
        return 0

    lax.fori_loop(0, PLANES, gates, 0)

    def share_keys(number, rows):
        landed, out = slabs[number], outs[number]

        def step(j, _):
            row_head = j < SIDE
            target = jnp.where(row_head, j * SIDE + x, y * SIDE + COPIES)
            piece = jnp.where(row_head, x * SIDE + y, y * SIDE + x)
            aside = (row_head & (x == COPIES)).astype(jnp.int32)
            region = jnp.where(aside == 1, 2, core)
            here, there = landed.at[j, :, rows], out.at[region, piece, :, rows]
            arrived = krecv.at[number, aside, piece]

            @pl.when(target != chip)
            def _():
                remote(
                    here, there, ysend.at[number], arrived, device_of(plane, target, core)
                ).start()

            @pl.when(target == chip)
            def _():
                pltpu.make_async_copy(here, there, arrived).start()

            return 0

        lax.fori_loop(0, HEADS_PLANE, step, 0)

    def pass_on(number, hop):
        out = outs[number]

        def step(s, _):
            turn = s // 2
            way, stop = 1 - 2 * turn, 2 - 2 * turn

            def role(aside, region, at, target_of):
                piece = (at + 8 - way * hop) % SIDE * SIDE + s
                block = out.at[region, piece]
                after = (at + SIDE + way) % SIDE

                @pl.when((at != COPIES) | (hop < 3))
                def _():
                    take_bytes(block, krecv.at[number, aside, piece])

                if hop < 3:
                    to_side = (in_row & (after == COPIES)).astype(jnp.int32)

                    @pl.when((at != stop) | (hop < 2))
                    def _():
                        remote(
                            block, out.at[jnp.where(to_side == 1, 2, core), piece],
                            lsend.at[number, aside], krecv.at[number, to_side, piece],
                            device_of(plane, target_of(after), core),
                        ).start()

                if aside == 0:
                    @pl.when(works)
                    def _():
                        remote(
                            block, block, fsend.at[number], frecv.at[number],
                            device_of(plane, chip, 1 - core),
                        ).start()

            role(0, core, spot, lambda after: on_line(x, y, after))

            @pl.when(x == COPIES)
            def _():
                role(1, 2, jnp.int32(COPIES), lambda after: y * SIDE + after)

            return 0

        lax.fori_loop(0, SIDE, step, 0)

    def share_queries(number, pick, place):
        def step(j, _):
            row_head = j < SIDE
            at, source = jnp.where(row_head, x, y), jnp.where(row_head, y, x)
            line = lambda to: jnp.where(row_head, j * SIDE + to, to * SIDE + COPIES)
            direct = at < COPIES
            target = line(jnp.where(direct, at, jnp.minimum(source, COPIES - 1)))
            group = jnp.where(direct, source, SIDE)

            @pl.when(works & (target != chip))
            def _():
                remote(
                    pick(j, ALL), place(group, ALL), psend.at[number],
                    qrecv.at[number - 2], device_of(plane, target, core),
                ).start()

            @pl.when(works & (target == chip))
            def _():
                pltpu.make_async_copy(
                    pick(j, ALL), place(group, ALL), qrecv.at[number - 2]
                ).start()

            @pl.when(chip >= WORKERS)
            def _():
                for copy, (first, count) in enumerate(EXTRA):
                    remote(
                        pick(j, pl.ds(first, count)), place(QGROUPS - 1, pl.ds(0, count)),
                        psend.at[number], xrecv.at[number - 2],
                        device_of(plane, line(copy), core),
                    ).start()

            return 0

        lax.fori_loop(0, HEADS_PLANE, step, 0)

    for stage in range(STAGES):
        number, rows = stage // 2, rows_of(stage % 2)
        take_bytes(slabs[number].at[:, :, rows], zrecv.at[stage])
        if stage + 2 < STAGES:
            start_stage(stage + 2)
        if stage + 2 == STAGES:
            start_along_z(STAGES, lambda t: pg.at[t], lambda t: pz.at[t])
        if number < 2:
            share_keys(number, rows)
        else:
            share_queries(
                number,
                lambda j, z, number=number, rows=rows: slabs[number].at[j, z, rows],
                lambda i, z, number=number, rows=rows: outs[number].at[i, z, rows],
            )
        for number, hop in HOPS[stage]:
            pass_on(number, hop)
    take_bytes(pz, zrecv.at[STAGES])
    share_queries(4, lambda j, z: pz.at[z], lambda i, z: ph.at[i, z])

    @pl.when(works)
    def _():
        for number, out in enumerate((qh, fh, ph)):
            take_bytes(out.at[pl.ds(0, QGROUPS - 1)], qrecv.at[number])
        for copy, (first, count) in enumerate(EXTRA):
            @pl.when(spot == copy)
            def _(count=count):
                for number, out in enumerate((qh, fh, ph)):
                    take_bytes(out.at[QGROUPS - 1, pl.ds(0, count)], xrecv.at[number])

        for number, out in ((0, kh), (1, vh)):
            take_bytes(out.at[1 - core], frecv.at[number])
            take_bytes(out.at[1 - core], fsend.at[number])
        for number, out in ((2, qh), (3, fh), (4, ph)):
            take_bytes(out.at[pl.ds(0, HEADS_PLANE - 1)], psend.at[number])

    @pl.when(chip >= WORKERS)
    def _():
        for number, out in ((2, qh), (3, fh), (4, ph)):
            take_bytes(out.at[pl.ds(0, HEADS_PLANE)], psend.at[number])

    for number, out in ((0, kh), (1, vh)):
        @pl.when(in_row)
        def _(number=number, out=out):
            take_bytes(out.at[0, pl.ds(0, 4)], ysend.at[number])

        @pl.when(x == COPIES)
        def _(number=number, out=out):
            take_bytes(out.at[0, pl.ds(0, 3)], ysend.at[number])
            take_bytes(out.at[0, pl.ds(0, 12)], lsend.at[number, 1])

        @pl.when(spot % 2 == 0)
        def _(number=number, out=out):
            take_bytes(out.at[0, pl.ds(0, 10)], lsend.at[number, 0])

        @pl.when(spot % 2 == 1)
        def _(number=number, out=out):
            take_bytes(out.at[0, pl.ds(0, 12)], lsend.at[number, 0])

    for stage in range(STAGES):
        landed = slabs[stage // 2].at[:, pl.ds(0, PLANES - 1), rows_of(stage % 2)]
        take_bytes(landed, zsend.at[stage])
    take_bytes(pz.at[pl.ds(0, PLANES - 1)], zsend.at[STAGES])


def bring(keys_in, values, queries, grad_out, fine_gate, coarse_gate):
    keys_shape = jax.ShapeDtypeStruct((3, CHIPS, PLANES, CUBE, HDIM), BF16)
    query_shape = jax.ShapeDtypeStruct((QGROUPS, PLANES, CUBE, HDIM), BF16)
    pooled_shape = jax.ShapeDtypeStruct((QGROUPS, PLANES, 16, HDIM), BF16)
    anywhere = pl.BlockSpec(memory_space=pl.ANY)
    in_vmem = pl.BlockSpec(memory_space=pltpu.VMEM)
    slab = pltpu.VMEM((HEADS_PLANE, PLANES, CUBE, HDIM), BF16)
    small = pltpu.VMEM((PLANES, 16, HDIM), BF16)
    return pl.pallas_call(
        bring_kernel,
        name="bring",
        out_shape=(keys_shape, keys_shape, query_shape, query_shape, pooled_shape),
        in_specs=[in_vmem] * 6,
        out_specs=[anywhere] * 5,
        scratch_shapes=[
            pltpu.VMEM((4, PLANES, HEADS_PLANE, CUBE, HDIM), BF16),
            slab, slab, slab, slab, small, small,
            pltpu.SemaphoreType.DMA((STAGES + 1,)),
            pltpu.SemaphoreType.DMA((STAGES + 1,)),
            pltpu.SemaphoreType.DMA((2,)),
            pltpu.SemaphoreType.DMA((2, 2)),
            pltpu.SemaphoreType.DMA((5,)),
            pltpu.SemaphoreType.DMA((2, 2, CHIPS)),
            pltpu.SemaphoreType.DMA((3,)),
            pltpu.SemaphoreType.DMA((3,)),
            pltpu.SemaphoreType.DMA((2,)),
            pltpu.SemaphoreType.DMA((2,)),
        ],
        compiler_params=pltpu.CompilerParams(
            collective_id=0, has_side_effects=True, vmem_limit_bytes=BRING_VMEM
        ),
    )(keys_in, values, queries, grad_out, fine_gate.T, coarse_gate.T)


def nt(a, b):
    return lax.dot_general(a, b, (((1,), (1,)), ((), ())), preferred_element_type=F32)


def tn(a, b):
    return lax.dot_general(a, b, (((0,), (0,)), ((), ())), preferred_element_type=F32)


def nn(a, b):
    return jnp.dot(a, b, preferred_element_type=F32)


def attend_kernel(
    toc, sel, q, fg, pg, k, v,
    dq, dk, dv,
    acc, wide, pk, pv, pq, cdq, part_k, part_v, cot, soc,
):
    _, chip, core = where_am_i()
    x, y, in_row, replica, head = place_of(chip)
    extra = jnp.where(replica == 0, EXTRA[0][1], EXTRA[1][1])
    skip = jnp.where(replica == 0, EXTRA[0][0], jnp.where(replica == 1, EXTRA[1][0], EXTRA[2][0]))
    units = jnp.where(chip < WORKERS, (QGROUPS - 1) * PLANES + extra, 0)
    factor = 1.0 / math.sqrt(HDIM)
    log2e = math.log2(math.e)

    def eighths(source, group):
        block = source[pl.ds(pl.multiple_of(group * 8, 8), 8)].astype(F32)
        return jnp.sum(block.reshape(8, 8, 8, HDIM), axis=1).reshape(64, HDIM)

    def prepare(group, _):
        rows = pl.ds(pl.multiple_of(group * 64, 64), 64)
        part_k[rows, :] = eighths(k, group)
        part_v[rows, :] = eighths(v, group)
        acc[pl.ds(pl.multiple_of(group * 8, 8), 8)] = jnp.zeros((8, CUBE, 2 * HDIM), F32)
        for i in range(8):
            cube = group * 8 + i
            tile = toc[cube]
            cot[tile] = cube
            at_x = tile & 3
            at_y = (lax.shift_right_logical(tile, 3) & 2) + (lax.shift_right_logical(tile, 2) & 1)
            piece = jnp.where(in_row, at_x * SIDE + at_y, at_y * SIDE + at_x)
            half = lax.shift_right_logical(tile, 3) & 1
            soc[cube] = (half * CHIPS + piece) * PLANES + lax.shift_right_logical(tile, 5)
        return 0

    lax.fori_loop(0, SLOTS // 8, prepare, 0)

    def pool(part, into):
        count = into.shape[0]
        total = part[pl.ds(0, count, stride=8), :]
        for row in range(1, 8):
            total += part[pl.ds(row, count, stride=8), :]
        into[...] = total * (1.0 / CUBE)

    pool(part_k, pk)
    pool(part_v, pv)

    def prepare_queries(group, _):
        part_k[pl.ds(pl.multiple_of(group * 64, 64), 64), :] = eighths(q, group)
        return 0

    lax.fori_loop(0, QGROUPS, prepare_queries, 0)
    pool(part_k, pq)
    unit_at = lax.broadcasted_iota(jnp.int32, (UNITS, 16, HDIM), 0)
    row_at = lax.broadcasted_iota(jnp.int32, (UNITS, 16, HDIM), 1)
    pooled_g = jnp.sum(
        jnp.where((unit_at < units) & (row_at == head), pg[...].astype(F32), 0.0), axis=1
    ).astype(BF16)
    live = lax.broadcasted_iota(jnp.int32, (UNITS, HDIM), 0) < units
    pooled_q = jnp.where(live, pq[...], 0.0).astype(BF16)
    pooled_k = pk[...].astype(BF16)
    pooled_v = pv[...].astype(BF16)
    scores = nt(pooled_q, pooled_k) * factor
    weights = jnp.exp(scores - jnp.max(scores, axis=1, keepdims=True))
    probs = weights / jnp.sum(weights, axis=1, keepdims=True)
    dprobs = nt(pooled_g, pooled_v)
    inner = jnp.sum(probs * dprobs, axis=1, keepdims=True)
    dscores = (probs * (dprobs - inner)).astype(BF16)
    cdq[...] = nn(dscores, pooled_k) * (factor / CUBE)
    pk[...] = tn(dscores, pooled_q) * (factor / CUBE)
    pv[...] = tn(probs.astype(BF16), pooled_g) * (1.0 / CUBE)
    wide[...] = jnp.zeros_like(wide)

    def listed(n):
        group, z = n // PLANES, n % PLANES
        origin = source_of(group, x, y)
        z = jnp.where(group == QGROUPS - 1, z + skip, z)
        tile = (z * 4 + origin // 8 * 2 + core) * 8 + origin % 8
        cube = cot[tile]
        slots = [soc[sel[r, cube]] for r in range(TOPK)]
        return [slots[c * 4:c * 4 + 4] for c in range(4)]

    def tiles_of(ref, quarter):
        return jnp.concatenate([ref[s] for s in quarter], axis=0)

    def softmax_terms(n, side, quarters):
        wide[side, :CUBE, :HDIM] = q[n]
        wide[side, CUBE:, HDIM:] = fg[n]
        both = [
            nt(wide[side], jnp.concatenate([tiles_of(k, quarter), tiles_of(v, quarter)], axis=1))
            for quarter in quarters
        ]
        score = [b[:CUBE] for b in both]
        dprob = [b[CUBE:] for b in both]
        top = functools.reduce(jnp.maximum, score)
        top = jnp.max(top, axis=1, keepdims=True)
        weight = [jnp.exp2((s - top) * (factor * log2e)) for s in score]
        total = jnp.sum(functools.reduce(jnp.add, weight), axis=1, keepdims=True)
        inverse = 1.0 / total
        mixed = functools.reduce(jnp.add, [w * d for w, d in zip(weight, dprob)])
        center = jnp.sum(mixed, axis=1, keepdims=True) * inverse
        probs = [w * inverse for w in weight]
        dscore = [(p * (d - center)).astype(BF16) for p, d in zip(probs, dprob)]
        return [p.astype(BF16) for p in probs], dscore

    def spread_terms(n, side, quarters, probs, dscore):
        dquery = jnp.zeros((CUBE, HDIM), F32)
        for c, quarter in enumerate(quarters):
            dquery += nn(dscore[c], tiles_of(k, quarter))
            terms = tn(jnp.concatenate([dscore[c], probs[c]], axis=0), wide[side])
            for i, s in enumerate(quarter):
                acc[s] += terms[i * CUBE:(i + 1) * CUBE]
        dq[n] = (dquery * factor + cdq[pl.ds(n, 1), :]).astype(BF16)

    def pair(m, _):
        numbers = [2 * m, 2 * m + 1]
        lists = [listed(n) for n in numbers]
        terms = [softmax_terms(n, i, quarters) for i, (n, quarters) in enumerate(zip(numbers, lists))]
        for i, (n, quarters, (probs, dscore)) in enumerate(zip(numbers, lists, terms)):
            spread_terms(n, i, quarters, probs, dscore)
        return 0

    lax.fori_loop(0, units // 2, pair, 0)

    def finish(group, _):
        for i in range(4):
            slot = group * 4 + i
            dk[slot] = (acc[slot, :, :HDIM] * factor + pk[pl.ds(slot, 1), :]).astype(BF16)
            dv[slot] = (acc[slot, :, HDIM:] + pv[pl.ds(slot, 1), :]).astype(BF16)
        return 0

    lax.fori_loop(0, SLOTS // 4, finish, 0)


def attend(tile_of_cube, select, qh, fh, ph, kh, vh):
    smem = pl.BlockSpec(memory_space=pltpu.SMEM)
    vmem = pl.BlockSpec(memory_space=pltpu.VMEM)
    query_shape = jax.ShapeDtypeStruct((UNITS, CUBE, HDIM), BF16)
    keys_shape = jax.ShapeDtypeStruct((SLOTS, CUBE, HDIM), BF16)
    return pl.pallas_call(
        attend_kernel,
        name="attend",
        out_shape=(query_shape, keys_shape, keys_shape),
        in_specs=[smem] * 2 + [vmem] * 5,
        out_specs=[vmem] * 3,
        scratch_shapes=[
            pltpu.VMEM((SLOTS, CUBE, 2 * HDIM), F32),
            pltpu.VMEM((2, 2 * CUBE, 2 * HDIM), BF16),
            pltpu.VMEM((SLOTS, HDIM), F32),
            pltpu.VMEM((SLOTS, HDIM), F32),
            pltpu.VMEM((UNITS, HDIM), F32),
            pltpu.VMEM((UNITS, HDIM), F32),
            pltpu.VMEM((SLOTS * 8, HDIM), F32),
            pltpu.VMEM((SLOTS * 8, HDIM), F32),
            pltpu.SMEM((SLOTS,), jnp.int32),
            pltpu.SMEM((SLOTS,), jnp.int32),
        ],
        compiler_params=pltpu.CompilerParams(vmem_limit_bytes=ATTEND_VMEM),
    )(
        tile_of_cube, select.T,
        qh.reshape(UNITS, CUBE, HDIM), fh.reshape(UNITS, CUBE, HDIM),
        ph.reshape(UNITS, 16, HDIM), kh.reshape(-1, CUBE, HDIM), vh.reshape(-1, CUBE, HDIM),
    )


def home_kernel(
    dq, dk, dv,
    oq, ok, ov,
    own_k, own_v, sib_k, sib_v, land_q, land_k, land_v, sum_k, sum_v, sum_q, chain_k, chain_v,
    ssend, srecv, psend, lsend, lrecv, ysend, precv, zsend, zrecv,
):
    plane, chip, core = where_am_i()
    x, y, in_row, spot, head = place_of(chip)
    works = chip < WORKERS
    greet(plane, chip, core)
    sources, owns, sibs, chains = (dk, dv), (own_k, own_v), (sib_k, sib_v), (chain_k, chain_v)
    lands, sums, outs = (land_k, land_v), (sum_k, sum_v), (ok, ov)
    mine = columns(plane)

    def turn_of(m):
        hop, s = m // SIDE, m % SIDE
        return hop, s, 1 - 2 * (s // 2), 2 - 2 * (s // 2)

    @pl.when(works)
    def _():
        def give(m, _):
            hop, s, way, _stop = turn_of(m)
            piece = (spot + 8 + way * (hop + 1)) % SIDE * SIDE + s
            for number in range(2):
                remote(
                    sources[number].at[(1 - core) * CHIPS + piece], sibs[number].at[piece],
                    ssend.at[number], srecv.at[number, piece],
                    device_of(plane, chip, 1 - core),
                ).start()
            return 0

        lax.fori_loop(0, CHIPS, give, 0)

        def send_query(i, _):
            target = source_of(i, x, y)

            @pl.when(target != chip)
            def _():
                remote(
                    dq.at[i], land_q.at[head], psend.at[0], precv.at[4],
                    device_of(plane, target, core),
                ).start()

            @pl.when(target == chip)
            def _():
                pltpu.make_async_copy(dq.at[i], land_q.at[head], precv.at[4]).start()

            return 0

        lax.fori_loop(0, QGROUPS - 1, send_query, 0)
        for copy, (first, count) in enumerate(EXTRA):
            @pl.when(spot == copy)
            def _(first=first, count=count):
                remote(
                    dq.at[QGROUPS - 1, pl.ds(0, count)], land_q.at[head, pl.ds(first, count)],
                    psend.at[1], precv.at[4], device_of(plane, CHIPS - 1, core),
                ).start()

    def gather(half):
        rows = rows_of(half)

        def step(m, _):
            hop, s, way, stop = turn_of(m)
            landing = jnp.minimum(hop, 2)
            arrival = jnp.maximum(hop - 1, 0)

            def deliver(number, block, at_x, at_y, to_head, aside):
                target = at_y * SIDE + at_x
                land, arrived = lands[number], precv.at[number * 2 + half]

                @pl.when(target != chip)
                def _():
                    remote(
                        block, land.at[to_head, :, rows], ysend.at[number, aside], arrived,
                        device_of(plane, target, core),
                    ).start()

                @pl.when(target == chip)
                def _():
                    pltpu.make_async_copy(block, land.at[to_head, :, rows], arrived).start()

            def hand_over(number, block, after, target, aside):
                to_side = (in_row & (after == COPIES)).astype(jnp.int32)
                remote(
                    block, chains[number].at[to_side, landing * SIDE + s, :, rows],
                    lsend.at[number, aside], lrecv.at[number, half, to_side, landing * SIDE + s],
                    device_of(plane, target, core),
                ).start()

            def relay(number, aside, target_of, at_x, at_y, to_head):
                block = chains[number].at[aside, arrival * SIDE + s, :, rows]
                after = (COPIES + SIDE - way) % SIDE

                @pl.when(hop > 0)
                def _():
                    take_bytes(block, lrecv.at[number, half, aside, arrival * SIDE + s])

                @pl.when((hop > 0) & (hop < 3))
                def _():
                    hand_over(number, block, after, target_of(after), aside)

                @pl.when(hop == 3)
                def _():
                    deliver(number, block, at_x, at_y, to_head, aside)

            for number in range(2):
                source, own, sib, chain = sources[number], owns[number], sibs[number], chains[number]

                @pl.when(works)
                def _(number=number, source=source, own=own, sib=sib, chain=chain):
                    piece = (spot + 8 + way * (hop + 1)) % SIDE * SIDE + s
                    if half == 0:
                        take_bytes(sib.at[piece], srecv.at[number, piece])
                    partial = lambda: (
                        source[core * CHIPS + piece, :, rows].astype(F32)
                        + sib[piece, :, rows].astype(F32)
                    )
                    fed = (hop > 1) | ((hop == 1) & (spot != stop))

                    @pl.when(fed)
                    def _():
                        came = chain.at[0, arrival * SIDE + s, :, rows]
                        take_bytes(came, lrecv.at[number, half, 0, arrival * SIDE + s])
                        own[piece, :, rows] = (partial() + came[...].astype(F32)).astype(BF16)

                    @pl.when(jnp.logical_not(fed))
                    def _():
                        own[piece, :, rows] = partial().astype(BF16)

                    block = own.at[piece, :, rows]
                    after = (spot + SIDE - way) % SIDE

                    @pl.when(hop < 3)
                    def _():
                        hand_over(number, block, after, on_line(x, y, after), 0)

                    @pl.when(hop == 3)
                    def _():
                        deliver(
                            number, block, jnp.where(in_row, x, s), jnp.where(in_row, s, y), head, 0
                        )

                @pl.when(chip >= WORKERS)
                def _(number=number):
                    relay(number, 0, lambda after: on_line(x, y, after), s, y, HEADS_PLANE - 1)

                @pl.when(x == COPIES)
                def _(number=number):
                    relay(number, 1, lambda after: y * SIDE + after, x, s, y)

            return 0

        lax.fori_loop(0, CHIPS, step, 0)

    def send_home(number, block, out, target):
        @pl.when(target != plane)
        def _():
            remote(
                block, out, zsend.at[number], zrecv.at[number], device_of(target, chip, core)
            ).start()

        @pl.when(target == plane)
        def _():
            pltpu.make_async_copy(block, out, zrecv.at[number]).start()

    def queries_home():
        take_bytes(land_q, precv.at[4])

        def step(d, _):
            target = (plane + d) % PLANES
            for j in range(HEADS_PLANE):
                sum_q[target, :, j * HDIM:(j + 1) * HDIM] = land_q[j, target]
            send_home(2, sum_q.at[target], oq.at[:, mine], target)
            return 0

        lax.fori_loop(0, PLANES, step, 0)

    def keys_home(number, half):
        rows = rows_of(half)
        land, total, out = lands[number], sums[number], outs[number]
        take_bytes(land.at[:, :, rows], precv.at[number * 2 + half])

        def step(d, _):
            target = (plane + d) % PLANES
            for j in range(HEADS_PLANE):
                total[target, rows, j * HDIM:(j + 1) * HDIM] = land[j, target, rows]
            send_home(number, total.at[target, rows], out.at[rows, mine], target)
            return 0

        lax.fori_loop(0, PLANES, step, 0)

    gather(0)
    queries_home()
    keys_home(0, 0)
    keys_home(1, 0)
    gather(1)
    keys_home(0, 1)
    keys_home(1, 1)

    for number, out in enumerate((ok, ov, oq)):
        take_bytes(out, zrecv.at[number])
        take_bytes(sum_q.at[pl.ds(0, PLANES - 1)], zsend.at[number])

    for number in range(2):
        own = owns[number]
        take_bytes(own.at[pl.ds(0, SIDE - 1)], ysend.at[number, 0])

        @pl.when(works)
        def _(number=number, own=own):
            take_bytes(sibs[number], ssend.at[number])
            take_bytes(own.at[pl.ds(0, 12)], lsend.at[number, 0])

        @pl.when(chip >= WORKERS)
        def _(number=number, own=own):
            take_bytes(own.at[pl.ds(0, 8)], lsend.at[number, 0])

        @pl.when(x == COPIES)
        def _(number=number, own=own):
            take_bytes(own.at[pl.ds(0, 8)], lsend.at[number, 1])
            take_bytes(own.at[pl.ds(0, SIDE - 1)], ysend.at[number, 1])

    @pl.when(works)
    def _():
        take_bytes(dq.at[pl.ds(0, QGROUPS - 2)], psend.at[0])
        for copy, (first, count) in enumerate(EXTRA):
            @pl.when(spot == copy)
            def _(count=count):
                take_bytes(dq.at[QGROUPS - 1, pl.ds(0, count)], psend.at[1])


def home(dq, dk, dv, rows, width):
    anywhere = pl.BlockSpec(memory_space=pl.ANY)
    in_vmem = pl.BlockSpec(memory_space=pltpu.VMEM)
    out_shape = jax.ShapeDtypeStruct((rows, width), BF16)
    half = pltpu.VMEM((CHIPS, PLANES, CUBE, HDIM), BF16)
    slab = pltpu.VMEM((PLANES, CUBE, WIDTH), BF16)
    by_head = pltpu.VMEM((HEADS_PLANE, PLANES, CUBE, HDIM), BF16)
    chain = pltpu.VMEM((2, 12, PLANES, CUBE, HDIM), BF16)
    return pl.pallas_call(
        home_kernel,
        name="home",
        out_shape=(out_shape,) * 3,
        in_specs=[anywhere, in_vmem, in_vmem],
        out_specs=[anywhere] * 3,
        scratch_shapes=[
            half, half, half, half, by_head, by_head, by_head, slab, slab, slab, chain, chain,
            pltpu.SemaphoreType.DMA((2,)),
            pltpu.SemaphoreType.DMA((2, CHIPS)),
            pltpu.SemaphoreType.DMA((2,)),
            pltpu.SemaphoreType.DMA((2, 2)),
            pltpu.SemaphoreType.DMA((2, 2, 2, 12)),
            pltpu.SemaphoreType.DMA((2, 2)),
            pltpu.SemaphoreType.DMA((5,)),
            pltpu.SemaphoreType.DMA((3,)),
            pltpu.SemaphoreType.DMA((3,)),
        ],
        compiler_params=pltpu.CompilerParams(
            collective_id=1, has_side_effects=True, vmem_limit_bytes=HOME_VMEM
        ),
    )(
        dq.reshape(QGROUPS, PLANES, CUBE, HDIM),
        dk.reshape(2 * CHIPS, PLANES, CUBE, HDIM),
        dv.reshape(2 * CHIPS, PLANES, CUBE, HDIM),
    )


def on_device(queries, keys_in, values, grad_out, fine_gate, coarse_gate, tile_of_cube, select):
    kh, vh, qh, fh, ph = bring(keys_in, values, queries, grad_out, fine_gate, coarse_gate)
    dq, dk, dv = attend(tile_of_cube, select, qh, fh, ph, kh, vh)
    return home(dq, dk, dv, *queries.shape)


def solution(mesh):
    split = P(("tok", "head"), None)
    return jax.shard_map(
        on_device,
        mesh=mesh,
        in_specs=(split,) * 6 + (P(), P()),
        out_specs=(split,) * 3,
        check_vma=False,
    )
```

```python
import functools
import math

import jax
import jax.numpy as jnp
from jax import lax
from jax.experimental import pallas as pl
from jax.experimental.pallas import tpu as pltpu
from jax.sharding import PartitionSpec as P

MESH = pl.DeviceIdType.MESH
BF16 = jnp.bfloat16
F32 = jnp.float32

CUBE = 64
HDIM = 128
PLANES = 8
CHIPS = 16
HEADS_PLANE = 5
COPIES = 2
WORKERS = HEADS_PLANE * COPIES
WIDTH = HEADS_PLANE * HDIM
QGROUPS = 8
TOPK = 16
SLOTS = 2 * CHIPS * PLANES
UNITS = QGROUPS * PLANES
HALF = CUBE // 2
STAGES = 8
ATTEND_VMEM = 30 * 2**20
HOME_VMEM = 20 * 2**20
BRING_VMEM = 16 * 2**20


def where_am_i():
    tok = lax.axis_index("tok")
    head = lax.axis_index("head")
    plane = tok // 4
    chip = (tok // 2) % 2 * 8 + head
    core = tok % 2
    return plane, chip, core


def role_of(chip):
    x, y = chip % 4, chip // 4
    even = y % 2 == 0
    return even | (x == y - 1), jnp.where(even, x, HEADS_PLANE - 1), y // 2


def chip_of(head, copy):
    return jnp.where(head < HEADS_PLANE - 1, 8 * copy + head, 10 * copy + 4)


def device_of(plane, chip, core):
    return {"tok": plane * 4 + chip // 8 * 2 + core, "head": chip % 8}


def remote(src, dst, send, recv, device):
    return pltpu.make_async_remote_copy(
        src_ref=src, dst_ref=dst, send_sem=send, recv_sem=recv, device_id=device, device_id_type=MESH
    )


def take_bytes(ref, sem):
    pltpu.make_async_copy(ref, ref, sem).wait()


def greet(plane, chip, core):
    barrier = pltpu.get_barrier_semaphore()

    def along_z(d, _):
        pl.semaphore_signal(
            barrier, inc=1, device_id=device_of((plane + d) % PLANES, chip, core), device_id_type=MESH
        )
        return 0

    def in_plane(d, _):
        pl.semaphore_signal(
            barrier, inc=1, device_id=device_of(plane, (chip + d) % CHIPS, core), device_id_type=MESH
        )
        return 0

    lax.fori_loop(1, PLANES, along_z, 0)
    lax.fori_loop(1, CHIPS, in_plane, 0)
    pl.semaphore_signal(
        barrier, inc=1, device_id=device_of(plane, chip, 1 - core), device_id_type=MESH
    )
    pl.semaphore_wait(barrier, PLANES - 1 + CHIPS - 1 + 1)


def columns(group, width=WIDTH):
    return pl.ds(pl.multiple_of(group * width, 128), width)


def rows_of(half):
    return pl.ds(half * HALF, HALF)


def bring_kernel(
    k_in, v_in, q_in, g_in, fgate, cgate,
    kh, vh, qh, fh, ph,
    packed, kz, vz, qz, fz, pz, pg,
    zsend, zrecv, psend, krecv, qrecv, fsend, frecv,
):
    plane, chip, core = where_am_i()
    greet(plane, chip, core)

    def start_along_z(stage, source, landing):
        def step(d, _):
            target = (plane + d) % PLANES
            remote(
                source(target), landing(plane), zsend.at[stage], zrecv.at[stage],
                device_of(target, chip, core),
            ).start()
            return 0

        lax.fori_loop(1, PLANES, step, 0)
        pltpu.make_async_copy(source(plane), landing(plane), zrecv.at[stage]).start()

    slabs = (kz, vz, qz, fz)
    outs = (kh, vh, qh, fh)

    def start_stage(stage):
        number, rows = stage // 2, rows_of(stage % 2)
        start_along_z(
            stage,
            lambda t: packed.at[number, t, :, rows],
            lambda t: slabs[number].at[:, t, rows],
        )

    def pack(number, source):
        def step(group, _):
            for j in range(HEADS_PLANE):
                packed[number, group, j] = source[:, columns(group * HEADS_PLANE + j, HDIM)]
            return 0

        lax.fori_loop(0, PLANES, step, 0)

    pack(0, k_in)
    start_stage(0)
    pack(1, v_in)
    pack(2, q_in)

    def gates(group, _):
        row = lax.broadcasted_iota(jnp.int32, (fgate.shape[0], WIDTH), 0)
        col = lax.broadcasted_iota(jnp.int32, (fgate.shape[0], WIDTH), 1)
        spread = jnp.where(
            row == group * HEADS_PLANE + lax.shift_right_logical(col, 7), 1.0, 0.0
        ).astype(BF16)
        grad = g_in[:, columns(group)].astype(F32)
        fine = (tn(fgate[...], spread) * grad).astype(BF16)
        coarse = tn(cgate[...], spread)
        pooled = jnp.sum(coarse * grad, axis=0, keepdims=True)
        rows = []
        for j in range(HEADS_PLANE):
            packed[3, group, j] = fine[:, j * HDIM:(j + 1) * HDIM]
            rows.append(pooled[:, j * HDIM:(j + 1) * HDIM])
        rows.append(jnp.zeros((16 - HEADS_PLANE, HDIM), F32))
        pg[group] = jnp.concatenate(rows, axis=0).astype(BF16)
        return 0

    lax.fori_loop(0, PLANES, gates, 0)
    start_stage(1)
    works, _, copy_here = role_of(chip)

    def share_keys(number, rows):
        landed, out = slabs[number], outs[number]

        def step(m, _):
            worker = (m + chip) % WORKERS
            head = worker % HEADS_PLANE
            target = chip_of(head, worker // HEADS_PLANE)
            here, there = landed.at[head, :, rows], out.at[core * CHIPS + chip, :, rows]

            @pl.when(target != chip)
            def _():
                remote(
                    here, there, psend.at[number], krecv.at[number, chip],
                    device_of(plane, target, core),
                ).start()

            @pl.when(target == chip)
            def _():
                pltpu.make_async_copy(here, there, krecv.at[number, chip]).start()

            return 0

        lax.fori_loop(0, WORKERS, step, 0)

    def share_queries(number, pick, place):
        def step(m, _):
            j = (m + chip) % HEADS_PLANE
            target = chip_of(j, copy_here)

            @pl.when(target != chip)
            def _():
                remote(
                    pick(j), place(chip % QGROUPS), psend.at[number],
                    qrecv.at[number - 2], device_of(plane, target, core),
                ).start()

            @pl.when(target == chip)
            def _():
                pltpu.make_async_copy(
                    pick(j), place(chip % QGROUPS), qrecv.at[number - 2]
                ).start()

            return 0

        lax.fori_loop(0, HEADS_PLANE, step, 0)

    for stage in range(STAGES):
        number, rows = stage // 2, rows_of(stage % 2)
        take_bytes(slabs[number].at[:, :, rows], zrecv.at[stage])
        if stage + 2 < STAGES:
            start_stage(stage + 2)
        if stage + 2 == STAGES:
            start_along_z(STAGES, lambda t: pg.at[t], lambda t: pz.at[t])
        if number < 2:
            share_keys(number, rows)
        else:
            share_queries(
                number,
                lambda j, number=number, rows=rows: slabs[number].at[j, :, rows],
                lambda i, number=number, rows=rows: outs[number].at[i, :, rows],
            )
    take_bytes(pz, zrecv.at[STAGES])
    share_queries(4, lambda j: pz, lambda i: ph.at[i])

    sibling = device_of(plane, chip, 1 - core)

    @pl.when(works)
    def _():
        for number, out in ((0, kh), (1, vh)):
            def forward(d, _, number=number, out=out):
                origin = (chip + CHIPS - d) % CHIPS
                block = out.at[core * CHIPS + origin]
                take_bytes(block, krecv.at[number, origin])
                remote(block, block, fsend.at[number], frecv.at[number], sibling).start()
                return 0

            lax.fori_loop(0, CHIPS, forward, 0)

        for number, out in enumerate((qh, fh, ph)):
            take_bytes(out, qrecv.at[number])

        for number, out in ((0, kh), (1, vh)):
            theirs = out.at[pl.ds((1 - core) * CHIPS, CHIPS)]
            take_bytes(theirs, frecv.at[number])
            take_bytes(theirs, fsend.at[number])

    for stage in range(STAGES):
        landed = slabs[stage // 2].at[:, pl.ds(0, PLANES - 1), rows_of(stage % 2)]
        take_bytes(landed, zsend.at[stage])
    take_bytes(pz.at[pl.ds(0, PLANES - 1)], zsend.at[STAGES])

    def drain(keys, queries):
        for number, out in ((0, kh), (1, vh)):
            take_bytes(out.at[pl.ds(0, keys)], psend.at[number])
        for number, out in ((2, qh), (3, fh), (4, ph)):
            take_bytes(out.at[pl.ds(0, queries)], psend.at[number])

    @pl.when(works)
    def _():
        drain(WORKERS - 1, HEADS_PLANE - 1)

    @pl.when(jnp.logical_not(works))
    def _():
        drain(WORKERS, HEADS_PLANE)


def bring(keys_in, values, queries, grad_out, fine_gate, coarse_gate):
    keys_shape = jax.ShapeDtypeStruct((2 * CHIPS, PLANES, CUBE, HDIM), BF16)
    query_shape = jax.ShapeDtypeStruct((QGROUPS, PLANES, CUBE, HDIM), BF16)
    pooled_shape = jax.ShapeDtypeStruct((QGROUPS, PLANES, 16, HDIM), BF16)
    anywhere = pl.BlockSpec(memory_space=pl.ANY)
    in_vmem = pl.BlockSpec(memory_space=pltpu.VMEM)
    slab = pltpu.VMEM((HEADS_PLANE, PLANES, CUBE, HDIM), BF16)
    small = pltpu.VMEM((PLANES, 16, HDIM), BF16)
    return pl.pallas_call(
        bring_kernel,
        name="bring",
        out_shape=(keys_shape, keys_shape, query_shape, query_shape, pooled_shape),
        in_specs=[in_vmem] * 6,
        out_specs=[anywhere] * 5,
        scratch_shapes=[
            pltpu.VMEM((4, PLANES, HEADS_PLANE, CUBE, HDIM), BF16),
            slab, slab, slab, slab, small, small,
            pltpu.SemaphoreType.DMA((STAGES + 1,)),
            pltpu.SemaphoreType.DMA((STAGES + 1,)),
            pltpu.SemaphoreType.DMA((5,)),
            pltpu.SemaphoreType.DMA((2, CHIPS)),
            pltpu.SemaphoreType.DMA((3,)),
            pltpu.SemaphoreType.DMA((2,)),
            pltpu.SemaphoreType.DMA((2,)),
        ],
        compiler_params=pltpu.CompilerParams(
            collective_id=0, has_side_effects=True, vmem_limit_bytes=BRING_VMEM
        ),
    )(keys_in, values, queries, grad_out, fine_gate.T, coarse_gate.T)


def nt(a, b):
    return lax.dot_general(a, b, (((1,), (1,)), ((), ())), preferred_element_type=F32)


def tn(a, b):
    return lax.dot_general(a, b, (((0,), (0,)), ((), ())), preferred_element_type=F32)


def nn(a, b):
    return jnp.dot(a, b, preferred_element_type=F32)


def attend_kernel(
    toc, sel, q, fg, pg, k, v,
    dq, dk, dv,
    acc, wide, pk, pv, pq, cdq, part_k, part_v, cot, soc,
):
    _, chip, core = where_am_i()
    works, head, copy = role_of(chip)
    units = jnp.where(works, UNITS, 0)
    factor = 1.0 / math.sqrt(HDIM)
    log2e = math.log2(math.e)

    def eighths(source, group):
        block = source[pl.ds(pl.multiple_of(group * 8, 8), 8)].astype(F32)
        return jnp.sum(block.reshape(8, 8, 8, HDIM), axis=1).reshape(64, HDIM)

    def prepare(group, _):
        rows = pl.ds(pl.multiple_of(group * 64, 64), 64)
        part_k[rows, :] = eighths(k, group)
        part_v[rows, :] = eighths(v, group)
        acc[pl.ds(pl.multiple_of(group * 8, 8), 8)] = jnp.zeros((8, CUBE, 2 * HDIM), F32)
        for i in range(8):
            cube = group * 8 + i
            tile = toc[cube]
            cot[tile] = cube
            soc[cube] = (
                lax.shift_left(lax.shift_right_logical(tile, 3) & 1, 7)
                + lax.shift_left(lax.shift_right_logical(tile, 4) & 1, 6)
                + lax.shift_left(tile & 7, 3)
                + lax.shift_right_logical(tile, 5)
            )
        return 0

    lax.fori_loop(0, SLOTS // 8, prepare, 0)

    def pool(part, into):
        count = into.shape[0]
        total = part[pl.ds(0, count, stride=8), :]
        for row in range(1, 8):
            total += part[pl.ds(row, count, stride=8), :]
        into[...] = total * (1.0 / CUBE)

    pool(part_k, pk)
    pool(part_v, pv)

    def prepare_queries(group, _):
        part_k[pl.ds(pl.multiple_of(group * 64, 64), 64), :] = eighths(q, group)
        return 0

    lax.fori_loop(0, QGROUPS, prepare_queries, 0)
    pool(part_k, pq)
    row_at = lax.broadcasted_iota(jnp.int32, (UNITS, 16, HDIM), 1)
    pooled_g = jnp.sum(
        jnp.where(row_at == head, pg[...].astype(F32), 0.0), axis=1
    ).astype(BF16)
    pooled_q = pq[...].astype(BF16)
    pooled_k = pk[...].astype(BF16)
    pooled_v = pv[...].astype(BF16)
    scores = nt(pooled_q, pooled_k) * factor
    weights = jnp.exp(scores - jnp.max(scores, axis=1, keepdims=True))
    probs = weights / jnp.sum(weights, axis=1, keepdims=True)
    dprobs = nt(pooled_g, pooled_v)
    inner = jnp.sum(probs * dprobs, axis=1, keepdims=True)
    dscores = (probs * (dprobs - inner)).astype(BF16)
    cdq[...] = nn(dscores, pooled_k) * (factor / CUBE)
    pk[...] = tn(dscores, pooled_q) * (factor / CUBE)
    pv[...] = tn(probs.astype(BF16), pooled_g) * (1.0 / CUBE)
    wide[...] = jnp.zeros_like(wide)

    def listed(n):
        tile = (n % PLANES * 4 + copy * 2 + core) * 8 + n // PLANES
        cube = cot[tile]
        slots = [soc[sel[r, cube]] for r in range(TOPK)]
        return [slots[c * 4:c * 4 + 4] for c in range(4)]

    def tiles_of(ref, quarter):
        return jnp.concatenate([ref[s] for s in quarter], axis=0)

    def pair(m, _):
        numbers = (2 * m, 2 * m + 1)
        lists = [listed(n) for n in numbers]
        for i, n in enumerate(numbers):
            wide[0, i * CUBE:(i + 1) * CUBE, i * HDIM:(i + 1) * HDIM] = q[n]
            wide[1, i * CUBE:(i + 1) * CUBE, i * HDIM:(i + 1) * HDIM] = fg[n]
        beside = lambda ref, c: jnp.concatenate([tiles_of(ref, quarters[c]) for quarters in lists], axis=1)
        score = [nt(beside(k, c), wide[0]) for c in range(4)]
        dprob = [nt(beside(v, c), wide[1]) for c in range(4)]
        top = jnp.max(functools.reduce(jnp.maximum, score), axis=0, keepdims=True)
        weight = [jnp.exp2((s - top) * (factor * log2e)) for s in score]
        total = jnp.sum(functools.reduce(jnp.add, weight), axis=0, keepdims=True)
        inverse = 1.0 / total
        mixed = functools.reduce(jnp.add, [w * d for w, d in zip(weight, dprob)])
        center = jnp.sum(mixed, axis=0, keepdims=True) * inverse
        dquery = jnp.zeros((2 * CUBE, 2 * HDIM), F32)
        for c in range(4):
            prob = weight[c] * inverse
            dscore = (prob * (dprob[c] - center)).astype(BF16)
            dquery += tn(dscore, beside(k, c))
            key_terms = nn(dscore, wide[0])
            value_terms = nn(prob.astype(BF16), wide[1])
            for i, quarters in enumerate(lists):
                for at, s in enumerate(quarters[c]):
                    rows, lanes = slice(at * CUBE, (at + 1) * CUBE), slice(i * HDIM, (i + 1) * HDIM)
                    acc[s, :, :HDIM] += key_terms[rows, lanes]
                    acc[s, :, HDIM:] += value_terms[rows, lanes]
        for i, n in enumerate(numbers):
            mine = dquery[i * CUBE:(i + 1) * CUBE, i * HDIM:(i + 1) * HDIM]
            dq[n] = (mine * factor + cdq[pl.ds(n, 1), :]).astype(BF16)
        return 0

    lax.fori_loop(0, units // 2, pair, 0)

    def finish(group, _):
        for i in range(4):
            slot = group * 4 + i
            dk[slot] = (acc[slot, :, :HDIM] * factor + pk[pl.ds(slot, 1), :]).astype(BF16)
            dv[slot] = (acc[slot, :, HDIM:] + pv[pl.ds(slot, 1), :]).astype(BF16)
        return 0

    lax.fori_loop(0, SLOTS // 4, finish, 0)


def attend(tile_of_cube, select, qh, fh, ph, kh, vh):
    smem = pl.BlockSpec(memory_space=pltpu.SMEM)
    vmem = pl.BlockSpec(memory_space=pltpu.VMEM)
    query_shape = jax.ShapeDtypeStruct((UNITS, CUBE, HDIM), BF16)
    keys_shape = jax.ShapeDtypeStruct((SLOTS, CUBE, HDIM), BF16)
    return pl.pallas_call(
        attend_kernel,
        name="attend",
        out_shape=(query_shape, keys_shape, keys_shape),
        in_specs=[smem] * 2 + [vmem] * 5,
        out_specs=[vmem] * 3,
        scratch_shapes=[
            pltpu.VMEM((SLOTS, CUBE, 2 * HDIM), F32),
            pltpu.VMEM((2, 2 * CUBE, 2 * HDIM), BF16),
            pltpu.VMEM((SLOTS, HDIM), F32),
            pltpu.VMEM((SLOTS, HDIM), F32),
            pltpu.VMEM((UNITS, HDIM), F32),
            pltpu.VMEM((UNITS, HDIM), F32),
            pltpu.VMEM((SLOTS * 8, HDIM), F32),
            pltpu.VMEM((SLOTS * 8, HDIM), F32),
            pltpu.SMEM((SLOTS,), jnp.int32),
            pltpu.SMEM((SLOTS,), jnp.int32),
        ],
        compiler_params=pltpu.CompilerParams(vmem_limit_bytes=ATTEND_VMEM),
    )(
        tile_of_cube, select.T,
        qh.reshape(UNITS, CUBE, HDIM), fh.reshape(UNITS, CUBE, HDIM),
        ph.reshape(UNITS, 16, HDIM), kh.reshape(SLOTS, CUBE, HDIM), vh.reshape(SLOTS, CUBE, HDIM),
    )


def home_kernel(
    dq, dk, dv,
    oq, ok, ov,
    own_k, own_v, sib_k, sib_v, land_q, land_k, land_v, sum_k, sum_v, sum_q,
    ssend, srecv, psend, precv, zsend, zrecv,
):
    plane, chip, core = where_am_i()
    works, head, replica = role_of(chip)
    greet(plane, chip, core)
    sibling = device_of(plane, chip, 1 - core)
    sources, owns, sibs = (dk, dv), (own_k, own_v), (sib_k, sib_v)
    lands, sums, outs = (land_k, land_v), (sum_k, sum_v), (ok, ov)
    mine = columns(plane)

    @pl.when(works)
    def _():
        for number in range(2):
            def give(d, _, number=number):
                target = (chip + d) % CHIPS
                remote(
                    sources[number].at[(1 - core) * CHIPS + target], sibs[number].at[target],
                    ssend.at[number], srecv.at[number, target], sibling,
                ).start()
                return 0

            lax.fori_loop(0, CHIPS, give, 0)

        def send_query(m, _):
            i = (m + chip) % QGROUPS
            target = replica * QGROUPS + i

            @pl.when(target != chip)
            def _():
                remote(
                    dq.at[i], land_q.at[head], psend.at[2], precv.at[4],
                    device_of(plane, target, core),
                ).start()

            @pl.when(target == chip)
            def _():
                pltpu.make_async_copy(dq.at[i], land_q.at[head], precv.at[4]).start()

            return 0

        lax.fori_loop(0, QGROUPS, send_query, 0)

    def settle(number, half):
        rows = rows_of(half)
        source, own, sib, land = sources[number], owns[number], sibs[number], lands[number]

        def step(d, _):
            target = (chip + d) % CHIPS
            if half == 0:
                take_bytes(sib.at[target], srecv.at[number, target])
            own[target, :, rows] = (
                source[core * CHIPS + target, :, rows].astype(F32)
                + sib[target, :, rows].astype(F32)
            ).astype(BF16)
            arrived = precv.at[number * 2 + half]

            @pl.when(target != chip)
            def _():
                remote(
                    own.at[target, :, rows], land.at[replica, head, :, rows], psend.at[number],
                    arrived, device_of(plane, target, core),
                ).start()

            @pl.when(target == chip)
            def _():
                pltpu.make_async_copy(
                    own.at[target, :, rows], land.at[replica, head, :, rows], arrived
                ).start()

            return 0

        @pl.when(works)
        def _():
            lax.fori_loop(0, CHIPS, step, 0)

    def send_home(number, block, out, target):
        @pl.when(target != plane)
        def _():
            remote(
                block, out, zsend.at[number], zrecv.at[number], device_of(target, chip, core)
            ).start()

        @pl.when(target == plane)
        def _():
            pltpu.make_async_copy(block, out, zrecv.at[number]).start()

    def queries_home():
        take_bytes(land_q, precv.at[4])

        def step(d, _):
            target = (plane + d) % PLANES
            for j in range(HEADS_PLANE):
                sum_q[target, :, j * HDIM:(j + 1) * HDIM] = land_q[j, target]
            send_home(2, sum_q.at[target], oq.at[:, mine], target)
            return 0

        lax.fori_loop(0, PLANES, step, 0)

    def keys_home(number, half):
        rows = rows_of(half)
        land, total, out = lands[number], sums[number], outs[number]
        take_bytes(land.at[:, :, :, rows], precv.at[number * 2 + half])

        def step(d, _):
            target = (plane + d) % PLANES
            for j in range(HEADS_PLANE):
                summed = land[0, j, target, rows].astype(F32)
                for r in range(1, COPIES):
                    summed += land[r, j, target, rows].astype(F32)
                total[target, rows, j * HDIM:(j + 1) * HDIM] = summed.astype(BF16)
            send_home(number, total.at[target, rows], out.at[rows, mine], target)
            return 0

        lax.fori_loop(0, PLANES, step, 0)

    settle(0, 0)
    settle(0, 1)
    queries_home()
    keys_home(0, 0)
    settle(1, 0)
    keys_home(0, 1)
    settle(1, 1)
    keys_home(1, 0)
    keys_home(1, 1)

    for number, out in enumerate((ok, ov, oq)):
        take_bytes(out, zrecv.at[number])
        take_bytes(sum_q.at[pl.ds(0, PLANES - 1)], zsend.at[number])

    @pl.when(works)
    def _():
        for number in range(2):
            take_bytes(sibs[number], ssend.at[number])
            take_bytes(owns[number].at[pl.ds(0, CHIPS - 1)], psend.at[number])

        take_bytes(dq.at[pl.ds(0, QGROUPS - 1)], psend.at[2])


def home(dq, dk, dv, rows, width):
    anywhere = pl.BlockSpec(memory_space=pl.ANY)
    in_vmem = pl.BlockSpec(memory_space=pltpu.VMEM)
    out_shape = jax.ShapeDtypeStruct((rows, width), BF16)
    half = pltpu.VMEM((CHIPS, PLANES, CUBE, HDIM), BF16)
    slab = pltpu.VMEM((PLANES, CUBE, WIDTH), BF16)
    by_head = pltpu.VMEM((HEADS_PLANE, PLANES, CUBE, HDIM), BF16)
    copies = pltpu.VMEM((COPIES, HEADS_PLANE, PLANES, CUBE, HDIM), BF16)
    return pl.pallas_call(
        home_kernel,
        name="home",
        out_shape=(out_shape,) * 3,
        in_specs=[anywhere, in_vmem, in_vmem],
        out_specs=[anywhere] * 3,
        scratch_shapes=[
            half, half, half, half, by_head, copies, copies, slab, slab, slab,
            pltpu.SemaphoreType.DMA((2,)),
            pltpu.SemaphoreType.DMA((2, CHIPS)),
            pltpu.SemaphoreType.DMA((3,)),
            pltpu.SemaphoreType.DMA((5,)),
            pltpu.SemaphoreType.DMA((3,)),
            pltpu.SemaphoreType.DMA((3,)),
        ],
        compiler_params=pltpu.CompilerParams(
            collective_id=1, has_side_effects=True, vmem_limit_bytes=HOME_VMEM
        ),
    )(
        dq.reshape(QGROUPS, PLANES, CUBE, HDIM),
        dk.reshape(2 * CHIPS, PLANES, CUBE, HDIM),
        dv.reshape(2 * CHIPS, PLANES, CUBE, HDIM),
    )


def on_device(queries, keys_in, values, grad_out, fine_gate, coarse_gate, tile_of_cube, select):
    kh, vh, qh, fh, ph = bring(keys_in, values, queries, grad_out, fine_gate, coarse_gate)
    dq, dk, dv = attend(tile_of_cube, select, qh, fh, ph, kh, vh)
    return home(dq, dk, dv, *queries.shape)


def solution(mesh):
    split = P(("tok", "head"), None)
    return jax.shard_map(
        on_device,
        mesh=mesh,
        in_specs=(split,) * 6 + (P(), P()),
        out_specs=(split,) * 3,
        check_vma=False,
    )
```

```python
import functools
import math

import jax
import jax.numpy as jnp
from jax import lax
from jax.experimental import pallas as pl
from jax.experimental.pallas import tpu as pltpu
from jax.sharding import PartitionSpec as P

MESH = pl.DeviceIdType.MESH
BF16 = jnp.bfloat16
F32 = jnp.float32

CUBE = 64
HDIM = 128
PLANES = 8
CHIPS = 16
HEADS_PLANE = 5
COPIES = 2
WORKERS = HEADS_PLANE * COPIES
WIDTH = HEADS_PLANE * HDIM
QGROUPS = 8
TOPK = 16
SLOTS = 2 * CHIPS * PLANES
UNITS = QGROUPS * PLANES
HALF = CUBE // 2
STAGES = 8
ATTEND_VMEM = 30 * 2**20
HOME_VMEM = 20 * 2**20
BRING_VMEM = 16 * 2**20


def where_am_i():
    tok = lax.axis_index("tok")
    head = lax.axis_index("head")
    plane = tok // 4
    chip = (tok // 2) % 2 * 8 + head
    core = tok % 2
    return plane, chip, core


def role_of(chip):
    x, y = chip % 4, chip // 4
    plain = y % 2 == x % 2
    return plain | ((y % 2 == 1) & (x == y - 1)), jnp.where(plain, x, HEADS_PLANE - 1), y // 2


def chip_of(head, copy):
    return jnp.where(head < HEADS_PLANE - 1, head % 2 * 4 + 8 * copy + head, 10 * copy + 4)


def lean_of(head):
    return jnp.where(head < HEADS_PLANE - 1, 0, 3)


def asks(head, chip):
    turned = (chip // 4 + lean_of(head)) % 4
    return turned // 2, turned % 2 * 4 + chip % 4


def asked_by(head, copy, group):
    return (2 * copy + group // 4 + 4 - lean_of(head)) % 4 * 4 + group % 4


def device_of(plane, chip, core):
    return {"tok": plane * 4 + chip // 8 * 2 + core, "head": chip % 8}


def remote(src, dst, send, recv, device):
    return pltpu.make_async_remote_copy(
        src_ref=src, dst_ref=dst, send_sem=send, recv_sem=recv, device_id=device, device_id_type=MESH
    )


def take_bytes(ref, sem):
    pltpu.make_async_copy(ref, ref, sem).wait()


def greet(plane, chip, core):
    barrier = pltpu.get_barrier_semaphore()

    def along_z(d, _):
        pl.semaphore_signal(
            barrier, inc=1, device_id=device_of((plane + d) % PLANES, chip, core), device_id_type=MESH
        )
        return 0

    def in_plane(d, _):
        pl.semaphore_signal(
            barrier, inc=1, device_id=device_of(plane, (chip + d) % CHIPS, core), device_id_type=MESH
        )
        return 0

    lax.fori_loop(1, PLANES, along_z, 0)
    lax.fori_loop(1, CHIPS, in_plane, 0)
    pl.semaphore_signal(
        barrier, inc=1, device_id=device_of(plane, chip, 1 - core), device_id_type=MESH
    )
    pl.semaphore_wait(barrier, PLANES - 1 + CHIPS - 1 + 1)


def columns(group, width=WIDTH):
    return pl.ds(pl.multiple_of(group * width, 128), width)


def rows_of(half):
    return pl.ds(half * HALF, HALF)


def bring_kernel(
    k_in, v_in, q_in, g_in, fgate, cgate,
    kh, vh, qh, fh, ph,
    packed, kz, vz, qz, fz, pz, pg,
    zsend, zrecv, psend, krecv, qrecv, fsend, frecv,
):
    plane, chip, core = where_am_i()
    greet(plane, chip, core)

    def start_along_z(stage, source, landing):
        def step(d, _):
            target = (plane + d) % PLANES
            remote(
                source(target), landing(plane), zsend.at[stage], zrecv.at[stage],
                device_of(target, chip, core),
            ).start()
            return 0

        lax.fori_loop(1, PLANES, step, 0)
        pltpu.make_async_copy(source(plane), landing(plane), zrecv.at[stage]).start()

    slabs = (kz, vz, qz, fz)
    outs = (kh, vh, qh, fh)

    def start_stage(stage):
        number, rows = stage // 2, rows_of(stage % 2)
        start_along_z(
            stage,
            lambda t: packed.at[number, t, :, rows],
            lambda t: slabs[number].at[:, t, rows],
        )

    def pack(number, source):
        def step(group, _):
            for j in range(HEADS_PLANE):
                packed[number, group, j] = source[:, columns(group * HEADS_PLANE + j, HDIM)]
            return 0

        lax.fori_loop(0, PLANES, step, 0)

    pack(0, k_in)
    start_stage(0)
    pack(1, v_in)
    pack(2, q_in)

    def gates(group, _):
        row = lax.broadcasted_iota(jnp.int32, (fgate.shape[0], WIDTH), 0)
        col = lax.broadcasted_iota(jnp.int32, (fgate.shape[0], WIDTH), 1)
        spread = jnp.where(
            row == group * HEADS_PLANE + lax.shift_right_logical(col, 7), 1.0, 0.0
        ).astype(BF16)
        grad = g_in[:, columns(group)].astype(F32)
        fine = (tn(fgate[...], spread) * grad).astype(BF16)
        coarse = tn(cgate[...], spread)
        pooled = jnp.sum(coarse * grad, axis=0, keepdims=True)
        rows = []
        for j in range(HEADS_PLANE):
            packed[3, group, j] = fine[:, j * HDIM:(j + 1) * HDIM]
            rows.append(pooled[:, j * HDIM:(j + 1) * HDIM])
        rows.append(jnp.zeros((16 - HEADS_PLANE, HDIM), F32))
        pg[group] = jnp.concatenate(rows, axis=0).astype(BF16)
        return 0

    lax.fori_loop(0, PLANES, gates, 0)
    start_stage(1)
    works, _, _ = role_of(chip)

    def share_keys(number, rows):
        landed, out = slabs[number], outs[number]

        def step(m, _):
            worker = (m + chip) % WORKERS
            head = worker % HEADS_PLANE
            target = chip_of(head, worker // HEADS_PLANE)
            here, there = landed.at[head, :, rows], out.at[core * CHIPS + chip, :, rows]

            @pl.when(target != chip)
            def _():
                remote(
                    here, there, psend.at[number], krecv.at[number, chip],
                    device_of(plane, target, core),
                ).start()

            @pl.when(target == chip)
            def _():
                pltpu.make_async_copy(here, there, krecv.at[number, chip]).start()

            return 0

        lax.fori_loop(0, WORKERS, step, 0)

    def share_queries(number, pick, place):
        def step(m, _):
            j = (m + chip) % HEADS_PLANE
            copy, group = asks(j, chip)
            target = chip_of(j, copy)

            @pl.when(target != chip)
            def _():
                remote(
                    pick(j), place(group), psend.at[number],
                    qrecv.at[number - 2], device_of(plane, target, core),
                ).start()

            @pl.when(target == chip)
            def _():
                pltpu.make_async_copy(
                    pick(j), place(group), qrecv.at[number - 2]
                ).start()

            return 0

        lax.fori_loop(0, HEADS_PLANE, step, 0)

    for stage in range(STAGES):
        number, rows = stage // 2, rows_of(stage % 2)
        take_bytes(slabs[number].at[:, :, rows], zrecv.at[stage])
        if stage + 2 < STAGES:
            start_stage(stage + 2)
        if stage + 2 == STAGES:
            start_along_z(STAGES, lambda t: pg.at[t], lambda t: pz.at[t])
        if number < 2:
            share_keys(number, rows)
        else:
            share_queries(
                number,
                lambda j, number=number, rows=rows: slabs[number].at[j, :, rows],
                lambda i, number=number, rows=rows: outs[number].at[i, :, rows],
            )
    take_bytes(pz, zrecv.at[STAGES])
    share_queries(4, lambda j: pz, lambda i: ph.at[i])

    sibling = device_of(plane, chip, 1 - core)

    @pl.when(works)
    def _():
        for number, out in ((0, kh), (1, vh)):
            def forward(d, _, number=number, out=out):
                origin = (chip + CHIPS - d) % CHIPS
                block = out.at[core * CHIPS + origin]
                take_bytes(block, krecv.at[number, origin])
                remote(block, block, fsend.at[number], frecv.at[number], sibling).start()
                return 0

            lax.fori_loop(0, CHIPS, forward, 0)

        for number, out in enumerate((qh, fh, ph)):
            take_bytes(out, qrecv.at[number])

        for number, out in ((0, kh), (1, vh)):
            theirs = out.at[pl.ds((1 - core) * CHIPS, CHIPS)]
            take_bytes(theirs, frecv.at[number])
            take_bytes(theirs, fsend.at[number])

    for stage in range(STAGES):
        landed = slabs[stage // 2].at[:, pl.ds(0, PLANES - 1), rows_of(stage % 2)]
        take_bytes(landed, zsend.at[stage])
    take_bytes(pz.at[pl.ds(0, PLANES - 1)], zsend.at[STAGES])

    def drain(keys, queries):
        for number, out in ((0, kh), (1, vh)):
            take_bytes(out.at[pl.ds(0, keys)], psend.at[number])
        for number, out in ((2, qh), (3, fh), (4, ph)):
            take_bytes(out.at[pl.ds(0, queries)], psend.at[number])

    @pl.when(works)
    def _():
        drain(WORKERS - 1, HEADS_PLANE - 1)

    @pl.when(jnp.logical_not(works))
    def _():
        drain(WORKERS, HEADS_PLANE)


def bring(keys_in, values, queries, grad_out, fine_gate, coarse_gate):
    keys_shape = jax.ShapeDtypeStruct((2 * CHIPS, PLANES, CUBE, HDIM), BF16)
    query_shape = jax.ShapeDtypeStruct((QGROUPS, PLANES, CUBE, HDIM), BF16)
    pooled_shape = jax.ShapeDtypeStruct((QGROUPS, PLANES, 16, HDIM), BF16)
    anywhere = pl.BlockSpec(memory_space=pl.ANY)
    in_vmem = pl.BlockSpec(memory_space=pltpu.VMEM)
    slab = pltpu.VMEM((HEADS_PLANE, PLANES, CUBE, HDIM), BF16)
    small = pltpu.VMEM((PLANES, 16, HDIM), BF16)
    return pl.pallas_call(
        bring_kernel,
        name="bring",
        out_shape=(keys_shape, keys_shape, query_shape, query_shape, pooled_shape),
        in_specs=[in_vmem] * 6,
        out_specs=[anywhere] * 5,
        scratch_shapes=[
            pltpu.VMEM((4, PLANES, HEADS_PLANE, CUBE, HDIM), BF16),
            slab, slab, slab, slab, small, small,
            pltpu.SemaphoreType.DMA((STAGES + 1,)),
            pltpu.SemaphoreType.DMA((STAGES + 1,)),
            pltpu.SemaphoreType.DMA((5,)),
            pltpu.SemaphoreType.DMA((2, CHIPS)),
            pltpu.SemaphoreType.DMA((3,)),
            pltpu.SemaphoreType.DMA((2,)),
            pltpu.SemaphoreType.DMA((2,)),
        ],
        compiler_params=pltpu.CompilerParams(
            collective_id=0, has_side_effects=True, vmem_limit_bytes=BRING_VMEM
        ),
    )(keys_in, values, queries, grad_out, fine_gate.T, coarse_gate.T)


def nt(a, b):
    return lax.dot_general(a, b, (((1,), (1,)), ((), ())), preferred_element_type=F32)


def tn(a, b):
    return lax.dot_general(a, b, (((0,), (0,)), ((), ())), preferred_element_type=F32)


def nn(a, b):
    return jnp.dot(a, b, preferred_element_type=F32)


def attend_kernel(
    toc, sel, q, fg, pg, k, v,
    dq, dk, dv,
    ak, av, wide_0, wide_1, prob_0, prob_1, dsc_0, dsc_1,
    pk, pv, pq, cdq, part_k, part_v, cot, soc, held,
):
    _, chip, core = where_am_i()
    works, head, copy = role_of(chip)
    units = jnp.where(works, UNITS, 0)
    factor = 1.0 / math.sqrt(HDIM)
    log2e = math.log2(math.e)

    def eighths(source, group):
        block = source[pl.ds(pl.multiple_of(group * 8, 8), 8)].astype(F32)
        return jnp.sum(block.reshape(8, 8, 8, HDIM), axis=1).reshape(64, HDIM)

    def prepare(group, _):
        rows = pl.ds(pl.multiple_of(group * 64, 64), 64)
        part_k[rows, :] = eighths(k, group)
        part_v[rows, :] = eighths(v, group)
        for total_of in (ak, av):
            total_of[pl.ds(pl.multiple_of(group * 8, 8), 8)] = jnp.zeros((8, CUBE, HDIM), F32)
        for i in range(8):
            cube = group * 8 + i
            tile = toc[cube]
            cot[tile] = cube
            soc[cube] = (
                lax.shift_left(lax.shift_right_logical(tile, 3) & 1, 7)
                + lax.shift_left(lax.shift_right_logical(tile, 4) & 1, 6)
                + lax.shift_left(tile & 7, 3)
                + lax.shift_right_logical(tile, 5)
            )
        return 0

    lax.fori_loop(0, SLOTS // 8, prepare, 0)

    def pool(part, into):
        count = into.shape[0]
        total = part[pl.ds(0, count, stride=8), :]
        for row in range(1, 8):
            total += part[pl.ds(row, count, stride=8), :]
        into[...] = total * (1.0 / CUBE)

    pool(part_k, pk)
    pool(part_v, pv)

    def prepare_queries(group, _):
        part_k[pl.ds(pl.multiple_of(group * 64, 64), 64), :] = eighths(q, group)
        return 0

    lax.fori_loop(0, QGROUPS, prepare_queries, 0)
    pool(part_k, pq)
    row_at = lax.broadcasted_iota(jnp.int32, (UNITS, 16, HDIM), 1)
    pooled_g = jnp.sum(
        jnp.where(row_at == head, pg[...].astype(F32), 0.0), axis=1
    ).astype(BF16)
    pooled_q = pq[...].astype(BF16)
    pooled_k = pk[...].astype(BF16)
    pooled_v = pv[...].astype(BF16)
    scores = nt(pooled_q, pooled_k) * factor
    weights = jnp.exp(scores - jnp.max(scores, axis=1, keepdims=True))
    probs = weights / jnp.sum(weights, axis=1, keepdims=True)
    dprobs = nt(pooled_g, pooled_v)
    inner = jnp.sum(probs * dprobs, axis=1, keepdims=True)
    dscores = (probs * (dprobs - inner)).astype(BF16)
    cdq[...] = nn(dscores, pooled_k) * (factor / CUBE)
    pk[...] = tn(dscores, pooled_q) * (factor / CUBE)
    pv[...] = tn(probs.astype(BF16), pooled_g) * (1.0 / CUBE)
    wide_0[...] = jnp.zeros_like(wide_0)
    wide_1[...] = jnp.zeros_like(wide_1)

    def listed(n):
        origin = asked_by(head, copy, n // PLANES)
        tile = (n % PLANES * 4 + origin // 8 * 2 + core) * 8 + origin % 8
        cube = cot[tile]
        return [soc[sel[r, cube]] for r in range(TOPK)]

    def beside(ref, lists, c):
        return jnp.concatenate(
            [jnp.concatenate([ref[s] for s in slots[c * 4:c * 4 + 4]], axis=0) for slots in lists],
            axis=1,
        )

    sides = ((prob_0, dsc_0, wide_0), (prob_1, dsc_1, wide_1))

    def advance(old, m_old, new, m_new):
        prob_new, dsc_new, wide_new = sides[new]
        lists_new = [listed(2 * m_new + i) for i in range(2)]
        for i, slots in enumerate(lists_new):
            for r, slot in enumerate(slots):
                held[new, i * TOPK + r] = slot
            rows, lanes = slice(i * CUBE, (i + 1) * CUBE), slice(i * HDIM, (i + 1) * HDIM)
            wide_new[0, rows, lanes] = q[2 * m_new + i]
            wide_new[1, rows, lanes] = fg[2 * m_new + i]
        score, dprob = [], []
        if old is not None:
            prob_old, dsc_old, wide_old = sides[old]
            lists_old = [[held[old, i * TOPK + r] for r in range(TOPK)] for i in range(2)]
            dquery = jnp.zeros((2 * CUBE, 2 * HDIM), F32)
        for c in range(4):
            score.append(nt(beside(k, lists_new, c), wide_new[0]))
            dprob.append(nt(beside(v, lists_new, c), wide_new[1]))
            if old is None:
                continue
            chunk = slice(c * 4 * CUBE, (c + 1) * 4 * CUBE)
            dscore = dsc_old[chunk]
            dquery += tn(dscore, beside(k, lists_old, c))
            key_terms = nn(dscore, wide_old[0])
            value_terms = nn(prob_old[chunk], wide_old[1])
            for i, slots in enumerate(lists_old):
                lanes = slice(i * HDIM, (i + 1) * HDIM)
                for total_of, terms in ((ak, key_terms), (av, value_terms)):
                    before = [total_of[s] for s in slots[c * 4:c * 4 + 4]]
                    for at, s in enumerate(slots[c * 4:c * 4 + 4]):
                        total_of[s] = before[at] + terms[at * CUBE:(at + 1) * CUBE, lanes]
        top = jnp.max(functools.reduce(jnp.maximum, score), axis=0, keepdims=True)
        weight = [jnp.exp2((s - top) * (factor * log2e)) for s in score]
        total = jnp.sum(functools.reduce(jnp.add, weight), axis=0, keepdims=True)
        inverse = 1.0 / total
        mixed = functools.reduce(jnp.add, [w * d for w, d in zip(weight, dprob)])
        center = jnp.sum(mixed, axis=0, keepdims=True) * inverse
        for c in range(4):
            chunk = slice(c * 4 * CUBE, (c + 1) * 4 * CUBE)
            prob = weight[c] * inverse
            prob_new[chunk] = prob.astype(BF16)
            dsc_new[chunk] = (prob * (dprob[c] - center)).astype(BF16)
        if old is not None:
            for i in range(2):
                n = 2 * m_old + i
                mine = dquery[i * CUBE:(i + 1) * CUBE, i * HDIM:(i + 1) * HDIM]
                dq[n] = (mine * factor + cdq[pl.ds(n, 1), :]).astype(BF16)

    advance(None, 0, 0, 0)

    def two_pairs(m, _):
        advance(0, 2 * m, 1, 2 * m + 1)
        advance(1, 2 * m + 1, 0, jnp.minimum(2 * m + 2, UNITS // 2 - 1))
        return 0

    lax.fori_loop(0, units // 4, two_pairs, 0)

    def finish(group, _):
        for i in range(4):
            slot = group * 4 + i
            dk[slot] = (ak[slot] * factor + pk[pl.ds(slot, 1), :]).astype(BF16)
            dv[slot] = (av[slot] + pv[pl.ds(slot, 1), :]).astype(BF16)
        return 0

    lax.fori_loop(0, SLOTS // 4, finish, 0)


def attend(tile_of_cube, select, qh, fh, ph, kh, vh):
    smem = pl.BlockSpec(memory_space=pltpu.SMEM)
    vmem = pl.BlockSpec(memory_space=pltpu.VMEM)
    query_shape = jax.ShapeDtypeStruct((UNITS, CUBE, HDIM), BF16)
    keys_shape = jax.ShapeDtypeStruct((SLOTS, CUBE, HDIM), BF16)
    return pl.pallas_call(
        attend_kernel,
        name="attend",
        out_shape=(query_shape, keys_shape, keys_shape),
        in_specs=[smem] * 2 + [vmem] * 5,
        out_specs=[vmem] * 3,
        scratch_shapes=[
            pltpu.VMEM((SLOTS, CUBE, HDIM), F32),
            pltpu.VMEM((SLOTS, CUBE, HDIM), F32),
            pltpu.VMEM((2, 2 * CUBE, 2 * HDIM), BF16),
            pltpu.VMEM((2, 2 * CUBE, 2 * HDIM), BF16),
            pltpu.VMEM((TOPK * CUBE, 2 * CUBE), BF16),
            pltpu.VMEM((TOPK * CUBE, 2 * CUBE), BF16),
            pltpu.VMEM((TOPK * CUBE, 2 * CUBE), BF16),
            pltpu.VMEM((TOPK * CUBE, 2 * CUBE), BF16),
            pltpu.VMEM((SLOTS, HDIM), F32),
            pltpu.VMEM((SLOTS, HDIM), F32),
            pltpu.VMEM((UNITS, HDIM), F32),
            pltpu.VMEM((UNITS, HDIM), F32),
            pltpu.VMEM((SLOTS * 8, HDIM), F32),
            pltpu.VMEM((SLOTS * 8, HDIM), F32),
            pltpu.SMEM((SLOTS,), jnp.int32),
            pltpu.SMEM((SLOTS,), jnp.int32),
            pltpu.SMEM((2, 2 * TOPK), jnp.int32),
        ],
        compiler_params=pltpu.CompilerParams(vmem_limit_bytes=ATTEND_VMEM),
    )(
        tile_of_cube, select.T,
        qh.reshape(UNITS, CUBE, HDIM), fh.reshape(UNITS, CUBE, HDIM),
        ph.reshape(UNITS, 16, HDIM), kh.reshape(SLOTS, CUBE, HDIM), vh.reshape(SLOTS, CUBE, HDIM),
    )


def home_kernel(
    dq, dk, dv,
    oq, ok, ov,
    own_k, own_v, sib_k, sib_v, land_q, land_k, land_v, sum_k, sum_v, sum_q,
    ssend, srecv, psend, precv, zsend, zrecv,
):
    plane, chip, core = where_am_i()
    works, head, replica = role_of(chip)
    greet(plane, chip, core)
    sibling = device_of(plane, chip, 1 - core)
    sources, owns, sibs = (dk, dv), (own_k, own_v), (sib_k, sib_v)
    lands, sums, outs = (land_k, land_v), (sum_k, sum_v), (ok, ov)
    mine = columns(plane)

    @pl.when(works)
    def _():
        for number in range(2):
            def give(d, _, number=number):
                target = (chip + d) % CHIPS
                remote(
                    sources[number].at[(1 - core) * CHIPS + target], sibs[number].at[target],
                    ssend.at[number], srecv.at[number, target], sibling,
                ).start()
                return 0

            lax.fori_loop(0, CHIPS, give, 0)

        def send_query(m, _):
            i = (m + chip) % QGROUPS
            target = asked_by(head, replica, i)

            @pl.when(target != chip)
            def _():
                remote(
                    dq.at[i], land_q.at[head], psend.at[2], precv.at[4],
                    device_of(plane, target, core),
                ).start()

            @pl.when(target == chip)
            def _():
                pltpu.make_async_copy(dq.at[i], land_q.at[head], precv.at[4]).start()

            return 0

        lax.fori_loop(0, QGROUPS, send_query, 0)

    def settle(number, half):
        rows = rows_of(half)
        source, own, sib, land = sources[number], owns[number], sibs[number], lands[number]

        def step(d, _):
            target = (chip + d) % CHIPS
            if half == 0:
                take_bytes(sib.at[target], srecv.at[number, target])
            own[target, :, rows] = (
                source[core * CHIPS + target, :, rows].astype(F32)
                + sib[target, :, rows].astype(F32)
            ).astype(BF16)
            arrived = precv.at[number * 2 + half]

            @pl.when(target != chip)
            def _():
                remote(
                    own.at[target, :, rows], land.at[replica, head, :, rows], psend.at[number],
                    arrived, device_of(plane, target, core),
                ).start()

            @pl.when(target == chip)
            def _():
                pltpu.make_async_copy(
                    own.at[target, :, rows], land.at[replica, head, :, rows], arrived
                ).start()

            return 0

        @pl.when(works)
        def _():
            lax.fori_loop(0, CHIPS, step, 0)

    def send_home(number, block, out, target):
        @pl.when(target != plane)
        def _():
            remote(
                block, out, zsend.at[number], zrecv.at[number], device_of(target, chip, core)
            ).start()

        @pl.when(target == plane)
        def _():
            pltpu.make_async_copy(block, out, zrecv.at[number]).start()

    def queries_home():
        take_bytes(land_q, precv.at[4])

        def step(d, _):
            target = (plane + d) % PLANES
            for j in range(HEADS_PLANE):
                sum_q[target, :, j * HDIM:(j + 1) * HDIM] = land_q[j, target]
            send_home(2, sum_q.at[target], oq.at[:, mine], target)
            return 0

        lax.fori_loop(0, PLANES, step, 0)

    def keys_home(number, half):
        rows = rows_of(half)
        land, total, out = lands[number], sums[number], outs[number]
        take_bytes(land.at[:, :, :, rows], precv.at[number * 2 + half])

        def step(d, _):
            target = (plane + d) % PLANES
            for j in range(HEADS_PLANE):
                summed = land[0, j, target, rows].astype(F32)
                for r in range(1, COPIES):
                    summed += land[r, j, target, rows].astype(F32)
                total[target, rows, j * HDIM:(j + 1) * HDIM] = summed.astype(BF16)
            send_home(number, total.at[target, rows], out.at[rows, mine], target)
            return 0

        lax.fori_loop(0, PLANES, step, 0)

    settle(0, 0)
    settle(0, 1)
    queries_home()
    keys_home(0, 0)
    settle(1, 0)
    keys_home(0, 1)
    settle(1, 1)
    keys_home(1, 0)
    keys_home(1, 1)

    for number, out in enumerate((ok, ov, oq)):
        take_bytes(out, zrecv.at[number])
        take_bytes(sum_q.at[pl.ds(0, PLANES - 1)], zsend.at[number])

    @pl.when(works)
    def _():
        for number in range(2):
            take_bytes(sibs[number], ssend.at[number])
            take_bytes(owns[number].at[pl.ds(0, CHIPS - 1)], psend.at[number])

        take_bytes(dq.at[pl.ds(0, QGROUPS - 1)], psend.at[2])


def home(dq, dk, dv, rows, width):
    anywhere = pl.BlockSpec(memory_space=pl.ANY)
    in_vmem = pl.BlockSpec(memory_space=pltpu.VMEM)
    out_shape = jax.ShapeDtypeStruct((rows, width), BF16)
    half = pltpu.VMEM((CHIPS, PLANES, CUBE, HDIM), BF16)
    slab = pltpu.VMEM((PLANES, CUBE, WIDTH), BF16)
    by_head = pltpu.VMEM((HEADS_PLANE, PLANES, CUBE, HDIM), BF16)
    copies = pltpu.VMEM((COPIES, HEADS_PLANE, PLANES, CUBE, HDIM), BF16)
    return pl.pallas_call(
        home_kernel,
        name="home",
        out_shape=(out_shape,) * 3,
        in_specs=[anywhere, in_vmem, in_vmem],
        out_specs=[anywhere] * 3,
        scratch_shapes=[
            half, half, half, half, by_head, copies, copies, slab, slab, slab,
            pltpu.SemaphoreType.DMA((2,)),
            pltpu.SemaphoreType.DMA((2, CHIPS)),
            pltpu.SemaphoreType.DMA((3,)),
            pltpu.SemaphoreType.DMA((5,)),
            pltpu.SemaphoreType.DMA((3,)),
            pltpu.SemaphoreType.DMA((3,)),
        ],
        compiler_params=pltpu.CompilerParams(
            collective_id=1, has_side_effects=True, vmem_limit_bytes=HOME_VMEM
        ),
    )(
        dq.reshape(QGROUPS, PLANES, CUBE, HDIM),
        dk.reshape(2 * CHIPS, PLANES, CUBE, HDIM),
        dv.reshape(2 * CHIPS, PLANES, CUBE, HDIM),
    )


def on_device(queries, keys_in, values, grad_out, fine_gate, coarse_gate, tile_of_cube, select):
    kh, vh, qh, fh, ph = bring(keys_in, values, queries, grad_out, fine_gate, coarse_gate)
    dq, dk, dv = attend(tile_of_cube, select, qh, fh, ph, kh, vh)
    return home(dq, dk, dv, *queries.shape)


def solution(mesh):
    split = P(("tok", "head"), None)
    return jax.shard_map(
        on_device,
        mesh=mesh,
        in_specs=(split,) * 6 + (P(), P()),
        out_specs=(split,) * 3,
        check_vma=False,
    )
```

```python
import functools
import math

import jax
import jax.numpy as jnp
from jax import lax
from jax.experimental import pallas as pl
from jax.experimental.pallas import tpu as pltpu
from jax.sharding import PartitionSpec as P

MESH = pl.DeviceIdType.MESH
BF16 = jnp.bfloat16
F32 = jnp.float32

CUBE = 64
HDIM = 128
PLANES = 8
CHIPS = 16
HEADS_PLANE = 5
COPIES = 2
WORKERS = HEADS_PLANE * COPIES
WIDTH = HEADS_PLANE * HDIM
QGROUPS = 8
TOPK = 16
SLOTS = 2 * CHIPS * PLANES
UNITS = QGROUPS * PLANES
HALF = CUBE // 2
STAGES = 8
ATTEND_VMEM = 30 * 2**20
HOME_VMEM = 20 * 2**20
BRING_VMEM = 16 * 2**20


def where_am_i():
    tok = lax.axis_index("tok")
    head = lax.axis_index("head")
    plane = tok // 4
    chip = (tok // 2) % 2 * 8 + head
    core = tok % 2
    return plane, chip, core


def role_of(chip):
    x, y = chip % 4, chip // 4
    plain = y % 2 == x % 2
    return plain | ((y % 2 == 1) & (x == y - 1)), jnp.where(plain, x, HEADS_PLANE - 1), y // 2


def chip_of(head, copy):
    return jnp.where(head < HEADS_PLANE - 1, head % 2 * 4 + 8 * copy + head, 10 * copy + 4)


def odd_rows(head):
    return jnp.where(head < HEADS_PLANE - 1, head % 2, 1)


def asks(head, chip):
    x, y = chip % 4, chip // 4
    own = y % 2 == odd_rows(head)
    row = jnp.where(own, y, (y + 5 - 2 * ((x + head) % 2)) % 4)
    return row // 2, jnp.where(own, x, 4 + x)


def asked_by(head, copy, group):
    x, row = group % 4, odd_rows(head) + 2 * copy
    y = jnp.where(group < 4, row, (row + 3 + 2 * ((x + head) % 2)) % 4)
    return y * 4 + x


def device_of(plane, chip, core):
    return {"tok": plane * 4 + chip // 8 * 2 + core, "head": chip % 8}


def remote(src, dst, send, recv, device):
    return pltpu.make_async_remote_copy(
        src_ref=src, dst_ref=dst, send_sem=send, recv_sem=recv, device_id=device, device_id_type=MESH
    )


def take_bytes(ref, sem):
    pltpu.make_async_copy(ref, ref, sem).wait()


def greet(plane, chip, core):
    barrier = pltpu.get_barrier_semaphore()

    def along_z(d, _):
        pl.semaphore_signal(
            barrier, inc=1, device_id=device_of((plane + d) % PLANES, chip, core), device_id_type=MESH
        )
        return 0

    def in_plane(d, _):
        pl.semaphore_signal(
            barrier, inc=1, device_id=device_of(plane, (chip + d) % CHIPS, core), device_id_type=MESH
        )
        return 0

    lax.fori_loop(1, PLANES, along_z, 0)
    lax.fori_loop(1, CHIPS, in_plane, 0)
    pl.semaphore_signal(
        barrier, inc=1, device_id=device_of(plane, chip, 1 - core), device_id_type=MESH
    )
    pl.semaphore_wait(barrier, PLANES - 1 + CHIPS - 1 + 1)


def columns(group, width=WIDTH):
    return pl.ds(pl.multiple_of(group * width, 128), width)


def rows_of(half):
    return pl.ds(half * HALF, HALF)


def bring_kernel(
    k_in, v_in, q_in, g_in, fgate, cgate,
    kh, vh, qh, fh, ph,
    packed, kz, vz, qz, fz, pz, pg,
    zsend, zrecv, psend, krecv, qrecv, fsend, frecv,
):
    plane, chip, core = where_am_i()
    greet(plane, chip, core)

    def start_along_z(stage, source, landing):
        def step(d, _):
            target = (plane + d) % PLANES
            remote(
                source(target), landing(plane), zsend.at[stage], zrecv.at[stage],
                device_of(target, chip, core),
            ).start()
            return 0

        lax.fori_loop(1, PLANES, step, 0)
        pltpu.make_async_copy(source(plane), landing(plane), zrecv.at[stage]).start()

    slabs = (kz, vz, qz, fz)
    outs = (kh, vh, qh, fh)

    def start_stage(stage):
        number, rows = stage // 2, rows_of(stage % 2)
        start_along_z(
            stage,
            lambda t: packed.at[number, t, :, rows],
            lambda t: slabs[number].at[:, t, rows],
        )

    def pack(number, source):
        def step(group, _):
            for j in range(HEADS_PLANE):
                packed[number, group, j] = source[:, columns(group * HEADS_PLANE + j, HDIM)]
            return 0

        lax.fori_loop(0, PLANES, step, 0)

    pack(0, k_in)
    start_stage(0)
    pack(1, v_in)
    pack(2, q_in)

    def gates(group, _):
        row = lax.broadcasted_iota(jnp.int32, (fgate.shape[0], WIDTH), 0)
        col = lax.broadcasted_iota(jnp.int32, (fgate.shape[0], WIDTH), 1)
        spread = jnp.where(
            row == group * HEADS_PLANE + lax.shift_right_logical(col, 7), 1.0, 0.0
        ).astype(BF16)
        grad = g_in[:, columns(group)].astype(F32)
        fine = (tn(fgate[...], spread) * grad).astype(BF16)
        coarse = tn(cgate[...], spread)
        pooled = jnp.sum(coarse * grad, axis=0, keepdims=True)
        rows = []
        for j in range(HEADS_PLANE):
            packed[3, group, j] = fine[:, j * HDIM:(j + 1) * HDIM]
            rows.append(pooled[:, j * HDIM:(j + 1) * HDIM])
        rows.append(jnp.zeros((16 - HEADS_PLANE, HDIM), F32))
        pg[group] = jnp.concatenate(rows, axis=0).astype(BF16)
        return 0

    lax.fori_loop(0, PLANES, gates, 0)
    start_stage(1)
    works, _, _ = role_of(chip)

    def share_keys(number, rows):
        landed, out = slabs[number], outs[number]

        def step(m, _):
            worker = (m + chip) % WORKERS
            head = worker % HEADS_PLANE
            target = chip_of(head, worker // HEADS_PLANE)
            here, there = landed.at[head, :, rows], out.at[core * CHIPS + chip, :, rows]

            @pl.when(target != chip)
            def _():
                remote(
                    here, there, psend.at[number], krecv.at[number, chip],
                    device_of(plane, target, core),
                ).start()

            @pl.when(target == chip)
            def _():
                pltpu.make_async_copy(here, there, krecv.at[number, chip]).start()

            return 0

        lax.fori_loop(0, WORKERS, step, 0)

    def share_queries(number, pick, place):
        def step(m, _):
            j = (m + chip) % HEADS_PLANE
            copy, group = asks(j, chip)
            target = chip_of(j, copy)

            @pl.when(target != chip)
            def _():
                remote(
                    pick(j), place(group), psend.at[number],
                    qrecv.at[number - 2], device_of(plane, target, core),
                ).start()

            @pl.when(target == chip)
            def _():
                pltpu.make_async_copy(
                    pick(j), place(group), qrecv.at[number - 2]
                ).start()

            return 0

        lax.fori_loop(0, HEADS_PLANE, step, 0)

    for stage in range(STAGES):
        number, rows = stage // 2, rows_of(stage % 2)
        take_bytes(slabs[number].at[:, :, rows], zrecv.at[stage])
        if stage + 2 < STAGES:
            start_stage(stage + 2)
        if stage + 2 == STAGES:
            start_along_z(STAGES, lambda t: pg.at[t], lambda t: pz.at[t])
        if number < 2:
            share_keys(number, rows)
        else:
            share_queries(
                number,
                lambda j, number=number, rows=rows: slabs[number].at[j, :, rows],
                lambda i, number=number, rows=rows: outs[number].at[i, :, rows],
            )
    take_bytes(pz, zrecv.at[STAGES])
    share_queries(4, lambda j: pz, lambda i: ph.at[i])

    sibling = device_of(plane, chip, 1 - core)

    @pl.when(works)
    def _():
        for number, out in ((0, kh), (1, vh)):
            def forward(d, _, number=number, out=out):
                origin = (chip + CHIPS - d) % CHIPS
                block = out.at[core * CHIPS + origin]
                take_bytes(block, krecv.at[number, origin])
                remote(block, block, fsend.at[number], frecv.at[number], sibling).start()
                return 0

            lax.fori_loop(0, CHIPS, forward, 0)

        for number, out in enumerate((qh, fh, ph)):
            take_bytes(out, qrecv.at[number])

        for number, out in ((0, kh), (1, vh)):
            theirs = out.at[pl.ds((1 - core) * CHIPS, CHIPS)]
            take_bytes(theirs, frecv.at[number])
            take_bytes(theirs, fsend.at[number])

    for stage in range(STAGES):
        landed = slabs[stage // 2].at[:, pl.ds(0, PLANES - 1), rows_of(stage % 2)]
        take_bytes(landed, zsend.at[stage])
    take_bytes(pz.at[pl.ds(0, PLANES - 1)], zsend.at[STAGES])

    def drain(keys, queries):
        for number, out in ((0, kh), (1, vh)):
            take_bytes(out.at[pl.ds(0, keys)], psend.at[number])
        for number, out in ((2, qh), (3, fh), (4, ph)):
            take_bytes(out.at[pl.ds(0, queries)], psend.at[number])

    @pl.when(works)
    def _():
        drain(WORKERS - 1, HEADS_PLANE - 1)

    @pl.when(jnp.logical_not(works))
    def _():
        drain(WORKERS, HEADS_PLANE)


def bring(keys_in, values, queries, grad_out, fine_gate, coarse_gate):
    keys_shape = jax.ShapeDtypeStruct((2 * CHIPS, PLANES, CUBE, HDIM), BF16)
    query_shape = jax.ShapeDtypeStruct((QGROUPS, PLANES, CUBE, HDIM), BF16)
    pooled_shape = jax.ShapeDtypeStruct((QGROUPS, PLANES, 16, HDIM), BF16)
    anywhere = pl.BlockSpec(memory_space=pl.ANY)
    in_vmem = pl.BlockSpec(memory_space=pltpu.VMEM)
    slab = pltpu.VMEM((HEADS_PLANE, PLANES, CUBE, HDIM), BF16)
    small = pltpu.VMEM((PLANES, 16, HDIM), BF16)
    return pl.pallas_call(
        bring_kernel,
        name="bring",
        out_shape=(keys_shape, keys_shape, query_shape, query_shape, pooled_shape),
        in_specs=[in_vmem] * 6,
        out_specs=[anywhere] * 5,
        scratch_shapes=[
            pltpu.VMEM((4, PLANES, HEADS_PLANE, CUBE, HDIM), BF16),
            slab, slab, slab, slab, small, small,
            pltpu.SemaphoreType.DMA((STAGES + 1,)),
            pltpu.SemaphoreType.DMA((STAGES + 1,)),
            pltpu.SemaphoreType.DMA((5,)),
            pltpu.SemaphoreType.DMA((2, CHIPS)),
            pltpu.SemaphoreType.DMA((3,)),
            pltpu.SemaphoreType.DMA((2,)),
            pltpu.SemaphoreType.DMA((2,)),
        ],
        compiler_params=pltpu.CompilerParams(
            collective_id=0, has_side_effects=True, vmem_limit_bytes=BRING_VMEM
        ),
    )(keys_in, values, queries, grad_out, fine_gate.T, coarse_gate.T)


def nt(a, b):
    return lax.dot_general(a, b, (((1,), (1,)), ((), ())), preferred_element_type=F32)


def tn(a, b):
    return lax.dot_general(a, b, (((0,), (0,)), ((), ())), preferred_element_type=F32)


def nn(a, b):
    return jnp.dot(a, b, preferred_element_type=F32)


def attend_kernel(
    toc, sel, q, fg, pg, k, v,
    dq, dk, dv,
    ak, av, wide_0, wide_1, prob_0, prob_1, dsc_0, dsc_1,
    pk, pv, pq, cdq, part_k, part_v, cot, soc, held,
):
    _, chip, core = where_am_i()
    works, head, copy = role_of(chip)
    units = jnp.where(works, UNITS, 0)
    factor = 1.0 / math.sqrt(HDIM)
    log2e = math.log2(math.e)

    def eighths(source, group):
        block = source[pl.ds(pl.multiple_of(group * 8, 8), 8)].astype(F32)
        return jnp.sum(block.reshape(8, 8, 8, HDIM), axis=1).reshape(64, HDIM)

    def prepare(group, _):
        rows = pl.ds(pl.multiple_of(group * 64, 64), 64)
        part_k[rows, :] = eighths(k, group)
        part_v[rows, :] = eighths(v, group)
        for total_of in (ak, av):
            total_of[pl.ds(pl.multiple_of(group * 8, 8), 8)] = jnp.zeros((8, CUBE, HDIM), F32)
        for i in range(8):
            cube = group * 8 + i
            tile = toc[cube]
            cot[tile] = cube
            soc[cube] = (
                lax.shift_left(lax.shift_right_logical(tile, 3) & 1, 7)
                + lax.shift_left(lax.shift_right_logical(tile, 4) & 1, 6)
                + lax.shift_left(tile & 7, 3)
                + lax.shift_right_logical(tile, 5)
            )
        return 0

    lax.fori_loop(0, SLOTS // 8, prepare, 0)

    def pool(part, into):
        count = into.shape[0]
        total = part[pl.ds(0, count, stride=8), :]
        for row in range(1, 8):
            total += part[pl.ds(row, count, stride=8), :]
        into[...] = total * (1.0 / CUBE)

    pool(part_k, pk)
    pool(part_v, pv)

    def prepare_queries(group, _):
        part_k[pl.ds(pl.multiple_of(group * 64, 64), 64), :] = eighths(q, group)
        return 0

    lax.fori_loop(0, QGROUPS, prepare_queries, 0)
    pool(part_k, pq)
    row_at = lax.broadcasted_iota(jnp.int32, (UNITS, 16, HDIM), 1)
    pooled_g = jnp.sum(
        jnp.where(row_at == head, pg[...].astype(F32), 0.0), axis=1
    ).astype(BF16)
    pooled_q = pq[...].astype(BF16)
    pooled_k = pk[...].astype(BF16)
    pooled_v = pv[...].astype(BF16)
    scores = nt(pooled_q, pooled_k) * factor
    weights = jnp.exp(scores - jnp.max(scores, axis=1, keepdims=True))
    probs = weights / jnp.sum(weights, axis=1, keepdims=True)
    dprobs = nt(pooled_g, pooled_v)
    inner = jnp.sum(probs * dprobs, axis=1, keepdims=True)
    dscores = (probs * (dprobs - inner)).astype(BF16)
    cdq[...] = nn(dscores, pooled_k) * (factor / CUBE)
    pk[...] = tn(dscores, pooled_q) * (factor / CUBE)
    pv[...] = tn(probs.astype(BF16), pooled_g) * (1.0 / CUBE)
    wide_0[...] = jnp.zeros_like(wide_0)
    wide_1[...] = jnp.zeros_like(wide_1)

    def listed(n):
        origin = asked_by(head, copy, n // PLANES)
        tile = (n % PLANES * 4 + origin // 8 * 2 + core) * 8 + origin % 8
        cube = cot[tile]
        return [soc[sel[r, cube]] for r in range(TOPK)]

    def beside(ref, lists, c):
        return jnp.concatenate(
            [jnp.concatenate([ref[s] for s in slots[c * 4:c * 4 + 4]], axis=0) for slots in lists],
            axis=1,
        )

    sides = ((prob_0, dsc_0, wide_0), (prob_1, dsc_1, wide_1))

    def advance(old, m_old, new, m_new):
        prob_new, dsc_new, wide_new = sides[new]
        lists_new = [listed(2 * m_new + i) for i in range(2)]
        for i, slots in enumerate(lists_new):
            for r, slot in enumerate(slots):
                held[new, i * TOPK + r] = slot
            rows, lanes = slice(i * CUBE, (i + 1) * CUBE), slice(i * HDIM, (i + 1) * HDIM)
            wide_new[0, rows, lanes] = q[2 * m_new + i]
            wide_new[1, rows, lanes] = fg[2 * m_new + i]
        score, dprob = [], []
        if old is not None:
            prob_old, dsc_old, wide_old = sides[old]
            lists_old = [[held[old, i * TOPK + r] for r in range(TOPK)] for i in range(2)]
            dquery = jnp.zeros((2 * CUBE, 2 * HDIM), F32)
        for c in range(4):
            score.append(nt(beside(k, lists_new, c), wide_new[0]))
            dprob.append(nt(beside(v, lists_new, c), wide_new[1]))
            if old is None:
                continue
            chunk = slice(c * 4 * CUBE, (c + 1) * 4 * CUBE)
            dscore = dsc_old[chunk]
            dquery += tn(dscore, beside(k, lists_old, c))
            key_terms = nn(dscore, wide_old[0])
            value_terms = nn(prob_old[chunk], wide_old[1])
            for i, slots in enumerate(lists_old):
                lanes = slice(i * HDIM, (i + 1) * HDIM)
                for total_of, terms in ((ak, key_terms), (av, value_terms)):
                    before = [total_of[s] for s in slots[c * 4:c * 4 + 4]]
                    for at, s in enumerate(slots[c * 4:c * 4 + 4]):
                        total_of[s] = before[at] + terms[at * CUBE:(at + 1) * CUBE, lanes]
        top = jnp.max(functools.reduce(jnp.maximum, score), axis=0, keepdims=True)
        weight = [jnp.exp2((s - top) * (factor * log2e)) for s in score]
        total = jnp.sum(functools.reduce(jnp.add, weight), axis=0, keepdims=True)
        inverse = 1.0 / total
        mixed = functools.reduce(jnp.add, [w * d for w, d in zip(weight, dprob)])
        center = jnp.sum(mixed, axis=0, keepdims=True) * inverse
        for c in range(4):
            chunk = slice(c * 4 * CUBE, (c + 1) * 4 * CUBE)
            prob = weight[c] * inverse
            prob_new[chunk] = prob.astype(BF16)
            dsc_new[chunk] = (prob * (dprob[c] - center)).astype(BF16)
        if old is not None:
            for i in range(2):
                n = 2 * m_old + i
                mine = dquery[i * CUBE:(i + 1) * CUBE, i * HDIM:(i + 1) * HDIM]
                dq[n] = (mine * factor + cdq[pl.ds(n, 1), :]).astype(BF16)

    advance(None, 0, 0, 0)

    def two_pairs(m, _):
        advance(0, 2 * m, 1, 2 * m + 1)
        advance(1, 2 * m + 1, 0, jnp.minimum(2 * m + 2, UNITS // 2 - 1))
        return 0

    lax.fori_loop(0, units // 4, two_pairs, 0)

    def finish(group, _):
        for i in range(4):
            slot = group * 4 + i
            dk[slot] = (ak[slot] * factor + pk[pl.ds(slot, 1), :]).astype(BF16)
            dv[slot] = (av[slot] + pv[pl.ds(slot, 1), :]).astype(BF16)
        return 0

    lax.fori_loop(0, SLOTS // 4, finish, 0)


def attend(tile_of_cube, select, qh, fh, ph, kh, vh):
    smem = pl.BlockSpec(memory_space=pltpu.SMEM)
    vmem = pl.BlockSpec(memory_space=pltpu.VMEM)
    query_shape = jax.ShapeDtypeStruct((UNITS, CUBE, HDIM), BF16)
    keys_shape = jax.ShapeDtypeStruct((SLOTS, CUBE, HDIM), BF16)
    return pl.pallas_call(
        attend_kernel,
        name="attend",
        out_shape=(query_shape, keys_shape, keys_shape),
        in_specs=[smem] * 2 + [vmem] * 5,
        out_specs=[vmem] * 3,
        scratch_shapes=[
            pltpu.VMEM((SLOTS, CUBE, HDIM), F32),
            pltpu.VMEM((SLOTS, CUBE, HDIM), F32),
            pltpu.VMEM((2, 2 * CUBE, 2 * HDIM), BF16),
            pltpu.VMEM((2, 2 * CUBE, 2 * HDIM), BF16),
            pltpu.VMEM((TOPK * CUBE, 2 * CUBE), BF16),
            pltpu.VMEM((TOPK * CUBE, 2 * CUBE), BF16),
            pltpu.VMEM((TOPK * CUBE, 2 * CUBE), BF16),
            pltpu.VMEM((TOPK * CUBE, 2 * CUBE), BF16),
            pltpu.VMEM((SLOTS, HDIM), F32),
            pltpu.VMEM((SLOTS, HDIM), F32),
            pltpu.VMEM((UNITS, HDIM), F32),
            pltpu.VMEM((UNITS, HDIM), F32),
            pltpu.VMEM((SLOTS * 8, HDIM), F32),
            pltpu.VMEM((SLOTS * 8, HDIM), F32),
            pltpu.SMEM((SLOTS,), jnp.int32),
            pltpu.SMEM((SLOTS,), jnp.int32),
            pltpu.SMEM((2, 2 * TOPK), jnp.int32),
        ],
        compiler_params=pltpu.CompilerParams(vmem_limit_bytes=ATTEND_VMEM),
    )(
        tile_of_cube, select.T,
        qh.reshape(UNITS, CUBE, HDIM), fh.reshape(UNITS, CUBE, HDIM),
        ph.reshape(UNITS, 16, HDIM), kh.reshape(SLOTS, CUBE, HDIM), vh.reshape(SLOTS, CUBE, HDIM),
    )


def home_kernel(
    dq, dk, dv,
    oq, ok, ov,
    own_k, own_v, sib_k, sib_v, land_q, land_k, land_v, sum_k, sum_v, sum_q,
    ssend, srecv, psend, precv, zsend, zrecv,
):
    plane, chip, core = where_am_i()
    works, head, replica = role_of(chip)
    greet(plane, chip, core)
    sibling = device_of(plane, chip, 1 - core)
    sources, owns, sibs = (dk, dv), (own_k, own_v), (sib_k, sib_v)
    lands, sums, outs = (land_k, land_v), (sum_k, sum_v), (ok, ov)
    mine = columns(plane)

    @pl.when(works)
    def _():
        for number in range(2):
            def give(d, _, number=number):
                target = (chip + d) % CHIPS
                remote(
                    sources[number].at[(1 - core) * CHIPS + target], sibs[number].at[target],
                    ssend.at[number], srecv.at[number, target], sibling,
                ).start()
                return 0

            lax.fori_loop(0, CHIPS, give, 0)

        def send_query(m, _):
            i = (m + chip) % QGROUPS
            target = asked_by(head, replica, i)

            @pl.when(target != chip)
            def _():
                remote(
                    dq.at[i], land_q.at[head], psend.at[2], precv.at[4],
                    device_of(plane, target, core),
                ).start()

            @pl.when(target == chip)
            def _():
                pltpu.make_async_copy(dq.at[i], land_q.at[head], precv.at[4]).start()

            return 0

        lax.fori_loop(0, QGROUPS, send_query, 0)

    def settle(number, half):
        rows = rows_of(half)
        source, own, sib, land = sources[number], owns[number], sibs[number], lands[number]

        def step(d, _):
            target = (chip + d) % CHIPS
            if half == 0:
                take_bytes(sib.at[target], srecv.at[number, target])
            own[target, :, rows] = (
                source[core * CHIPS + target, :, rows].astype(F32)
                + sib[target, :, rows].astype(F32)
            ).astype(BF16)
            arrived = precv.at[number * 2 + half]

            @pl.when(target != chip)
            def _():
                remote(
                    own.at[target, :, rows], land.at[replica, head, :, rows], psend.at[number],
                    arrived, device_of(plane, target, core),
                ).start()

            @pl.when(target == chip)
            def _():
                pltpu.make_async_copy(
                    own.at[target, :, rows], land.at[replica, head, :, rows], arrived
                ).start()

            return 0

        @pl.when(works)
        def _():
            lax.fori_loop(0, CHIPS, step, 0)

    def send_home(number, block, out, target):
        @pl.when(target != plane)
        def _():
            remote(
                block, out, zsend.at[number], zrecv.at[number], device_of(target, chip, core)
            ).start()

        @pl.when(target == plane)
        def _():
            pltpu.make_async_copy(block, out, zrecv.at[number]).start()

    def queries_home():
        take_bytes(land_q, precv.at[4])

        def step(d, _):
            target = (plane + d) % PLANES
            for j in range(HEADS_PLANE):
                sum_q[target, :, j * HDIM:(j + 1) * HDIM] = land_q[j, target]
            send_home(2, sum_q.at[target], oq.at[:, mine], target)
            return 0

        lax.fori_loop(0, PLANES, step, 0)

    def keys_home(number, half):
        rows = rows_of(half)
        land, total, out = lands[number], sums[number], outs[number]
        take_bytes(land.at[:, :, :, rows], precv.at[number * 2 + half])

        def step(d, _):
            target = (plane + d) % PLANES
            for j in range(HEADS_PLANE):
                summed = land[0, j, target, rows].astype(F32)
                for r in range(1, COPIES):
                    summed += land[r, j, target, rows].astype(F32)
                total[target, rows, j * HDIM:(j + 1) * HDIM] = summed.astype(BF16)
            send_home(number, total.at[target, rows], out.at[rows, mine], target)
            return 0

        lax.fori_loop(0, PLANES, step, 0)

    settle(0, 0)
    settle(0, 1)
    queries_home()
    keys_home(0, 0)
    settle(1, 0)
    keys_home(0, 1)
    settle(1, 1)
    keys_home(1, 0)
    keys_home(1, 1)

    for number, out in enumerate((ok, ov, oq)):
        take_bytes(out, zrecv.at[number])
        take_bytes(sum_q.at[pl.ds(0, PLANES - 1)], zsend.at[number])

    @pl.when(works)
    def _():
        for number in range(2):
            take_bytes(sibs[number], ssend.at[number])
            take_bytes(owns[number].at[pl.ds(0, CHIPS - 1)], psend.at[number])

        take_bytes(dq.at[pl.ds(0, QGROUPS - 1)], psend.at[2])


def home(dq, dk, dv, rows, width):
    anywhere = pl.BlockSpec(memory_space=pl.ANY)
    in_vmem = pl.BlockSpec(memory_space=pltpu.VMEM)
    out_shape = jax.ShapeDtypeStruct((rows, width), BF16)
    half = pltpu.VMEM((CHIPS, PLANES, CUBE, HDIM), BF16)
    slab = pltpu.VMEM((PLANES, CUBE, WIDTH), BF16)
    by_head = pltpu.VMEM((HEADS_PLANE, PLANES, CUBE, HDIM), BF16)
    copies = pltpu.VMEM((COPIES, HEADS_PLANE, PLANES, CUBE, HDIM), BF16)
    return pl.pallas_call(
        home_kernel,
        name="home",
        out_shape=(out_shape,) * 3,
        in_specs=[anywhere, in_vmem, in_vmem],
        out_specs=[anywhere] * 3,
        scratch_shapes=[
            half, half, half, half, by_head, copies, copies, slab, slab, slab,
            pltpu.SemaphoreType.DMA((2,)),
            pltpu.SemaphoreType.DMA((2, CHIPS)),
            pltpu.SemaphoreType.DMA((3,)),
            pltpu.SemaphoreType.DMA((5,)),
            pltpu.SemaphoreType.DMA((3,)),
            pltpu.SemaphoreType.DMA((3,)),
        ],
        compiler_params=pltpu.CompilerParams(
            collective_id=1, has_side_effects=True, vmem_limit_bytes=HOME_VMEM
        ),
    )(
        dq.reshape(QGROUPS, PLANES, CUBE, HDIM),
        dk.reshape(2 * CHIPS, PLANES, CUBE, HDIM),
        dv.reshape(2 * CHIPS, PLANES, CUBE, HDIM),
    )


def on_device(queries, keys_in, values, grad_out, fine_gate, coarse_gate, tile_of_cube, select):
    kh, vh, qh, fh, ph = bring(keys_in, values, queries, grad_out, fine_gate, coarse_gate)
    dq, dk, dv = attend(tile_of_cube, select, qh, fh, ph, kh, vh)
    return home(dq, dk, dv, *queries.shape)


def solution(mesh):
    split = P(("tok", "head"), None)
    return jax.shard_map(
        on_device,
        mesh=mesh,
        in_specs=(split,) * 6 + (P(), P()),
        out_specs=(split,) * 3,
        check_vma=False,
    )
```

```python
import functools
import math

import jax
import jax.numpy as jnp
from jax import lax
from jax.experimental import pallas as pl
from jax.experimental.pallas import tpu as pltpu
from jax.sharding import PartitionSpec as P

MESH = pl.DeviceIdType.MESH
BF16 = jnp.bfloat16
F32 = jnp.float32

CUBE = 64
HDIM = 128
PLANES = 8
CHIPS = 16
HEADS_PLANE = 5
COPIES = 2
WORKERS = HEADS_PLANE * COPIES
WIDTH = HEADS_PLANE * HDIM
QGROUPS = 8
TOPK = 16
SPAN = 16
SLOTS = 2 * CHIPS * PLANES
UNITS = QGROUPS * PLANES
HALF = CUBE // 2
STAGES = 8
ATTEND_VMEM = 30 * 2**20
HOME_VMEM = 20 * 2**20
BRING_VMEM = 16 * 2**20


def where_am_i():
    tok = lax.axis_index("tok")
    head = lax.axis_index("head")
    plane = tok // 4
    chip = (tok // 2) % 2 * 8 + head
    core = tok % 2
    return plane, chip, core


def role_of(chip):
    x, y = chip % 4, chip // 4
    plain = y % 2 == x % 2
    return plain | ((y % 2 == 1) & (x == y - 1)), jnp.where(plain, x, HEADS_PLANE - 1), y // 2


def chip_of(head, copy):
    return jnp.where(head < HEADS_PLANE - 1, head % 2 * 4 + 8 * copy + head, 10 * copy + 4)


def odd_rows(head):
    return jnp.where(head < HEADS_PLANE - 1, head % 2, 1)


def asks(head, chip):
    x, y = chip % 4, chip // 4
    own = y % 2 == odd_rows(head)
    row = jnp.where(own, y, (y + 5 - 2 * ((x + head) % 2)) % 4)
    return row // 2, jnp.where(own, x, 4 + x)


def asked_by(head, copy, group):
    x, row = group % 4, odd_rows(head) + 2 * copy
    y = jnp.where(group < 4, row, (row + 3 + 2 * ((x + head) % 2)) % 4)
    return y * 4 + x


def device_of(plane, chip, core):
    return {"tok": plane * 4 + chip // 8 * 2 + core, "head": chip % 8}


def remote(src, dst, send, recv, device):
    return pltpu.make_async_remote_copy(
        src_ref=src, dst_ref=dst, send_sem=send, recv_sem=recv, device_id=device, device_id_type=MESH
    )


def take_bytes(ref, sem):
    pltpu.make_async_copy(ref, ref, sem).wait()


def greet(plane, chip, core):
    barrier = pltpu.get_barrier_semaphore()

    def along_z(d, _):
        pl.semaphore_signal(
            barrier, inc=1, device_id=device_of((plane + d) % PLANES, chip, core), device_id_type=MESH
        )
        return 0

    def in_plane(d, _):
        pl.semaphore_signal(
            barrier, inc=1, device_id=device_of(plane, (chip + d) % CHIPS, core), device_id_type=MESH
        )
        return 0

    lax.fori_loop(1, PLANES, along_z, 0)
    lax.fori_loop(1, CHIPS, in_plane, 0)
    pl.semaphore_signal(
        barrier, inc=1, device_id=device_of(plane, chip, 1 - core), device_id_type=MESH
    )
    pl.semaphore_wait(barrier, PLANES - 1 + CHIPS - 1 + 1)


def columns(group, width=WIDTH):
    return pl.ds(pl.multiple_of(group * width, 128), width)


def rows_of(half):
    return pl.ds(half * HALF, HALF)


def bring_kernel(
    k_in, v_in, q_in, g_in, fgate, cgate,
    kh, vh, qh, fh, ph,
    packed, kz, vz, qz, fz, pz, pg,
    zsend, zrecv, psend, krecv, qrecv, fsend, frecv,
):
    plane, chip, core = where_am_i()
    greet(plane, chip, core)

    def start_along_z(stage, source, landing):
        def step(d, _):
            target = (plane + d) % PLANES
            remote(
                source(target), landing(plane), zsend.at[stage], zrecv.at[stage],
                device_of(target, chip, core),
            ).start()
            return 0

        lax.fori_loop(1, PLANES, step, 0)
        pltpu.make_async_copy(source(plane), landing(plane), zrecv.at[stage]).start()

    slabs = (kz, vz, qz, fz)
    outs = (kh, vh, qh, fh)

    def start_stage(stage):
        number, rows = stage // 2, rows_of(stage % 2)
        start_along_z(
            stage,
            lambda t: packed.at[number, t, :, rows],
            lambda t: slabs[number].at[:, t, rows],
        )

    def pack(number, source):
        def step(group, _):
            for j in range(HEADS_PLANE):
                packed[number, group, j] = source[:, columns(group * HEADS_PLANE + j, HDIM)]
            return 0

        lax.fori_loop(0, PLANES, step, 0)

    pack(0, k_in)
    start_stage(0)
    pack(1, v_in)
    pack(2, q_in)

    def gates(group, _):
        row = lax.broadcasted_iota(jnp.int32, (fgate.shape[0], WIDTH), 0)
        col = lax.broadcasted_iota(jnp.int32, (fgate.shape[0], WIDTH), 1)
        spread = jnp.where(
            row == group * HEADS_PLANE + lax.shift_right_logical(col, 7), 1.0, 0.0
        ).astype(BF16)
        grad = g_in[:, columns(group)].astype(F32)
        fine = (tn(fgate[...], spread) * grad).astype(BF16)
        coarse = tn(cgate[...], spread)
        pooled = jnp.sum(coarse * grad, axis=0, keepdims=True)
        rows = []
        for j in range(HEADS_PLANE):
            packed[3, group, j] = fine[:, j * HDIM:(j + 1) * HDIM]
            rows.append(pooled[:, j * HDIM:(j + 1) * HDIM])
        rows.append(jnp.zeros((16 - HEADS_PLANE, HDIM), F32))
        pg[group] = jnp.concatenate(rows, axis=0).astype(BF16)
        return 0

    lax.fori_loop(0, PLANES, gates, 0)
    start_stage(1)
    works, _, _ = role_of(chip)

    def share_keys(number, rows):
        landed, out = slabs[number], outs[number]

        def step(m, _):
            worker = (m + chip) % WORKERS
            head = worker % HEADS_PLANE
            target = chip_of(head, worker // HEADS_PLANE)
            here, there = landed.at[head, :, rows], out.at[core * CHIPS + chip, :, rows]

            @pl.when(target != chip)
            def _():
                remote(
                    here, there, psend.at[number], krecv.at[number, chip],
                    device_of(plane, target, core),
                ).start()

            @pl.when(target == chip)
            def _():
                pltpu.make_async_copy(here, there, krecv.at[number, chip]).start()

            return 0

        lax.fori_loop(0, WORKERS, step, 0)

    def share_queries(number, pick, place):
        def step(m, _):
            j = (m + chip) % HEADS_PLANE
            copy, group = asks(j, chip)
            target = chip_of(j, copy)

            @pl.when(target != chip)
            def _():
                remote(
                    pick(j), place(group), psend.at[number],
                    qrecv.at[number - 2], device_of(plane, target, core),
                ).start()

            @pl.when(target == chip)
            def _():
                pltpu.make_async_copy(
                    pick(j), place(group), qrecv.at[number - 2]
                ).start()

            return 0

        lax.fori_loop(0, HEADS_PLANE, step, 0)

    for stage in range(STAGES):
        number, rows = stage // 2, rows_of(stage % 2)
        take_bytes(slabs[number].at[:, :, rows], zrecv.at[stage])
        if stage + 2 < STAGES:
            start_stage(stage + 2)
        if stage + 2 == STAGES:
            start_along_z(STAGES, lambda t: pg.at[t], lambda t: pz.at[t])
        if number < 2:
            share_keys(number, rows)
        else:
            share_queries(
                number,
                lambda j, number=number, rows=rows: slabs[number].at[j, :, rows],
                lambda i, number=number, rows=rows: outs[number].at[i, :, rows],
            )
    take_bytes(pz, zrecv.at[STAGES])
    share_queries(4, lambda j: pz, lambda i: ph.at[i])

    sibling = device_of(plane, chip, 1 - core)

    @pl.when(works)
    def _():
        for number, out in ((0, kh), (1, vh)):
            def forward(d, _, number=number, out=out):
                origin = (chip + CHIPS - d) % CHIPS
                block = out.at[core * CHIPS + origin]
                take_bytes(block, krecv.at[number, origin])
                remote(block, block, fsend.at[number], frecv.at[number], sibling).start()
                return 0

            lax.fori_loop(0, CHIPS, forward, 0)

        for number, out in enumerate((qh, fh, ph)):
            take_bytes(out, qrecv.at[number])

        for number, out in ((0, kh), (1, vh)):
            theirs = out.at[pl.ds((1 - core) * CHIPS, CHIPS)]
            take_bytes(theirs, frecv.at[number])
            take_bytes(theirs, fsend.at[number])

    for stage in range(STAGES):
        landed = slabs[stage // 2].at[:, pl.ds(0, PLANES - 1), rows_of(stage % 2)]
        take_bytes(landed, zsend.at[stage])
    take_bytes(pz.at[pl.ds(0, PLANES - 1)], zsend.at[STAGES])

    def drain(keys, queries):
        for number, out in ((0, kh), (1, vh)):
            take_bytes(out.at[pl.ds(0, keys)], psend.at[number])
        for number, out in ((2, qh), (3, fh), (4, ph)):
            take_bytes(out.at[pl.ds(0, queries)], psend.at[number])

    @pl.when(works)
    def _():
        drain(WORKERS - 1, HEADS_PLANE - 1)

    @pl.when(jnp.logical_not(works))
    def _():
        drain(WORKERS, HEADS_PLANE)


def bring(keys_in, values, queries, grad_out, fine_gate, coarse_gate):
    keys_shape = jax.ShapeDtypeStruct((2 * CHIPS, PLANES, CUBE, HDIM), BF16)
    query_shape = jax.ShapeDtypeStruct((QGROUPS, PLANES, CUBE, HDIM), BF16)
    pooled_shape = jax.ShapeDtypeStruct((QGROUPS, PLANES, 16, HDIM), BF16)
    anywhere = pl.BlockSpec(memory_space=pl.ANY)
    in_vmem = pl.BlockSpec(memory_space=pltpu.VMEM)
    slab = pltpu.VMEM((HEADS_PLANE, PLANES, CUBE, HDIM), BF16)
    small = pltpu.VMEM((PLANES, 16, HDIM), BF16)
    return pl.pallas_call(
        bring_kernel,
        name="bring",
        out_shape=(keys_shape, keys_shape, query_shape, query_shape, pooled_shape),
        in_specs=[in_vmem] * 6,
        out_specs=[anywhere] * 5,
        scratch_shapes=[
            pltpu.VMEM((4, PLANES, HEADS_PLANE, CUBE, HDIM), BF16),
            slab, slab, slab, slab, small, small,
            pltpu.SemaphoreType.DMA((STAGES + 1,)),
            pltpu.SemaphoreType.DMA((STAGES + 1,)),
            pltpu.SemaphoreType.DMA((5,)),
            pltpu.SemaphoreType.DMA((2, CHIPS)),
            pltpu.SemaphoreType.DMA((3,)),
            pltpu.SemaphoreType.DMA((2,)),
            pltpu.SemaphoreType.DMA((2,)),
        ],
        compiler_params=pltpu.CompilerParams(
            collective_id=0, has_side_effects=True, vmem_limit_bytes=BRING_VMEM
        ),
    )(keys_in, values, queries, grad_out, fine_gate.T, coarse_gate.T)


def nt(a, b):
    return lax.dot_general(a, b, (((1,), (1,)), ((), ())), preferred_element_type=F32)


def tn(a, b):
    return lax.dot_general(a, b, (((0,), (0,)), ((), ())), preferred_element_type=F32)


def nn(a, b):
    return jnp.dot(a, b, preferred_element_type=F32)


def attend_kernel(
    toc, sel, q, fg, pg, k, v,
    dq, dk, dv,
    ak, av, wide_0, wide_1, prob_0, prob_1, dsc_0, dsc_1,
    pk, pv, pq, cdq, part_k, part_v, cot, soc, held,
):
    _, chip, core = where_am_i()
    works, head, copy = role_of(chip)
    units = jnp.where(works, UNITS, 0)
    factor = 1.0 / math.sqrt(HDIM)
    log2e = math.log2(math.e)

    def eighths(source, group):
        block = source[pl.ds(pl.multiple_of(group * 8, 8), 8)].astype(F32)
        return jnp.sum(block.reshape(8, 8, 8, HDIM), axis=1).reshape(64, HDIM)

    def prepare(group, _):
        rows = pl.ds(pl.multiple_of(group * 64, 64), 64)
        part_k[rows, :] = eighths(k, group)
        part_v[rows, :] = eighths(v, group)
        for total_of in (ak, av):
            total_of[pl.ds(pl.multiple_of(group * 8, 8), 8)] = jnp.zeros((8, CUBE, HDIM), F32)
        for i in range(8):
            cube = group * 8 + i
            tile = toc[cube]
            cot[tile] = cube
            soc[cube] = (
                lax.shift_left(lax.shift_right_logical(tile, 3) & 1, 7)
                + lax.shift_left(lax.shift_right_logical(tile, 4) & 1, 6)
                + lax.shift_left(tile & 7, 3)
                + lax.shift_right_logical(tile, 5)
            )
        return 0

    lax.fori_loop(0, SLOTS // 8, prepare, 0)

    def pool(part, into):
        count = into.shape[0]
        total = part[pl.ds(0, count, stride=8), :]
        for row in range(1, 8):
            total += part[pl.ds(row, count, stride=8), :]
        into[...] = total * (1.0 / CUBE)

    pool(part_k, pk)
    pool(part_v, pv)

    def prepare_queries(group, _):
        part_k[pl.ds(pl.multiple_of(group * 64, 64), 64), :] = eighths(q, group)
        return 0

    lax.fori_loop(0, QGROUPS, prepare_queries, 0)
    pool(part_k, pq)
    row_at = lax.broadcasted_iota(jnp.int32, (UNITS, 16, HDIM), 1)
    pooled_g = jnp.sum(
        jnp.where(row_at == head, pg[...].astype(F32), 0.0), axis=1
    ).astype(BF16)
    pooled_q = pq[...].astype(BF16)
    pooled_k = pk[...].astype(BF16)
    pooled_v = pv[...].astype(BF16)
    scores = nt(pooled_q, pooled_k) * factor
    weights = jnp.exp(scores - jnp.max(scores, axis=1, keepdims=True))
    probs = weights / jnp.sum(weights, axis=1, keepdims=True)
    dprobs = nt(pooled_g, pooled_v)
    inner = jnp.sum(probs * dprobs, axis=1, keepdims=True)
    dscores = (probs * (dprobs - inner)).astype(BF16)
    cdq[...] = nn(dscores, pooled_k) * (factor / CUBE)
    pk[...] = tn(dscores, pooled_q) * (factor / CUBE)
    pv[...] = tn(probs.astype(BF16), pooled_g) * (1.0 / CUBE)
    wide_0[...] = jnp.zeros_like(wide_0)
    wide_1[...] = jnp.zeros_like(wide_1)

    def listed(n):
        origin = asked_by(head, copy, n // PLANES)
        tile = (n % PLANES * 4 + origin // 8 * 2 + core) * 8 + origin % 8
        cube = cot[tile]
        return [soc[sel[r, cube]] for r in range(TOPK)]

    def beside(ref, lists, c):
        return jnp.concatenate(
            [
                jnp.concatenate([ref[s] for s in slots[c * SPAN:(c + 1) * SPAN]], axis=0)
                for slots in lists
            ],
            axis=1,
        )

    sides = ((prob_0, dsc_0, wide_0), (prob_1, dsc_1, wide_1))

    def advance(old, m_old, new, m_new):
        prob_new, dsc_new, wide_new = sides[new]
        lists_new = [listed(2 * m_new + i) for i in range(2)]
        for i, slots in enumerate(lists_new):
            for r, slot in enumerate(slots):
                held[new, i * TOPK + r] = slot
            rows, lanes = slice(i * CUBE, (i + 1) * CUBE), slice(i * HDIM, (i + 1) * HDIM)
            wide_new[0, rows, lanes] = q[2 * m_new + i]
            wide_new[1, rows, lanes] = fg[2 * m_new + i]
        score, dprob = [], []
        if old is not None:
            prob_old, dsc_old, wide_old = sides[old]
            lists_old = [[held[old, i * TOPK + r] for r in range(TOPK)] for i in range(2)]
            dquery = jnp.zeros((2 * CUBE, 2 * HDIM), F32)
        for c in range(TOPK // SPAN):
            score.append(nt(beside(k, lists_new, c), wide_new[0]))
            dprob.append(nt(beside(v, lists_new, c), wide_new[1]))
            if old is None:
                continue
            chunk = slice(c * SPAN * CUBE, (c + 1) * SPAN * CUBE)
            dscore = dsc_old[chunk]
            dquery += tn(dscore, beside(k, lists_old, c))
            key_terms = nn(dscore, wide_old[0])
            value_terms = nn(prob_old[chunk], wide_old[1])
            for i, slots in enumerate(lists_old):
                lanes = slice(i * HDIM, (i + 1) * HDIM)
                for total_of, terms in ((ak, key_terms), (av, value_terms)):
                    for first in range(0, SPAN, 4):
                        some = slots[c * SPAN + first:c * SPAN + first + 4]
                        before = [total_of[s] for s in some]
                        for at, s in enumerate(some):
                            rows = slice((first + at) * CUBE, (first + at + 1) * CUBE)
                            total_of[s] = before[at] + terms[rows, lanes]
        top = jnp.max(functools.reduce(jnp.maximum, score), axis=0, keepdims=True)
        weight = [jnp.exp2((s - top) * (factor * log2e)) for s in score]
        total = jnp.sum(functools.reduce(jnp.add, weight), axis=0, keepdims=True)
        inverse = 1.0 / total
        mixed = functools.reduce(jnp.add, [w * d for w, d in zip(weight, dprob)])
        center = jnp.sum(mixed, axis=0, keepdims=True) * inverse
        for c in range(TOPK // SPAN):
            chunk = slice(c * SPAN * CUBE, (c + 1) * SPAN * CUBE)
            prob = weight[c] * inverse
            prob_new[chunk] = prob.astype(BF16)
            dsc_new[chunk] = (prob * (dprob[c] - center)).astype(BF16)
        if old is not None:
            for i in range(2):
                n = 2 * m_old + i
                mine = dquery[i * CUBE:(i + 1) * CUBE, i * HDIM:(i + 1) * HDIM]
                dq[n] = (mine * factor + cdq[pl.ds(n, 1), :]).astype(BF16)

    advance(None, 0, 0, 0)

    def two_pairs(m, _):
        advance(0, 2 * m, 1, 2 * m + 1)
        advance(1, 2 * m + 1, 0, jnp.minimum(2 * m + 2, UNITS // 2 - 1))
        return 0

    lax.fori_loop(0, units // 4, two_pairs, 0)

    def finish(group, _):
        for i in range(4):
            slot = group * 4 + i
            dk[slot] = (ak[slot] * factor + pk[pl.ds(slot, 1), :]).astype(BF16)
            dv[slot] = (av[slot] + pv[pl.ds(slot, 1), :]).astype(BF16)
        return 0

    lax.fori_loop(0, SLOTS // 4, finish, 0)


def attend(tile_of_cube, select, qh, fh, ph, kh, vh):
    smem = pl.BlockSpec(memory_space=pltpu.SMEM)
    vmem = pl.BlockSpec(memory_space=pltpu.VMEM)
    query_shape = jax.ShapeDtypeStruct((UNITS, CUBE, HDIM), BF16)
    keys_shape = jax.ShapeDtypeStruct((SLOTS, CUBE, HDIM), BF16)
    return pl.pallas_call(
        attend_kernel,
        name="attend",
        out_shape=(query_shape, keys_shape, keys_shape),
        in_specs=[smem] * 2 + [vmem] * 5,
        out_specs=[vmem] * 3,
        scratch_shapes=[
            pltpu.VMEM((SLOTS, CUBE, HDIM), F32),
            pltpu.VMEM((SLOTS, CUBE, HDIM), F32),
            pltpu.VMEM((2, 2 * CUBE, 2 * HDIM), BF16),
            pltpu.VMEM((2, 2 * CUBE, 2 * HDIM), BF16),
            pltpu.VMEM((TOPK * CUBE, 2 * CUBE), BF16),
            pltpu.VMEM((TOPK * CUBE, 2 * CUBE), BF16),
            pltpu.VMEM((TOPK * CUBE, 2 * CUBE), BF16),
            pltpu.VMEM((TOPK * CUBE, 2 * CUBE), BF16),
            pltpu.VMEM((SLOTS, HDIM), F32),
            pltpu.VMEM((SLOTS, HDIM), F32),
            pltpu.VMEM((UNITS, HDIM), F32),
            pltpu.VMEM((UNITS, HDIM), F32),
            pltpu.VMEM((SLOTS * 8, HDIM), F32),
            pltpu.VMEM((SLOTS * 8, HDIM), F32),
            pltpu.SMEM((SLOTS,), jnp.int32),
            pltpu.SMEM((SLOTS,), jnp.int32),
            pltpu.SMEM((2, 2 * TOPK), jnp.int32),
        ],
        compiler_params=pltpu.CompilerParams(vmem_limit_bytes=ATTEND_VMEM),
    )(
        tile_of_cube, select.T,
        qh.reshape(UNITS, CUBE, HDIM), fh.reshape(UNITS, CUBE, HDIM),
        ph.reshape(UNITS, 16, HDIM), kh.reshape(SLOTS, CUBE, HDIM), vh.reshape(SLOTS, CUBE, HDIM),
    )


def home_kernel(
    dq, dk, dv,
    oq, ok, ov,
    own_k, own_v, sib_k, sib_v, land_q, land_k, land_v, sum_k, sum_v, sum_q,
    ssend, srecv, psend, precv, zsend, zrecv,
):
    plane, chip, core = where_am_i()
    works, head, replica = role_of(chip)
    greet(plane, chip, core)
    sibling = device_of(plane, chip, 1 - core)
    sources, owns, sibs = (dk, dv), (own_k, own_v), (sib_k, sib_v)
    lands, sums, outs = (land_k, land_v), (sum_k, sum_v), (ok, ov)
    mine = columns(plane)

    @pl.when(works)
    def _():
        for number in range(2):
            def give(d, _, number=number):
                target = (chip + d) % CHIPS
                remote(
                    sources[number].at[(1 - core) * CHIPS + target], sibs[number].at[target],
                    ssend.at[number], srecv.at[number, target], sibling,
                ).start()
                return 0

            lax.fori_loop(0, CHIPS, give, 0)

        def send_query(m, _):
            i = (m + chip) % QGROUPS
            target = asked_by(head, replica, i)

            @pl.when(target != chip)
            def _():
                remote(
                    dq.at[i], land_q.at[head], psend.at[2], precv.at[4],
                    device_of(plane, target, core),
                ).start()

            @pl.when(target == chip)
            def _():
                pltpu.make_async_copy(dq.at[i], land_q.at[head], precv.at[4]).start()

            return 0

        lax.fori_loop(0, QGROUPS, send_query, 0)

    def settle(number, half):
        rows = rows_of(half)
        source, own, sib, land = sources[number], owns[number], sibs[number], lands[number]

        def step(d, _):
            target = (chip + d) % CHIPS
            if half == 0:
                take_bytes(sib.at[target], srecv.at[number, target])
            own[target, :, rows] = (
                source[core * CHIPS + target, :, rows].astype(F32)
                + sib[target, :, rows].astype(F32)
            ).astype(BF16)
            arrived = precv.at[number * 2 + half]

            @pl.when(target != chip)
            def _():
                remote(
                    own.at[target, :, rows], land.at[replica, head, :, rows], psend.at[number],
                    arrived, device_of(plane, target, core),
                ).start()

            @pl.when(target == chip)
            def _():
                pltpu.make_async_copy(
                    own.at[target, :, rows], land.at[replica, head, :, rows], arrived
                ).start()

            return 0

        @pl.when(works)
        def _():
            lax.fori_loop(0, CHIPS, step, 0)

    def send_home(number, block, out, target):
        @pl.when(target != plane)
        def _():
            remote(
                block, out, zsend.at[number], zrecv.at[number], device_of(target, chip, core)
            ).start()

        @pl.when(target == plane)
        def _():
            pltpu.make_async_copy(block, out, zrecv.at[number]).start()

    def queries_home():
        take_bytes(land_q, precv.at[4])

        def step(d, _):
            target = (plane + d) % PLANES
            for j in range(HEADS_PLANE):
                sum_q[target, :, j * HDIM:(j + 1) * HDIM] = land_q[j, target]
            send_home(2, sum_q.at[target], oq.at[:, mine], target)
            return 0

        lax.fori_loop(0, PLANES, step, 0)

    def keys_home(number, half):
        rows = rows_of(half)
        land, total, out = lands[number], sums[number], outs[number]
        take_bytes(land.at[:, :, :, rows], precv.at[number * 2 + half])

        def step(d, _):
            target = (plane + d) % PLANES
            for j in range(HEADS_PLANE):
                summed = land[0, j, target, rows].astype(F32)
                for r in range(1, COPIES):
                    summed += land[r, j, target, rows].astype(F32)
                total[target, rows, j * HDIM:(j + 1) * HDIM] = summed.astype(BF16)
            send_home(number, total.at[target, rows], out.at[rows, mine], target)
            return 0

        lax.fori_loop(0, PLANES, step, 0)

    settle(0, 0)
    settle(0, 1)
    queries_home()
    keys_home(0, 0)
    settle(1, 0)
    keys_home(0, 1)
    settle(1, 1)
    keys_home(1, 0)
    keys_home(1, 1)

    for number, out in enumerate((ok, ov, oq)):
        take_bytes(out, zrecv.at[number])
        take_bytes(sum_q.at[pl.ds(0, PLANES - 1)], zsend.at[number])

    @pl.when(works)
    def _():
        for number in range(2):
            take_bytes(sibs[number], ssend.at[number])
            take_bytes(owns[number].at[pl.ds(0, CHIPS - 1)], psend.at[number])

        take_bytes(dq.at[pl.ds(0, QGROUPS - 1)], psend.at[2])


def home(dq, dk, dv, rows, width):
    anywhere = pl.BlockSpec(memory_space=pl.ANY)
    in_vmem = pl.BlockSpec(memory_space=pltpu.VMEM)
    out_shape = jax.ShapeDtypeStruct((rows, width), BF16)
    half = pltpu.VMEM((CHIPS, PLANES, CUBE, HDIM), BF16)
    slab = pltpu.VMEM((PLANES, CUBE, WIDTH), BF16)
    by_head = pltpu.VMEM((HEADS_PLANE, PLANES, CUBE, HDIM), BF16)
    copies = pltpu.VMEM((COPIES, HEADS_PLANE, PLANES, CUBE, HDIM), BF16)
    return pl.pallas_call(
        home_kernel,
        name="home",
        out_shape=(out_shape,) * 3,
        in_specs=[anywhere, in_vmem, in_vmem],
        out_specs=[anywhere] * 3,
        scratch_shapes=[
            half, half, half, half, by_head, copies, copies, slab, slab, slab,
            pltpu.SemaphoreType.DMA((2,)),
            pltpu.SemaphoreType.DMA((2, CHIPS)),
            pltpu.SemaphoreType.DMA((3,)),
            pltpu.SemaphoreType.DMA((5,)),
            pltpu.SemaphoreType.DMA((3,)),
            pltpu.SemaphoreType.DMA((3,)),
        ],
        compiler_params=pltpu.CompilerParams(
            collective_id=1, has_side_effects=True, vmem_limit_bytes=HOME_VMEM
        ),
    )(
        dq.reshape(QGROUPS, PLANES, CUBE, HDIM),
        dk.reshape(2 * CHIPS, PLANES, CUBE, HDIM),
        dv.reshape(2 * CHIPS, PLANES, CUBE, HDIM),
    )


def on_device(queries, keys_in, values, grad_out, fine_gate, coarse_gate, tile_of_cube, select):
    kh, vh, qh, fh, ph = bring(keys_in, values, queries, grad_out, fine_gate, coarse_gate)
    dq, dk, dv = attend(tile_of_cube, select, qh, fh, ph, kh, vh)
    return home(dq, dk, dv, *queries.shape)


def solution(mesh):
    split = P(("tok", "head"), None)
    return jax.shard_map(
        on_device,
        mesh=mesh,
        in_specs=(split,) * 6 + (P(), P()),
        out_specs=(split,) * 3,
        check_vma=False,
    )
```

```python
import functools
import math

import jax
import jax.numpy as jnp
from jax import lax
from jax.experimental import pallas as pl
from jax.experimental.pallas import tpu as pltpu
from jax.sharding import PartitionSpec as P

MESH = pl.DeviceIdType.MESH
BF16 = jnp.bfloat16
F32 = jnp.float32

CUBE = 64
HDIM = 128
PLANES = 8
CHIPS = 16
HEADS_PLANE = 5
COPIES = 2
WORKERS = HEADS_PLANE * COPIES
WIDTH = HEADS_PLANE * HDIM
QGROUPS = 8
TOPK = 16
SLOTS = 2 * CHIPS * PLANES
UNITS = QGROUPS * PLANES
HALF = CUBE // 2
STAGES = 8
ATTEND_VMEM = 30 * 2**20
HOME_VMEM = 20 * 2**20
BRING_VMEM = 16 * 2**20


def where_am_i():
    tok = lax.axis_index("tok")
    head = lax.axis_index("head")
    plane = tok // 4
    chip = (tok // 2) % 2 * 8 + head
    core = tok % 2
    return plane, chip, core


def role_of(chip):
    x, y = chip % 4, chip // 4
    plain = y % 2 == x % 2
    return plain | ((y % 2 == 1) & (x == y - 1)), jnp.where(plain, x, HEADS_PLANE - 1), y // 2


def chip_of(head, copy):
    return jnp.where(head < HEADS_PLANE - 1, head % 2 * 4 + 8 * copy + head, 10 * copy + 4)


def odd_rows(head):
    return jnp.where(head < HEADS_PLANE - 1, head % 2, 1)


def asks(head, chip):
    x, y = chip % 4, chip // 4
    own = y % 2 == odd_rows(head)
    row = jnp.where(own, y, (y + 5 - 2 * ((x + head) % 2)) % 4)
    return row // 2, jnp.where(own, x, 4 + x)


def asked_by(head, copy, group):
    x, row = group % 4, odd_rows(head) + 2 * copy
    y = jnp.where(group < 4, row, (row + 3 + 2 * ((x + head) % 2)) % 4)
    return y * 4 + x


def device_of(plane, chip, core):
    return {"tok": plane * 4 + chip // 8 * 2 + core, "head": chip % 8}


def remote(src, dst, send, recv, device):
    return pltpu.make_async_remote_copy(
        src_ref=src, dst_ref=dst, send_sem=send, recv_sem=recv, device_id=device, device_id_type=MESH
    )


def take_bytes(ref, sem):
    pltpu.make_async_copy(ref, ref, sem).wait()


def greet(plane, chip, core):
    barrier = pltpu.get_barrier_semaphore()

    def along_z(d, _):
        pl.semaphore_signal(
            barrier, inc=1, device_id=device_of((plane + d) % PLANES, chip, core), device_id_type=MESH
        )
        return 0

    def in_plane(d, _):
        pl.semaphore_signal(
            barrier, inc=1, device_id=device_of(plane, (chip + d) % CHIPS, core), device_id_type=MESH
        )
        return 0

    lax.fori_loop(1, PLANES, along_z, 0)
    lax.fori_loop(1, CHIPS, in_plane, 0)
    pl.semaphore_signal(
        barrier, inc=1, device_id=device_of(plane, chip, 1 - core), device_id_type=MESH
    )
    pl.semaphore_wait(barrier, PLANES - 1 + CHIPS - 1 + 1)


def columns(group, width=WIDTH):
    return pl.ds(pl.multiple_of(group * width, 128), width)


def rows_of(half):
    return pl.ds(half * HALF, HALF)


def bring_kernel(
    k_in, v_in, q_in, g_in, fgate, cgate,
    kh, vh, qh, fh, ph,
    packed, kz, vz, qz, fz, pz, pg,
    zsend, zrecv, psend, krecv, qrecv, fsend, frecv,
):
    plane, chip, core = where_am_i()
    greet(plane, chip, core)

    def start_along_z(stage, source, landing):
        def step(d, _):
            target = (plane + d) % PLANES
            remote(
                source(target), landing(plane), zsend.at[stage], zrecv.at[stage],
                device_of(target, chip, core),
            ).start()
            return 0

        lax.fori_loop(1, PLANES, step, 0)
        pltpu.make_async_copy(source(plane), landing(plane), zrecv.at[stage]).start()

    slabs = (kz, vz, qz, fz)
    outs = (kh, vh, qh, fh)

    def start_stage(stage):
        number, rows = stage // 2, rows_of(stage % 2)
        start_along_z(
            stage,
            lambda t: packed.at[number, t, :, rows],
            lambda t: slabs[number].at[:, t, rows],
        )

    def pack(number, source):
        def step(group, _):
            for j in range(HEADS_PLANE):
                packed[number, group, j] = source[:, columns(group * HEADS_PLANE + j, HDIM)]
            return 0

        lax.fori_loop(0, PLANES, step, 0)

    pack(0, k_in)
    start_stage(0)
    pack(1, v_in)
    pack(2, q_in)

    def gates(group, _):
        row = lax.broadcasted_iota(jnp.int32, (fgate.shape[0], WIDTH), 0)
        col = lax.broadcasted_iota(jnp.int32, (fgate.shape[0], WIDTH), 1)
        spread = jnp.where(
            row == group * HEADS_PLANE + lax.shift_right_logical(col, 7), 1.0, 0.0
        ).astype(BF16)
        grad = g_in[:, columns(group)].astype(F32)
        fine = (tn(fgate[...], spread) * grad).astype(BF16)
        coarse = tn(cgate[...], spread)
        pooled = jnp.sum(coarse * grad, axis=0, keepdims=True)
        rows = []
        for j in range(HEADS_PLANE):
            packed[3, group, j] = fine[:, j * HDIM:(j + 1) * HDIM]
            rows.append(pooled[:, j * HDIM:(j + 1) * HDIM])
        rows.append(jnp.zeros((16 - HEADS_PLANE, HDIM), F32))
        pg[group] = jnp.concatenate(rows, axis=0).astype(BF16)
        return 0

    lax.fori_loop(0, PLANES, gates, 0)
    start_stage(1)
    works, _, _ = role_of(chip)

    def share_keys(number, rows):
        landed, out = slabs[number], outs[number]

        def step(m, _):
            worker = (m + chip) % WORKERS
            head = worker % HEADS_PLANE
            target = chip_of(head, worker // HEADS_PLANE)
            here, there = landed.at[head, :, rows], out.at[core * CHIPS + chip, :, rows]

            @pl.when(target != chip)
            def _():
                remote(
                    here, there, psend.at[number], krecv.at[number, chip],
                    device_of(plane, target, core),
                ).start()

            @pl.when(target == chip)
            def _():
                pltpu.make_async_copy(here, there, krecv.at[number, chip]).start()

            return 0

        lax.fori_loop(0, WORKERS, step, 0)

    def share_queries(number, pick, place):
        def step(m, _):
            j = (m + chip) % HEADS_PLANE
            copy, group = asks(j, chip)
            target = chip_of(j, copy)

            @pl.when(target != chip)
            def _():
                remote(
                    pick(j), place(group), psend.at[number],
                    qrecv.at[number - 2], device_of(plane, target, core),
                ).start()

            @pl.when(target == chip)
            def _():
                pltpu.make_async_copy(
                    pick(j), place(group), qrecv.at[number - 2]
                ).start()

            return 0

        lax.fori_loop(0, HEADS_PLANE, step, 0)

    sibling = device_of(plane, chip, 1 - core)

    def forward(number):
        out = outs[number]

        def step(d, _):
            origin = (chip + CHIPS - d) % CHIPS
            block = out.at[core * CHIPS + origin]
            take_bytes(block, krecv.at[number, origin])
            remote(block, block, fsend.at[number], frecv.at[number], sibling).start()
            return 0

        @pl.when(works)
        def _():
            lax.fori_loop(0, CHIPS, step, 0)

    for stage in range(STAGES):
        number, rows = stage // 2, rows_of(stage % 2)
        take_bytes(slabs[number].at[:, :, rows], zrecv.at[stage])
        if stage + 2 == STAGES - 2:
            start_along_z(STAGES, lambda t: pg.at[t], lambda t: pz.at[t])
        if stage + 2 < STAGES:
            start_stage(stage + 2)
        if number < 2:
            share_keys(number, rows)
        else:
            share_queries(
                number,
                lambda j, number=number, rows=rows: slabs[number].at[j, :, rows],
                lambda i, number=number, rows=rows: outs[number].at[i, :, rows],
            )
        if stage == STAGES - 2:
            take_bytes(pz, zrecv.at[STAGES])
            share_queries(4, lambda j: pz, lambda i: ph.at[i])
            forward(0)
    forward(1)

    @pl.when(works)
    def _():
        for number, out in enumerate((qh, fh, ph)):
            take_bytes(out, qrecv.at[number])

        for number, out in ((0, kh), (1, vh)):
            theirs = out.at[pl.ds((1 - core) * CHIPS, CHIPS)]
            take_bytes(theirs, frecv.at[number])
            take_bytes(theirs, fsend.at[number])

    for stage in range(STAGES):
        landed = slabs[stage // 2].at[:, pl.ds(0, PLANES - 1), rows_of(stage % 2)]
        take_bytes(landed, zsend.at[stage])
    take_bytes(pz.at[pl.ds(0, PLANES - 1)], zsend.at[STAGES])

    def drain(keys, queries):
        for number, out in ((0, kh), (1, vh)):
            take_bytes(out.at[pl.ds(0, keys)], psend.at[number])
        for number, out in ((2, qh), (3, fh), (4, ph)):
            take_bytes(out.at[pl.ds(0, queries)], psend.at[number])

    @pl.when(works)
    def _():
        drain(WORKERS - 1, HEADS_PLANE - 1)

    @pl.when(jnp.logical_not(works))
    def _():
        drain(WORKERS, HEADS_PLANE)


def bring(keys_in, values, queries, grad_out, fine_gate, coarse_gate):
    keys_shape = jax.ShapeDtypeStruct((2 * CHIPS, PLANES, CUBE, HDIM), BF16)
    query_shape = jax.ShapeDtypeStruct((QGROUPS, PLANES, CUBE, HDIM), BF16)
    pooled_shape = jax.ShapeDtypeStruct((QGROUPS, PLANES, 16, HDIM), BF16)
    anywhere = pl.BlockSpec(memory_space=pl.ANY)
    in_vmem = pl.BlockSpec(memory_space=pltpu.VMEM)
    slab = pltpu.VMEM((HEADS_PLANE, PLANES, CUBE, HDIM), BF16)
    small = pltpu.VMEM((PLANES, 16, HDIM), BF16)
    return pl.pallas_call(
        bring_kernel,
        name="bring",
        out_shape=(keys_shape, keys_shape, query_shape, query_shape, pooled_shape),
        in_specs=[in_vmem] * 6,
        out_specs=[anywhere] * 5,
        scratch_shapes=[
            pltpu.VMEM((4, PLANES, HEADS_PLANE, CUBE, HDIM), BF16),
            slab, slab, slab, slab, small, small,
            pltpu.SemaphoreType.DMA((STAGES + 1,)),
            pltpu.SemaphoreType.DMA((STAGES + 1,)),
            pltpu.SemaphoreType.DMA((5,)),
            pltpu.SemaphoreType.DMA((2, CHIPS)),
            pltpu.SemaphoreType.DMA((3,)),
            pltpu.SemaphoreType.DMA((2,)),
            pltpu.SemaphoreType.DMA((2,)),
        ],
        compiler_params=pltpu.CompilerParams(
            collective_id=0, has_side_effects=True, vmem_limit_bytes=BRING_VMEM
        ),
    )(keys_in, values, queries, grad_out, fine_gate.T, coarse_gate.T)


def nt(a, b):
    return lax.dot_general(a, b, (((1,), (1,)), ((), ())), preferred_element_type=F32)


def tn(a, b):
    return lax.dot_general(a, b, (((0,), (0,)), ((), ())), preferred_element_type=F32)


def nn(a, b):
    return jnp.dot(a, b, preferred_element_type=F32)


def attend_kernel(
    toc, sel, q, fg, pg, k, v,
    dq, dk, dv,
    ak, av, wide_0, wide_1, prob_0, prob_1, dsc_0, dsc_1,
    pk, pv, pq, cdq, part_k, part_v, cot, soc, held,
):
    _, chip, core = where_am_i()
    works, head, copy = role_of(chip)
    units = jnp.where(works, UNITS, 0)
    factor = 1.0 / math.sqrt(HDIM)

    def eighths(source, group):
        block = source[pl.ds(pl.multiple_of(group * 8, 8), 8)].astype(F32)
        return jnp.sum(block.reshape(8, 8, 8, HDIM), axis=1).reshape(64, HDIM)

    def prepare(group, _):
        rows = pl.ds(pl.multiple_of(group * 64, 64), 64)
        part_k[rows, :] = eighths(k, group)
        part_v[rows, :] = eighths(v, group)
        for total_of in (ak, av):
            total_of[pl.ds(pl.multiple_of(group * 8, 8), 8)] = jnp.zeros((8, CUBE, HDIM), F32)
        for i in range(8):
            cube = group * 8 + i
            tile = toc[cube]
            cot[tile] = cube
            soc[cube] = (
                lax.shift_left(lax.shift_right_logical(tile, 3) & 1, 7)
                + lax.shift_left(lax.shift_right_logical(tile, 4) & 1, 6)
                + lax.shift_left(tile & 7, 3)
                + lax.shift_right_logical(tile, 5)
            )
        return 0

    lax.fori_loop(0, SLOTS // 8, prepare, 0)

    def pool(part, into):
        count = into.shape[0]
        total = part[pl.ds(0, count, stride=8), :]
        for row in range(1, 8):
            total += part[pl.ds(row, count, stride=8), :]
        into[...] = total * (1.0 / CUBE)

    pool(part_k, pk)
    pool(part_v, pv)

    def prepare_queries(group, _):
        part_k[pl.ds(pl.multiple_of(group * 64, 64), 64), :] = eighths(q, group)
        return 0

    lax.fori_loop(0, QGROUPS, prepare_queries, 0)
    pool(part_k, pq)
    row_at = lax.broadcasted_iota(jnp.int32, (UNITS, 16, HDIM), 1)
    pooled_g = jnp.sum(
        jnp.where(row_at == head, pg[...].astype(F32), 0.0), axis=1
    ).astype(BF16)
    pooled_q = pq[...].astype(BF16)
    pooled_k = pk[...].astype(BF16)
    pooled_v = pv[...].astype(BF16)
    scores = nt(pooled_q, pooled_k) * factor
    weights = jnp.exp(scores - jnp.max(scores, axis=1, keepdims=True))
    probs = weights / jnp.sum(weights, axis=1, keepdims=True)
    dprobs = nt(pooled_g, pooled_v)
    inner = jnp.sum(probs * dprobs, axis=1, keepdims=True)
    dscores = (probs * (dprobs - inner)).astype(BF16)
    cdq[...] = nn(dscores, pooled_k) * (factor / CUBE)
    pk[...] = tn(dscores, pooled_q) * (factor / CUBE)
    pv[...] = tn(probs.astype(BF16), pooled_g) * (1.0 / CUBE)
    wide_0[...] = jnp.zeros_like(wide_0)
    wide_1[...] = jnp.zeros_like(wide_1)

    def listed(n):
        origin = asked_by(head, copy, n // PLANES)
        tile = (n % PLANES * 4 + origin // 8 * 2 + core) * 8 + origin % 8
        cube = cot[tile]
        return [soc[sel[r, cube]] for r in range(TOPK)]

    def beside(ref, lists, c):
        return jnp.concatenate(
            [jnp.concatenate([ref[s] for s in slots[c * 4:c * 4 + 4]], axis=0) for slots in lists],
            axis=1,
        )

    sides = ((prob_0, dsc_0, wide_0), (prob_1, dsc_1, wide_1))

    def advance(old, m_old, new, m_new):
        prob_new, dsc_new, wide_new = sides[new]
        lists_new = [listed(2 * m_new + i) for i in range(2)]
        for i, slots in enumerate(lists_new):
            for r, slot in enumerate(slots):
                held[new, i * TOPK + r] = slot
            rows, lanes = slice(i * CUBE, (i + 1) * CUBE), slice(i * HDIM, (i + 1) * HDIM)
            wide_new[0, rows, lanes] = q[2 * m_new + i]
            wide_new[1, rows, lanes] = fg[2 * m_new + i]
        score, dprob = [], []
        if old is not None:
            prob_old, dsc_old, wide_old = sides[old]
            lists_old = [[held[old, i * TOPK + r] for r in range(TOPK)] for i in range(2)]
            dquery = jnp.zeros((2 * CUBE, 2 * HDIM), F32)
        for c in range(4):
            score.append(nt(beside(k, lists_new, c), wide_new[0]))
            dprob.append(nt(beside(v, lists_new, c), wide_new[1]))
            if old is None:
                continue
            chunk = slice(c * 4 * CUBE, (c + 1) * 4 * CUBE)
            dscore = dsc_old[chunk]
            dquery += tn(dscore, beside(k, lists_old, c))
            key_terms = nn(dscore, wide_old[0])
            value_terms = nn(prob_old[chunk], wide_old[1])
            for i, slots in enumerate(lists_old):
                lanes = slice(i * HDIM, (i + 1) * HDIM)
                for total_of, terms in ((ak, key_terms), (av, value_terms)):
                    before = [total_of[s] for s in slots[c * 4:c * 4 + 4]]
                    for at, s in enumerate(slots[c * 4:c * 4 + 4]):
                        total_of[s] = before[at] + terms[at * CUBE:(at + 1) * CUBE, lanes]
        top = jnp.max(functools.reduce(jnp.maximum, score), axis=0, keepdims=True)
        weight = [jnp.exp((s - top) * factor) for s in score]
        total = jnp.sum(functools.reduce(jnp.add, weight), axis=0, keepdims=True)
        inverse = 1.0 / total
        mixed = functools.reduce(jnp.add, [w * d for w, d in zip(weight, dprob)])
        center = jnp.sum(mixed, axis=0, keepdims=True) * inverse
        for c in range(4):
            chunk = slice(c * 4 * CUBE, (c + 1) * 4 * CUBE)
            prob = weight[c] * inverse
            prob_new[chunk] = prob.astype(BF16)
            dsc_new[chunk] = (prob * (dprob[c] - center)).astype(BF16)
        if old is not None:
            for i in range(2):
                n = 2 * m_old + i
                mine = dquery[i * CUBE:(i + 1) * CUBE, i * HDIM:(i + 1) * HDIM]
                dq[n] = (mine * factor + cdq[pl.ds(n, 1), :]).astype(BF16)

    advance(None, 0, 0, 0)

    def two_pairs(m, _):
        advance(0, 2 * m, 1, 2 * m + 1)
        advance(1, 2 * m + 1, 0, jnp.minimum(2 * m + 2, UNITS // 2 - 1))
        return 0

    lax.fori_loop(0, units // 4, two_pairs, 0)

    def finish(group, _):
        for i in range(4):
            slot = group * 4 + i
            dk[slot] = (ak[slot] * factor + pk[pl.ds(slot, 1), :]).astype(BF16)
            dv[slot] = (av[slot] + pv[pl.ds(slot, 1), :]).astype(BF16)
        return 0

    lax.fori_loop(0, SLOTS // 4, finish, 0)


def attend(tile_of_cube, select, qh, fh, ph, kh, vh):
    smem = pl.BlockSpec(memory_space=pltpu.SMEM)
    vmem = pl.BlockSpec(memory_space=pltpu.VMEM)
    query_shape = jax.ShapeDtypeStruct((UNITS, CUBE, HDIM), BF16)
    keys_shape = jax.ShapeDtypeStruct((SLOTS, CUBE, HDIM), BF16)
    return pl.pallas_call(
        attend_kernel,
        name="attend",
        out_shape=(query_shape, keys_shape, keys_shape),
        in_specs=[smem] * 2 + [vmem] * 5,
        out_specs=[vmem] * 3,
        scratch_shapes=[
            pltpu.VMEM((SLOTS, CUBE, HDIM), F32),
            pltpu.VMEM((SLOTS, CUBE, HDIM), F32),
            pltpu.VMEM((2, 2 * CUBE, 2 * HDIM), BF16),
            pltpu.VMEM((2, 2 * CUBE, 2 * HDIM), BF16),
            pltpu.VMEM((TOPK * CUBE, 2 * CUBE), BF16),
            pltpu.VMEM((TOPK * CUBE, 2 * CUBE), BF16),
            pltpu.VMEM((TOPK * CUBE, 2 * CUBE), BF16),
            pltpu.VMEM((TOPK * CUBE, 2 * CUBE), BF16),
            pltpu.VMEM((SLOTS, HDIM), F32),
            pltpu.VMEM((SLOTS, HDIM), F32),
            pltpu.VMEM((UNITS, HDIM), F32),
            pltpu.VMEM((UNITS, HDIM), F32),
            pltpu.VMEM((SLOTS * 8, HDIM), F32),
            pltpu.VMEM((SLOTS * 8, HDIM), F32),
            pltpu.SMEM((SLOTS,), jnp.int32),
            pltpu.SMEM((SLOTS,), jnp.int32),
            pltpu.SMEM((2, 2 * TOPK), jnp.int32),
        ],
        compiler_params=pltpu.CompilerParams(vmem_limit_bytes=ATTEND_VMEM),
    )(
        tile_of_cube, select.T,
        qh.reshape(UNITS, CUBE, HDIM), fh.reshape(UNITS, CUBE, HDIM),
        ph.reshape(UNITS, 16, HDIM), kh.reshape(SLOTS, CUBE, HDIM), vh.reshape(SLOTS, CUBE, HDIM),
    )


def home_kernel(
    dq, dk, dv,
    oq, ok, ov,
    own_k, own_v, sib_k, sib_v, land_q, land_k, land_v, sum_k, sum_v, sum_q,
    ssend, srecv, psend, precv, zsend, zrecv,
):
    plane, chip, core = where_am_i()
    works, head, replica = role_of(chip)
    greet(plane, chip, core)
    sibling = device_of(plane, chip, 1 - core)
    sources, owns, sibs = (dk, dv), (own_k, own_v), (sib_k, sib_v)
    lands, sums, outs = (land_k, land_v), (sum_k, sum_v), (ok, ov)
    mine = columns(plane)

    @pl.when(works)
    def _():
        for number in range(2):
            def give(d, _, number=number):
                target = (chip + d) % CHIPS
                remote(
                    sources[number].at[(1 - core) * CHIPS + target], sibs[number].at[target],
                    ssend.at[number], srecv.at[number, target], sibling,
                ).start()
                return 0

            lax.fori_loop(0, CHIPS, give, 0)

        def send_query(m, _):
            i = (m + chip) % QGROUPS
            target = asked_by(head, replica, i)

            @pl.when(target != chip)
            def _():
                remote(
                    dq.at[i], land_q.at[head], psend.at[2], precv.at[4],
                    device_of(plane, target, core),
                ).start()

            @pl.when(target == chip)
            def _():
                pltpu.make_async_copy(dq.at[i], land_q.at[head], precv.at[4]).start()

            return 0

        lax.fori_loop(0, QGROUPS, send_query, 0)

    def settle(number, half):
        rows = rows_of(half)
        source, own, sib, land = sources[number], owns[number], sibs[number], lands[number]

        def step(d, _):
            target = (chip + d) % CHIPS
            if half == 0:
                take_bytes(sib.at[target], srecv.at[number, target])
            own[target, :, rows] = (
                source[core * CHIPS + target, :, rows].astype(F32)
                + sib[target, :, rows].astype(F32)
            ).astype(BF16)
            arrived = precv.at[number * 2 + half]

            @pl.when(target != chip)
            def _():
                remote(
                    own.at[target, :, rows], land.at[replica, head, :, rows], psend.at[number],
                    arrived, device_of(plane, target, core),
                ).start()

            @pl.when(target == chip)
            def _():
                pltpu.make_async_copy(
                    own.at[target, :, rows], land.at[replica, head, :, rows], arrived
                ).start()

            return 0

        @pl.when(works)
        def _():
            lax.fori_loop(0, CHIPS, step, 0)

    def send_home(number, block, out, target):
        @pl.when(target != plane)
        def _():
            remote(
                block, out, zsend.at[number], zrecv.at[number], device_of(target, chip, core)
            ).start()

        @pl.when(target == plane)
        def _():
            pltpu.make_async_copy(block, out, zrecv.at[number]).start()

    def queries_home():
        take_bytes(land_q, precv.at[4])

        def step(d, _):
            target = (plane + d) % PLANES
            for j in range(HEADS_PLANE):
                sum_q[target, :, j * HDIM:(j + 1) * HDIM] = land_q[j, target]
            send_home(2, sum_q.at[target], oq.at[:, mine], target)
            return 0

        lax.fori_loop(0, PLANES, step, 0)

    def keys_home(number, half):
        rows = rows_of(half)
        land, total, out = lands[number], sums[number], outs[number]
        take_bytes(land.at[:, :, :, rows], precv.at[number * 2 + half])

        def step(d, _):
            target = (plane + d) % PLANES
            for j in range(HEADS_PLANE):
                summed = land[0, j, target, rows].astype(F32)
                for r in range(1, COPIES):
                    summed += land[r, j, target, rows].astype(F32)
                total[target, rows, j * HDIM:(j + 1) * HDIM] = summed.astype(BF16)
            send_home(number, total.at[target, rows], out.at[rows, mine], target)
            return 0

        lax.fori_loop(0, PLANES, step, 0)

    settle(0, 0)
    settle(0, 1)
    queries_home()
    keys_home(0, 0)
    settle(1, 0)
    keys_home(0, 1)
    settle(1, 1)
    keys_home(1, 0)
    keys_home(1, 1)

    for number, out in enumerate((ok, ov, oq)):
        take_bytes(out, zrecv.at[number])
        take_bytes(sum_q.at[pl.ds(0, PLANES - 1)], zsend.at[number])

    @pl.when(works)
    def _():
        for number in range(2):
            take_bytes(sibs[number], ssend.at[number])
            take_bytes(owns[number].at[pl.ds(0, CHIPS - 1)], psend.at[number])

        take_bytes(dq.at[pl.ds(0, QGROUPS - 1)], psend.at[2])


def home(dq, dk, dv, rows, width):
    anywhere = pl.BlockSpec(memory_space=pl.ANY)
    in_vmem = pl.BlockSpec(memory_space=pltpu.VMEM)
    out_shape = jax.ShapeDtypeStruct((rows, width), BF16)
    half = pltpu.VMEM((CHIPS, PLANES, CUBE, HDIM), BF16)
    slab = pltpu.VMEM((PLANES, CUBE, WIDTH), BF16)
    by_head = pltpu.VMEM((HEADS_PLANE, PLANES, CUBE, HDIM), BF16)
    copies = pltpu.VMEM((COPIES, HEADS_PLANE, PLANES, CUBE, HDIM), BF16)
    return pl.pallas_call(
        home_kernel,
        name="home",
        out_shape=(out_shape,) * 3,
        in_specs=[anywhere, in_vmem, in_vmem],
        out_specs=[anywhere] * 3,
        scratch_shapes=[
            half, half, half, half, by_head, copies, copies, slab, slab, slab,
            pltpu.SemaphoreType.DMA((2,)),
            pltpu.SemaphoreType.DMA((2, CHIPS)),
            pltpu.SemaphoreType.DMA((3,)),
            pltpu.SemaphoreType.DMA((5,)),
            pltpu.SemaphoreType.DMA((3,)),
            pltpu.SemaphoreType.DMA((3,)),
        ],
        compiler_params=pltpu.CompilerParams(
            collective_id=1, has_side_effects=True, vmem_limit_bytes=HOME_VMEM
        ),
    )(
        dq.reshape(QGROUPS, PLANES, CUBE, HDIM),
        dk.reshape(2 * CHIPS, PLANES, CUBE, HDIM),
        dv.reshape(2 * CHIPS, PLANES, CUBE, HDIM),
    )


def on_device(queries, keys_in, values, grad_out, fine_gate, coarse_gate, tile_of_cube, select):
    kh, vh, qh, fh, ph = bring(keys_in, values, queries, grad_out, fine_gate, coarse_gate)
    dq, dk, dv = attend(tile_of_cube, select, qh, fh, ph, kh, vh)
    return home(dq, dk, dv, *queries.shape)


def solution(mesh):
    split = P(("tok", "head"), None)
    return jax.shard_map(
        on_device,
        mesh=mesh,
        in_specs=(split,) * 6 + (P(), P()),
        out_specs=(split,) * 3,
        check_vma=False,
    )
```

```python
import functools
import math

import jax
import jax.numpy as jnp
from jax import lax
from jax.experimental import pallas as pl
from jax.experimental.pallas import tpu as pltpu
from jax.sharding import PartitionSpec as P

MESH = pl.DeviceIdType.MESH
BF16 = jnp.bfloat16
F32 = jnp.float32

CUBE = 64
HDIM = 128
PLANES = 8
CHIPS = 16
HEADS_PLANE = 5
COPIES = 2
WORKERS = HEADS_PLANE * COPIES
WIDTH = HEADS_PLANE * HDIM
QGROUPS = 8
TOPK = 16
SLOTS = 2 * CHIPS * PLANES
UNITS = QGROUPS * PLANES
HALF = CUBE // 2
STAGES = 8
ATTEND_VMEM = 30 * 2**20
HOME_VMEM = 20 * 2**20
BRING_VMEM = 16 * 2**20


def where_am_i():
    tok = lax.axis_index("tok")
    head = lax.axis_index("head")
    plane = tok // 4
    chip = (tok // 2) % 2 * 8 + head
    core = tok % 2
    return plane, chip, core


def role_of(chip):
    x, y = chip % 4, chip // 4
    plain = y % 2 == x % 2
    return plain | ((y % 2 == 1) & (x == y - 1)), jnp.where(plain, x, HEADS_PLANE - 1), y // 2


def chip_of(head, copy):
    return jnp.where(head < HEADS_PLANE - 1, head % 2 * 4 + 8 * copy + head, 10 * copy + 4)


def odd_rows(head):
    return jnp.where(head < HEADS_PLANE - 1, head % 2, 1)


def asks(head, chip):
    x, y = chip % 4, chip // 4
    own = y % 2 == odd_rows(head)
    row = jnp.where(own, y, (y + 5 - 2 * ((x + head) % 2)) % 4)
    return row // 2, jnp.where(own, x, 4 + x)


def asked_by(head, copy, group):
    x, row = group % 4, odd_rows(head) + 2 * copy
    y = jnp.where(group < 4, row, (row + 3 + 2 * ((x + head) % 2)) % 4)
    return y * 4 + x


def device_of(plane, chip, core):
    return {"tok": plane * 4 + chip // 8 * 2 + core, "head": chip % 8}


def remote(src, dst, send, recv, device):
    return pltpu.make_async_remote_copy(
        src_ref=src, dst_ref=dst, send_sem=send, recv_sem=recv, device_id=device, device_id_type=MESH
    )


def take_bytes(ref, sem):
    pltpu.make_async_copy(ref, ref, sem).wait()


def greet(plane, chip, core):
    barrier = pltpu.get_barrier_semaphore()

    def along_z(d, _):
        pl.semaphore_signal(
            barrier, inc=1, device_id=device_of((plane + d) % PLANES, chip, core), device_id_type=MESH
        )
        return 0

    def in_plane(d, _):
        pl.semaphore_signal(
            barrier, inc=1, device_id=device_of(plane, (chip + d) % CHIPS, core), device_id_type=MESH
        )
        return 0

    lax.fori_loop(1, PLANES, along_z, 0)
    lax.fori_loop(1, CHIPS, in_plane, 0)
    pl.semaphore_signal(
        barrier, inc=1, device_id=device_of(plane, chip, 1 - core), device_id_type=MESH
    )
    pl.semaphore_wait(barrier, PLANES - 1 + CHIPS - 1 + 1)


def columns(group, width=WIDTH):
    return pl.ds(pl.multiple_of(group * width, 128), width)


def rows_of(half):
    return pl.ds(half * HALF, HALF)


def bring_kernel(
    tokens, gates_in,
    kh, vh, qh, fh, ph,
    packed, kz, vz, qz, fz, pz, pg,
    zsend, zrecv, psend, krecv, qrecv, fsend, frecv,
):
    plane, chip, core = where_am_i()
    greet(plane, chip, core)

    def start_along_z(stage, source, landing):
        def step(d, _):
            target = (plane + d) % PLANES
            remote(
                source(target), landing(plane), zsend.at[stage], zrecv.at[stage],
                device_of(target, chip, core),
            ).start()
            return 0

        lax.fori_loop(1, PLANES, step, 0)
        pltpu.make_async_copy(source(plane), landing(plane), zrecv.at[stage]).start()

    slabs = (kz, vz, qz, fz)
    outs = (kh, vh, qh, fh)

    def start_stage(stage):
        number, rows = stage // 2, rows_of(stage % 2)
        start_along_z(
            stage,
            lambda t: packed.at[number, t, :, rows],
            lambda t: slabs[number].at[:, t, rows],
        )

    def pack(number):
        def step(group, _):
            for j in range(HEADS_PLANE):
                packed[number, group, j] = tokens[number, :, columns(group * HEADS_PLANE + j, HDIM)]
            return 0

        lax.fori_loop(0, PLANES, step, 0)

    pack(0)
    start_stage(0)
    pack(1)
    pack(2)

    heads = gates_in.shape[0] // 2

    def gates(group, _):
        row = lax.broadcasted_iota(jnp.int32, (heads, WIDTH), 0)
        col = lax.broadcasted_iota(jnp.int32, (heads, WIDTH), 1)
        spread = jnp.where(
            row == group * HEADS_PLANE + lax.shift_right_logical(col, 7), 1.0, 0.0
        ).astype(BF16)
        grad = tokens[3, :, columns(group)].astype(F32)
        fine = (tn(gates_in[:heads], spread) * grad).astype(BF16)
        coarse = tn(gates_in[heads:], spread)
        pooled = jnp.sum(coarse * grad, axis=0, keepdims=True)
        rows = []
        for j in range(HEADS_PLANE):
            packed[3, group, j] = fine[:, j * HDIM:(j + 1) * HDIM]
            rows.append(pooled[:, j * HDIM:(j + 1) * HDIM])
        rows.append(jnp.zeros((16 - HEADS_PLANE, HDIM), F32))
        pg[group] = jnp.concatenate(rows, axis=0).astype(BF16)
        return 0

    lax.fori_loop(0, PLANES, gates, 0)
    start_stage(1)
    works, _, _ = role_of(chip)

    def share_keys(number, rows):
        landed, out = slabs[number], outs[number]

        def step(m, _):
            worker = (m + chip) % WORKERS
            head = worker % HEADS_PLANE
            target = chip_of(head, worker // HEADS_PLANE)
            here, there = landed.at[head, :, rows], out.at[core * CHIPS + chip, :, rows]

            @pl.when(target != chip)
            def _():
                remote(
                    here, there, psend.at[number], krecv.at[number, chip],
                    device_of(plane, target, core),
                ).start()

            @pl.when(target == chip)
            def _():
                pltpu.make_async_copy(here, there, krecv.at[number, chip]).start()

            return 0

        lax.fori_loop(0, WORKERS, step, 0)

    def share_queries(number, pick, place):
        def step(m, _):
            j = (m + chip) % HEADS_PLANE
            copy, group = asks(j, chip)
            target = chip_of(j, copy)

            @pl.when(target != chip)
            def _():
                remote(
                    pick(j), place(group), psend.at[number],
                    qrecv.at[number - 2], device_of(plane, target, core),
                ).start()

            @pl.when(target == chip)
            def _():
                pltpu.make_async_copy(
                    pick(j), place(group), qrecv.at[number - 2]
                ).start()

            return 0

        lax.fori_loop(0, HEADS_PLANE, step, 0)

    sibling = device_of(plane, chip, 1 - core)

    def forward(number):
        out = outs[number]

        def step(d, _):
            origin = (chip + CHIPS - d) % CHIPS
            block = out.at[core * CHIPS + origin]
            take_bytes(block, krecv.at[number, origin])
            remote(block, block, fsend.at[number], frecv.at[number], sibling).start()
            return 0

        @pl.when(works)
        def _():
            lax.fori_loop(0, CHIPS, step, 0)

    for stage in range(STAGES):
        number, rows = stage // 2, rows_of(stage % 2)
        take_bytes(slabs[number].at[:, :, rows], zrecv.at[stage])
        if stage + 2 == STAGES - 2:
            start_along_z(STAGES, lambda t: pg.at[t], lambda t: pz.at[t])
        if stage + 2 < STAGES:
            start_stage(stage + 2)
        if number < 2:
            share_keys(number, rows)
        else:
            share_queries(
                number,
                lambda j, number=number, rows=rows: slabs[number].at[j, :, rows],
                lambda i, number=number, rows=rows: outs[number].at[i, :, rows],
            )
        if stage == STAGES - 2:
            take_bytes(pz, zrecv.at[STAGES])
            share_queries(4, lambda j: pz, lambda i: ph.at[i])
            forward(0)
    forward(1)

    @pl.when(works)
    def _():
        for number, out in enumerate((qh, fh, ph)):
            take_bytes(out, qrecv.at[number])

        for number, out in ((0, kh), (1, vh)):
            theirs = out.at[pl.ds((1 - core) * CHIPS, CHIPS)]
            take_bytes(theirs, frecv.at[number])
            take_bytes(theirs, fsend.at[number])

    for stage in range(STAGES):
        landed = slabs[stage // 2].at[:, pl.ds(0, PLANES - 1), rows_of(stage % 2)]
        take_bytes(landed, zsend.at[stage])
    take_bytes(pz.at[pl.ds(0, PLANES - 1)], zsend.at[STAGES])

    def drain(keys, queries):
        for number, out in ((0, kh), (1, vh)):
            take_bytes(out.at[pl.ds(0, keys)], psend.at[number])
        for number, out in ((2, qh), (3, fh), (4, ph)):
            take_bytes(out.at[pl.ds(0, queries)], psend.at[number])

    @pl.when(works)
    def _():
        drain(WORKERS - 1, HEADS_PLANE - 1)

    @pl.when(jnp.logical_not(works))
    def _():
        drain(WORKERS, HEADS_PLANE)


def bring(keys_in, values, queries, grad_out, fine_gate, coarse_gate):
    keys_shape = jax.ShapeDtypeStruct((2 * CHIPS, PLANES, CUBE, HDIM), BF16)
    query_shape = jax.ShapeDtypeStruct((QGROUPS, PLANES, CUBE, HDIM), BF16)
    pooled_shape = jax.ShapeDtypeStruct((QGROUPS, PLANES, 16, HDIM), BF16)
    anywhere = pl.BlockSpec(memory_space=pl.ANY)
    in_vmem = pl.BlockSpec(memory_space=pltpu.VMEM)
    slab = pltpu.VMEM((HEADS_PLANE, PLANES, CUBE, HDIM), BF16)
    small = pltpu.VMEM((PLANES, 16, HDIM), BF16)
    return pl.pallas_call(
        bring_kernel,
        name="bring",
        out_shape=(keys_shape, keys_shape, query_shape, query_shape, pooled_shape),
        in_specs=[in_vmem] * 2,
        out_specs=[anywhere] * 5,
        scratch_shapes=[
            pltpu.VMEM((4, PLANES, HEADS_PLANE, CUBE, HDIM), BF16),
            slab, slab, slab, slab, small, small,
            pltpu.SemaphoreType.DMA((STAGES + 1,)),
            pltpu.SemaphoreType.DMA((STAGES + 1,)),
            pltpu.SemaphoreType.DMA((5,)),
            pltpu.SemaphoreType.DMA((2, CHIPS)),
            pltpu.SemaphoreType.DMA((3,)),
            pltpu.SemaphoreType.DMA((2,)),
            pltpu.SemaphoreType.DMA((2,)),
        ],
        compiler_params=pltpu.CompilerParams(
            collective_id=0, has_side_effects=True, vmem_limit_bytes=BRING_VMEM
        ),
    )(
        jnp.stack([keys_in, values, queries, grad_out]),
        jnp.concatenate([fine_gate.T, coarse_gate.T], axis=0),
    )


def nt(a, b):
    return lax.dot_general(a, b, (((1,), (1,)), ((), ())), preferred_element_type=F32)


def tn(a, b):
    return lax.dot_general(a, b, (((0,), (0,)), ((), ())), preferred_element_type=F32)


def nn(a, b):
    return jnp.dot(a, b, preferred_element_type=F32)


def attend_kernel(
    toc, sel, q, fg, pg, k, v,
    dq, dk, dv,
    ak, av, wide_0, wide_1, prob_0, prob_1, dsc_0, dsc_1,
    pk, pv, pq, cdq, part_k, part_v, cot, soc, held,
):
    _, chip, core = where_am_i()
    works, head, copy = role_of(chip)
    units = jnp.where(works, UNITS, 0)
    factor = 1.0 / math.sqrt(HDIM)
    log2e = math.log2(math.e)

    def eighths(source, group):
        block = source[pl.ds(pl.multiple_of(group * 8, 8), 8)].astype(F32)
        return jnp.sum(block.reshape(8, 8, 8, HDIM), axis=1).reshape(64, HDIM)

    def prepare(group, _):
        rows = pl.ds(pl.multiple_of(group * 64, 64), 64)
        part_k[rows, :] = eighths(k, group)
        part_v[rows, :] = eighths(v, group)
        for total_of in (ak, av):
            total_of[pl.ds(pl.multiple_of(group * 8, 8), 8)] = jnp.zeros((8, CUBE, HDIM), F32)
        for i in range(8):
            cube = group * 8 + i
            tile = toc[cube]
            cot[tile] = cube
            soc[cube] = (
                lax.shift_left(lax.shift_right_logical(tile, 3) & 1, 7)
                + lax.shift_left(lax.shift_right_logical(tile, 4) & 1, 6)
                + lax.shift_left(tile & 7, 3)
                + lax.shift_right_logical(tile, 5)
            )
        return 0

    lax.fori_loop(0, SLOTS // 8, prepare, 0)

    def pool(part, into):
        count = into.shape[0]
        total = part[pl.ds(0, count, stride=8), :]
        for row in range(1, 8):
            total += part[pl.ds(row, count, stride=8), :]
        into[...] = total * (1.0 / CUBE)

    pool(part_k, pk)
    pool(part_v, pv)

    def prepare_queries(group, _):
        part_k[pl.ds(pl.multiple_of(group * 64, 64), 64), :] = eighths(q, group)
        return 0

    lax.fori_loop(0, QGROUPS, prepare_queries, 0)
    pool(part_k, pq)
    row_at = lax.broadcasted_iota(jnp.int32, (UNITS, 16, HDIM), 1)
    pooled_g = jnp.sum(
        jnp.where(row_at == head, pg[...].astype(F32), 0.0), axis=1
    ).astype(BF16)
    pooled_q = pq[...].astype(BF16)
    pooled_k = pk[...].astype(BF16)
    pooled_v = pv[...].astype(BF16)
    scores = nt(pooled_q, pooled_k) * factor
    weights = jnp.exp(scores - jnp.max(scores, axis=1, keepdims=True))
    probs = weights / jnp.sum(weights, axis=1, keepdims=True)
    dprobs = nt(pooled_g, pooled_v)
    inner = jnp.sum(probs * dprobs, axis=1, keepdims=True)
    dscores = (probs * (dprobs - inner)).astype(BF16)
    cdq[...] = nn(dscores, pooled_k) * (factor / CUBE)
    pk[...] = tn(dscores, pooled_q) * (factor / CUBE)
    pv[...] = tn(probs.astype(BF16), pooled_g) * (1.0 / CUBE)
    wide_0[...] = jnp.zeros_like(wide_0)
    wide_1[...] = jnp.zeros_like(wide_1)

    def listed(n):
        origin = asked_by(head, copy, n // PLANES)
        tile = (n % PLANES * 4 + origin // 8 * 2 + core) * 8 + origin % 8
        cube = cot[tile]
        return [soc[sel[r, cube]] for r in range(TOPK)]

    def beside(ref, lists, c):
        return jnp.concatenate(
            [jnp.concatenate([ref[s] for s in slots[c * 4:c * 4 + 4]], axis=0) for slots in lists],
            axis=1,
        )

    sides = ((prob_0, dsc_0, wide_0), (prob_1, dsc_1, wide_1))

    def advance(old, m_old, new, m_new):
        prob_new, dsc_new, wide_new = sides[new]
        lists_new = [listed(2 * m_new + i) for i in range(2)]
        for i, slots in enumerate(lists_new):
            for r, slot in enumerate(slots):
                held[new, i * TOPK + r] = slot
            rows, lanes = slice(i * CUBE, (i + 1) * CUBE), slice(i * HDIM, (i + 1) * HDIM)
            wide_new[0, rows, lanes] = q[2 * m_new + i]
            wide_new[1, rows, lanes] = fg[2 * m_new + i]
        score, dprob = [], []
        if old is not None:
            prob_old, dsc_old, wide_old = sides[old]
            lists_old = [[held[old, i * TOPK + r] for r in range(TOPK)] for i in range(2)]
            dquery = jnp.zeros((2 * CUBE, 2 * HDIM), F32)
        for c in range(4):
            score.append(nt(beside(k, lists_new, c), wide_new[0]))
            dprob.append(nt(beside(v, lists_new, c), wide_new[1]))
            if old is None:
                continue
            chunk = slice(c * 4 * CUBE, (c + 1) * 4 * CUBE)
            dscore = dsc_old[chunk]
            dquery += tn(dscore, beside(k, lists_old, c))
            key_terms = nn(dscore, wide_old[0])
            value_terms = nn(prob_old[chunk], wide_old[1])
            for i, slots in enumerate(lists_old):
                lanes = slice(i * HDIM, (i + 1) * HDIM)
                for total_of, terms in ((ak, key_terms), (av, value_terms)):
                    before = [total_of[s] for s in slots[c * 4:c * 4 + 4]]
                    for at, s in enumerate(slots[c * 4:c * 4 + 4]):
                        total_of[s] = before[at] + terms[at * CUBE:(at + 1) * CUBE, lanes]
        top = jnp.max(functools.reduce(jnp.maximum, score), axis=0, keepdims=True)
        weight = [jnp.exp2((s - top) * (factor * log2e)) for s in score]
        total = jnp.sum(functools.reduce(jnp.add, weight), axis=0, keepdims=True)
        inverse = 1.0 / total
        mixed = functools.reduce(jnp.add, [w * d for w, d in zip(weight, dprob)])
        center = jnp.sum(mixed, axis=0, keepdims=True) * inverse
        for c in range(4):
            chunk = slice(c * 4 * CUBE, (c + 1) * 4 * CUBE)
            prob = weight[c] * inverse
            prob_new[chunk] = prob.astype(BF16)
            dsc_new[chunk] = (prob * (dprob[c] - center)).astype(BF16)
        if old is not None:
            for i in range(2):
                n = 2 * m_old + i
                mine = dquery[i * CUBE:(i + 1) * CUBE, i * HDIM:(i + 1) * HDIM]
                dq[n] = (mine * factor + cdq[pl.ds(n, 1), :]).astype(BF16)

    advance(None, 0, 0, 0)

    def two_pairs(m, _):
        advance(0, 2 * m, 1, 2 * m + 1)
        advance(1, 2 * m + 1, 0, jnp.minimum(2 * m + 2, UNITS // 2 - 1))
        return 0

    lax.fori_loop(0, units // 4, two_pairs, 0)

    def finish(group, _):
        for i in range(4):
            slot = group * 4 + i
            dk[slot] = (ak[slot] * factor + pk[pl.ds(slot, 1), :]).astype(BF16)
            dv[slot] = (av[slot] + pv[pl.ds(slot, 1), :]).astype(BF16)
        return 0

    lax.fori_loop(0, SLOTS // 4, finish, 0)


def attend(tile_of_cube, select, qh, fh, ph, kh, vh):
    smem = pl.BlockSpec(memory_space=pltpu.SMEM)
    vmem = pl.BlockSpec(memory_space=pltpu.VMEM)
    query_shape = jax.ShapeDtypeStruct((UNITS, CUBE, HDIM), BF16)
    keys_shape = jax.ShapeDtypeStruct((SLOTS, CUBE, HDIM), BF16)
    return pl.pallas_call(
        attend_kernel,
        name="attend",
        out_shape=(query_shape, keys_shape, keys_shape),
        in_specs=[smem] * 2 + [vmem] * 5,
        out_specs=[vmem] * 3,
        scratch_shapes=[
            pltpu.VMEM((SLOTS, CUBE, HDIM), F32),
            pltpu.VMEM((SLOTS, CUBE, HDIM), F32),
            pltpu.VMEM((2, 2 * CUBE, 2 * HDIM), BF16),
            pltpu.VMEM((2, 2 * CUBE, 2 * HDIM), BF16),
            pltpu.VMEM((TOPK * CUBE, 2 * CUBE), BF16),
            pltpu.VMEM((TOPK * CUBE, 2 * CUBE), BF16),
            pltpu.VMEM((TOPK * CUBE, 2 * CUBE), BF16),
            pltpu.VMEM((TOPK * CUBE, 2 * CUBE), BF16),
            pltpu.VMEM((SLOTS, HDIM), F32),
            pltpu.VMEM((SLOTS, HDIM), F32),
            pltpu.VMEM((UNITS, HDIM), F32),
            pltpu.VMEM((UNITS, HDIM), F32),
            pltpu.VMEM((SLOTS * 8, HDIM), F32),
            pltpu.VMEM((SLOTS * 8, HDIM), F32),
            pltpu.SMEM((SLOTS,), jnp.int32),
            pltpu.SMEM((SLOTS,), jnp.int32),
            pltpu.SMEM((2, 2 * TOPK), jnp.int32),
        ],
        compiler_params=pltpu.CompilerParams(vmem_limit_bytes=ATTEND_VMEM),
    )(
        tile_of_cube, select.T,
        qh.reshape(UNITS, CUBE, HDIM), fh.reshape(UNITS, CUBE, HDIM),
        ph.reshape(UNITS, 16, HDIM), kh.reshape(SLOTS, CUBE, HDIM), vh.reshape(SLOTS, CUBE, HDIM),
    )


def home_kernel(
    dq, dk, dv,
    oq, ok, ov,
    own_k, own_v, sib_k, sib_v, land_q, land_k, land_v, sum_k, sum_v, sum_q,
    ssend, srecv, psend, precv, zsend, zrecv,
):
    plane, chip, core = where_am_i()
    works, head, replica = role_of(chip)
    greet(plane, chip, core)
    sibling = device_of(plane, chip, 1 - core)
    sources, owns, sibs = (dk, dv), (own_k, own_v), (sib_k, sib_v)
    lands, sums, outs = (land_k, land_v), (sum_k, sum_v), (ok, ov)
    mine = columns(plane)

    @pl.when(works)
    def _():
        for number in range(2):
            def give(d, _, number=number):
                target = (chip + d) % CHIPS
                remote(
                    sources[number].at[(1 - core) * CHIPS + target], sibs[number].at[target],
                    ssend.at[number], srecv.at[number, target], sibling,
                ).start()
                return 0

            lax.fori_loop(0, CHIPS, give, 0)

        def send_query(m, _):
            i = (m + chip) % QGROUPS
            target = asked_by(head, replica, i)

            @pl.when(target != chip)
            def _():
                remote(
                    dq.at[i], land_q.at[head], psend.at[2], precv.at[4],
                    device_of(plane, target, core),
                ).start()

            @pl.when(target == chip)
            def _():
                pltpu.make_async_copy(dq.at[i], land_q.at[head], precv.at[4]).start()

            return 0

        lax.fori_loop(0, QGROUPS, send_query, 0)

    def settle(number, half):
        rows = rows_of(half)
        source, own, sib, land = sources[number], owns[number], sibs[number], lands[number]

        def step(d, _):
            target = (chip + d) % CHIPS
            if half == 0:
                take_bytes(sib.at[target], srecv.at[number, target])
            own[target, :, rows] = (
                source[core * CHIPS + target, :, rows].astype(F32)
                + sib[target, :, rows].astype(F32)
            ).astype(BF16)
            arrived = precv.at[number * 2 + half]

            @pl.when(target != chip)
            def _():
                remote(
                    own.at[target, :, rows], land.at[replica, head, :, rows], psend.at[number],
                    arrived, device_of(plane, target, core),
                ).start()

            @pl.when(target == chip)
            def _():
                pltpu.make_async_copy(
                    own.at[target, :, rows], land.at[replica, head, :, rows], arrived
                ).start()

            return 0

        @pl.when(works)
        def _():
            lax.fori_loop(0, CHIPS, step, 0)

    def send_home(number, block, out, target):
        @pl.when(target != plane)
        def _():
            remote(
                block, out, zsend.at[number], zrecv.at[number], device_of(target, chip, core)
            ).start()

        @pl.when(target == plane)
        def _():
            pltpu.make_async_copy(block, out, zrecv.at[number]).start()

    def queries_home():
        take_bytes(land_q, precv.at[4])

        def step(d, _):
            target = (plane + d) % PLANES
            for j in range(HEADS_PLANE):
                sum_q[target, :, j * HDIM:(j + 1) * HDIM] = land_q[j, target]
            send_home(2, sum_q.at[target], oq.at[:, mine], target)
            return 0

        lax.fori_loop(0, PLANES, step, 0)

    def keys_home(number, half):
        rows = rows_of(half)
        land, total, out = lands[number], sums[number], outs[number]
        take_bytes(land.at[:, :, :, rows], precv.at[number * 2 + half])

        def step(d, _):
            target = (plane + d) % PLANES
            for j in range(HEADS_PLANE):
                summed = land[0, j, target, rows].astype(F32)
                for r in range(1, COPIES):
                    summed += land[r, j, target, rows].astype(F32)
                total[target, rows, j * HDIM:(j + 1) * HDIM] = summed.astype(BF16)
            send_home(number, total.at[target, rows], out.at[rows, mine], target)
            return 0

        lax.fori_loop(0, PLANES, step, 0)

    settle(0, 0)
    settle(0, 1)
    queries_home()
    keys_home(0, 0)
    settle(1, 0)
    keys_home(0, 1)
    settle(1, 1)
    keys_home(1, 0)
    keys_home(1, 1)

    for number, out in enumerate((ok, ov, oq)):
        take_bytes(out, zrecv.at[number])
        take_bytes(sum_q.at[pl.ds(0, PLANES - 1)], zsend.at[number])

    @pl.when(works)
    def _():
        for number in range(2):
            take_bytes(sibs[number], ssend.at[number])
            take_bytes(owns[number].at[pl.ds(0, CHIPS - 1)], psend.at[number])

        take_bytes(dq.at[pl.ds(0, QGROUPS - 1)], psend.at[2])


def home(dq, dk, dv, rows, width):
    anywhere = pl.BlockSpec(memory_space=pl.ANY)
    in_vmem = pl.BlockSpec(memory_space=pltpu.VMEM)
    out_shape = jax.ShapeDtypeStruct((rows, width), BF16)
    half = pltpu.VMEM((CHIPS, PLANES, CUBE, HDIM), BF16)
    slab = pltpu.VMEM((PLANES, CUBE, WIDTH), BF16)
    by_head = pltpu.VMEM((HEADS_PLANE, PLANES, CUBE, HDIM), BF16)
    copies = pltpu.VMEM((COPIES, HEADS_PLANE, PLANES, CUBE, HDIM), BF16)
    return pl.pallas_call(
        home_kernel,
        name="home",
        out_shape=(out_shape,) * 3,
        in_specs=[anywhere, in_vmem, in_vmem],
        out_specs=[anywhere] * 3,
        scratch_shapes=[
            half, half, half, half, by_head, copies, copies, slab, slab, slab,
            pltpu.SemaphoreType.DMA((2,)),
            pltpu.SemaphoreType.DMA((2, CHIPS)),
            pltpu.SemaphoreType.DMA((3,)),
            pltpu.SemaphoreType.DMA((5,)),
            pltpu.SemaphoreType.DMA((3,)),
            pltpu.SemaphoreType.DMA((3,)),
        ],
        compiler_params=pltpu.CompilerParams(
            collective_id=1, has_side_effects=True, vmem_limit_bytes=HOME_VMEM
        ),
    )(
        dq.reshape(QGROUPS, PLANES, CUBE, HDIM),
        dk.reshape(2 * CHIPS, PLANES, CUBE, HDIM),
        dv.reshape(2 * CHIPS, PLANES, CUBE, HDIM),
    )


def on_device(queries, keys_in, values, grad_out, fine_gate, coarse_gate, tile_of_cube, select):
    kh, vh, qh, fh, ph = bring(keys_in, values, queries, grad_out, fine_gate, coarse_gate)
    dq, dk, dv = attend(tile_of_cube, select, qh, fh, ph, kh, vh)
    return home(dq, dk, dv, *queries.shape)


def solution(mesh):
    split = P(("tok", "head"), None)
    return jax.shard_map(
        on_device,
        mesh=mesh,
        in_specs=(split,) * 6 + (P(), P()),
        out_specs=(split,) * 3,
        check_vma=False,
    )
```

```python
import functools
import math

import jax
import jax.numpy as jnp
from jax import lax
from jax.experimental import pallas as pl
from jax.experimental.pallas import tpu as pltpu
from jax.sharding import PartitionSpec as P

MESH = pl.DeviceIdType.MESH
BF16 = jnp.bfloat16
F32 = jnp.float32

CUBE = 64
HDIM = 128
PLANES = 8
CHIPS = 16
HEADS_PLANE = 5
COPIES = 2
WORKERS = HEADS_PLANE * COPIES
WIDTH = HEADS_PLANE * HDIM
QGROUPS = 8
TOPK = 16
SLOTS = 2 * CHIPS * PLANES
UNITS = QGROUPS * PLANES
HALF = CUBE // 2
STAGES = 8
ATTEND_VMEM = 30 * 2**20
HOME_VMEM = 20 * 2**20
BRING_VMEM = 16 * 2**20


def where_am_i():
    tok = lax.axis_index("tok")
    head = lax.axis_index("head")
    plane = tok // 4
    chip = (tok // 2) % 2 * 8 + head
    core = tok % 2
    return plane, chip, core


def role_of(chip):
    x, y = chip % 4, chip // 4
    plain = y % 2 == x % 2
    return plain | ((y % 2 == 1) & (x == y - 1)), jnp.where(plain, x, HEADS_PLANE - 1), y // 2


def chip_of(head, copy):
    return jnp.where(head < HEADS_PLANE - 1, head % 2 * 4 + 8 * copy + head, 10 * copy + 4)


def odd_rows(head):
    return jnp.where(head < HEADS_PLANE - 1, head % 2, 1)


def asks(head, chip):
    x, y = chip % 4, chip // 4
    own = y % 2 == odd_rows(head)
    row = jnp.where(own, y, (y + 5 - 2 * ((x + head) % 2)) % 4)
    return row // 2, jnp.where(own, x, 4 + x)


def asked_by(head, copy, group):
    x, row = group % 4, odd_rows(head) + 2 * copy
    y = jnp.where(group < 4, row, (row + 3 + 2 * ((x + head) % 2)) % 4)
    return y * 4 + x


def device_of(plane, chip, core):
    return {"tok": plane * 4 + chip // 8 * 2 + core, "head": chip % 8}


def remote(src, dst, send, recv, device):
    return pltpu.make_async_remote_copy(
        src_ref=src, dst_ref=dst, send_sem=send, recv_sem=recv, device_id=device, device_id_type=MESH
    )


def take_bytes(ref, sem):
    pltpu.make_async_copy(ref, ref, sem).wait()


def greet(plane, chip, core):
    barrier = pltpu.get_barrier_semaphore()

    def along_z(d, _):
        pl.semaphore_signal(
            barrier, inc=1, device_id=device_of((plane + d) % PLANES, chip, core), device_id_type=MESH
        )
        return 0

    def in_plane(d, _):
        pl.semaphore_signal(
            barrier, inc=1, device_id=device_of(plane, (chip + d) % CHIPS, core), device_id_type=MESH
        )
        return 0

    lax.fori_loop(1, PLANES, along_z, 0)
    lax.fori_loop(1, CHIPS, in_plane, 0)
    pl.semaphore_signal(
        barrier, inc=1, device_id=device_of(plane, chip, 1 - core), device_id_type=MESH
    )
    pl.semaphore_wait(barrier, PLANES - 1 + CHIPS - 1 + 1)


def columns(group, width=WIDTH):
    return pl.ds(pl.multiple_of(group * width, 128), width)


def rows_of(half):
    return pl.ds(half * HALF, HALF)


def bring_kernel(
    tokens, gates_in,
    kh, vh, qh, fh, ph,
    packed, kz, vz, qz, fz, pz, pg,
    zsend, zrecv, psend, krecv, qrecv, fsend, frecv,
):
    plane, chip, core = where_am_i()
    greet(plane, chip, core)

    def start_along_z(stage, source, landing):
        def step(d, _):
            target = (plane + d) % PLANES
            remote(
                source(target), landing(plane), zsend.at[stage], zrecv.at[stage],
                device_of(target, chip, core),
            ).start()
            return 0

        lax.fori_loop(1, PLANES, step, 0)
        pltpu.make_async_copy(source(plane), landing(plane), zrecv.at[stage]).start()

    slabs = (kz, vz, qz, fz)
    outs = (kh, vh, qh, fh)

    def start_stage(stage):
        number, rows = stage // 2, rows_of(stage % 2)
        start_along_z(
            stage,
            lambda t: packed.at[number, t, :, rows],
            lambda t: slabs[number].at[:, t, rows],
        )

    def pack(number):
        def step(group, _):
            for j in range(HEADS_PLANE):
                packed[number, group, j] = tokens[number, :, columns(group * HEADS_PLANE + j, HDIM)]
            return 0

        lax.fori_loop(0, PLANES, step, 0)

    pack(0)
    start_stage(0)
    pack(1)
    pack(2)

    heads = gates_in.shape[0] // 2

    def gates(group, _):
        row = lax.broadcasted_iota(jnp.int32, (heads, WIDTH), 0)
        col = lax.broadcasted_iota(jnp.int32, (heads, WIDTH), 1)
        spread = jnp.where(
            row == group * HEADS_PLANE + lax.shift_right_logical(col, 7), 1.0, 0.0
        ).astype(BF16)
        grad = tokens[3, :, columns(group)].astype(F32)
        fine = (tn(gates_in[:heads], spread) * grad).astype(BF16)
        coarse = tn(gates_in[heads:], spread)
        pooled = jnp.sum(coarse * grad, axis=0, keepdims=True)
        rows = []
        for j in range(HEADS_PLANE):
            packed[3, group, j] = fine[:, j * HDIM:(j + 1) * HDIM]
            rows.append(pooled[:, j * HDIM:(j + 1) * HDIM])
        rows.append(jnp.zeros((16 - HEADS_PLANE, HDIM), F32))
        pg[group] = jnp.concatenate(rows, axis=0).astype(BF16)
        return 0

    lax.fori_loop(0, PLANES, gates, 0)
    start_stage(1)
    works, _, _ = role_of(chip)

    def share_keys(number, rows):
        landed, out = slabs[number], outs[number]

        def step(m, _):
            worker = (m + chip) % WORKERS
            head = worker % HEADS_PLANE
            target = chip_of(head, worker // HEADS_PLANE)
            here, there = landed.at[head, :, rows], out.at[core * CHIPS + chip, :, rows]

            @pl.when(target != chip)
            def _():
                remote(
                    here, there, psend.at[number], krecv.at[number, chip],
                    device_of(plane, target, core),
                ).start()

            @pl.when(target == chip)
            def _():
                pltpu.make_async_copy(here, there, krecv.at[number, chip]).start()

            return 0

        lax.fori_loop(0, WORKERS, step, 0)

    def share_queries(number, pick, place):
        def step(m, _):
            j = (m + chip) % HEADS_PLANE
            copy, group = asks(j, chip)
            target = chip_of(j, copy)

            @pl.when(target != chip)
            def _():
                remote(
                    pick(j), place(group), psend.at[number],
                    qrecv.at[number - 2], device_of(plane, target, core),
                ).start()

            @pl.when(target == chip)
            def _():
                pltpu.make_async_copy(
                    pick(j), place(group), qrecv.at[number - 2]
                ).start()

            return 0

        lax.fori_loop(0, HEADS_PLANE, step, 0)

    sibling = device_of(plane, chip, 1 - core)

    def forward(number):
        out = outs[number]

        def step(d, _):
            origin = (chip + CHIPS - d) % CHIPS
            block = out.at[core * CHIPS + origin]
            take_bytes(block, krecv.at[number, origin])
            remote(block, block, fsend.at[number], frecv.at[number], sibling).start()
            return 0

        @pl.when(works)
        def _():
            lax.fori_loop(0, CHIPS, step, 0)

    for stage in range(STAGES):
        number, rows = stage // 2, rows_of(stage % 2)
        take_bytes(slabs[number].at[:, :, rows], zrecv.at[stage])
        if stage + 2 == STAGES - 2:
            start_along_z(STAGES, lambda t: pg.at[t], lambda t: pz.at[t])
        if stage + 2 < STAGES:
            start_stage(stage + 2)
        if number < 2:
            share_keys(number, rows)
        else:
            share_queries(
                number,
                lambda j, number=number, rows=rows: slabs[number].at[j, :, rows],
                lambda i, number=number, rows=rows: outs[number].at[i, :, rows],
            )
        if stage == STAGES - 2:
            take_bytes(pz, zrecv.at[STAGES])
            share_queries(4, lambda j: pz, lambda i: ph.at[i])
            forward(0)
    forward(1)

    @pl.when(works)
    def _():
        for number, out in enumerate((qh, fh, ph)):
            take_bytes(out, qrecv.at[number])

        for number, out in ((0, kh), (1, vh)):
            theirs = out.at[pl.ds((1 - core) * CHIPS, CHIPS)]
            take_bytes(theirs, frecv.at[number])
            take_bytes(theirs, fsend.at[number])

    for stage in range(STAGES):
        landed = slabs[stage // 2].at[:, pl.ds(0, PLANES - 1), rows_of(stage % 2)]
        take_bytes(landed, zsend.at[stage])
    take_bytes(pz.at[pl.ds(0, PLANES - 1)], zsend.at[STAGES])

    def drain(keys, queries):
        for number, out in ((0, kh), (1, vh)):
            take_bytes(out.at[pl.ds(0, keys)], psend.at[number])
        for number, out in ((2, qh), (3, fh), (4, ph)):
            take_bytes(out.at[pl.ds(0, queries)], psend.at[number])

    @pl.when(works)
    def _():
        drain(WORKERS - 1, HEADS_PLANE - 1)

    @pl.when(jnp.logical_not(works))
    def _():
        drain(WORKERS, HEADS_PLANE)


def bring(keys_in, values, queries, grad_out, fine_gate, coarse_gate):
    keys_shape = jax.ShapeDtypeStruct((2 * CHIPS, PLANES, CUBE, HDIM), BF16)
    query_shape = jax.ShapeDtypeStruct((QGROUPS, PLANES, CUBE, HDIM), BF16)
    pooled_shape = jax.ShapeDtypeStruct((QGROUPS, PLANES, 16, HDIM), BF16)
    anywhere = pl.BlockSpec(memory_space=pl.ANY)
    in_vmem = pl.BlockSpec(memory_space=pltpu.VMEM)
    slab = pltpu.VMEM((HEADS_PLANE, PLANES, CUBE, HDIM), BF16)
    small = pltpu.VMEM((PLANES, 16, HDIM), BF16)
    return pl.pallas_call(
        bring_kernel,
        name="bring",
        out_shape=(keys_shape, keys_shape, query_shape, query_shape, pooled_shape),
        in_specs=[in_vmem] * 2,
        out_specs=[anywhere] * 5,
        scratch_shapes=[
            pltpu.VMEM((4, PLANES, HEADS_PLANE, CUBE, HDIM), BF16),
            slab, slab, slab, slab, small, small,
            pltpu.SemaphoreType.DMA((STAGES + 1,)),
            pltpu.SemaphoreType.DMA((STAGES + 1,)),
            pltpu.SemaphoreType.DMA((5,)),
            pltpu.SemaphoreType.DMA((2, CHIPS)),
            pltpu.SemaphoreType.DMA((3,)),
            pltpu.SemaphoreType.DMA((2,)),
            pltpu.SemaphoreType.DMA((2,)),
        ],
        compiler_params=pltpu.CompilerParams(
            collective_id=0, has_side_effects=True, vmem_limit_bytes=BRING_VMEM
        ),
    )(
        jnp.stack([keys_in, values, queries, grad_out]),
        jnp.concatenate([fine_gate.T, coarse_gate.T], axis=0),
    )


def nt(a, b):
    return lax.dot_general(a, b, (((1,), (1,)), ((), ())), preferred_element_type=F32)


def tn(a, b):
    return lax.dot_general(a, b, (((0,), (0,)), ((), ())), preferred_element_type=F32)


def nn(a, b):
    return jnp.dot(a, b, preferred_element_type=F32)


def attend_kernel(
    toc, sel, q, fg, pg, k, v,
    dq, dk, dv,
    ak, av, wide_0, wide_1, prob_0, prob_1, dsc_0, dsc_1,
    pk, pv, pq, cdq, part_k, part_v, cot, soc, held,
):
    _, chip, core = where_am_i()
    works, head, copy = role_of(chip)
    units = jnp.where(works, UNITS, 0)
    factor = 1.0 / math.sqrt(HDIM)
    log2e = math.log2(math.e)

    def eighths(source, group):
        block = source[pl.ds(pl.multiple_of(group * 8, 8), 8)].astype(F32)
        return jnp.sum(block.reshape(8, 8, 8, HDIM), axis=1).reshape(64, HDIM)

    def prepare(group, _):
        rows = pl.ds(pl.multiple_of(group * 64, 64), 64)
        part_k[rows, :] = eighths(k, group)
        part_v[rows, :] = eighths(v, group)
        for total_of in (ak, av):
            total_of[pl.ds(pl.multiple_of(group * 8, 8), 8)] = jnp.zeros((8, CUBE, HDIM), F32)
        for i in range(8):
            cube = group * 8 + i
            tile = toc[cube]
            cot[tile] = cube
            soc[cube] = (
                lax.shift_left(lax.shift_right_logical(tile, 3) & 1, 7)
                + lax.shift_left(lax.shift_right_logical(tile, 4) & 1, 6)
                + lax.shift_left(tile & 7, 3)
                + lax.shift_right_logical(tile, 5)
            )
        return 0

    lax.fori_loop(0, SLOTS // 8, prepare, 0)

    def pool(part, into):
        count = into.shape[0]
        total = part[pl.ds(0, count, stride=8), :]
        for row in range(1, 8):
            total += part[pl.ds(row, count, stride=8), :]
        into[...] = total * (1.0 / CUBE)

    pool(part_k, pk)
    pool(part_v, pv)

    def prepare_queries(group, _):
        part_k[pl.ds(pl.multiple_of(group * 64, 64), 64), :] = eighths(q, group)
        return 0

    lax.fori_loop(0, QGROUPS, prepare_queries, 0)
    pool(part_k, pq)
    row_at = lax.broadcasted_iota(jnp.int32, (UNITS, 16, HDIM), 1)
    pooled_g = jnp.sum(
        jnp.where(row_at == head, pg[...].astype(F32), 0.0), axis=1
    ).astype(BF16)
    pooled_q = pq[...].astype(BF16)
    pooled_k = pk[...].astype(BF16)
    pooled_v = pv[...].astype(BF16)
    scores = nt(pooled_q, pooled_k) * factor
    weights = jnp.exp(scores - jnp.max(scores, axis=1, keepdims=True))
    probs = weights / jnp.sum(weights, axis=1, keepdims=True)
    dprobs = nt(pooled_g, pooled_v)
    inner = jnp.sum(probs * dprobs, axis=1, keepdims=True)
    dscores = (probs * (dprobs - inner)).astype(BF16)
    cdq[...] = nn(dscores, pooled_k) * (factor / CUBE)
    pk[...] = tn(dscores, pooled_q) * (factor / CUBE)
    pv[...] = tn(probs.astype(BF16), pooled_g) * (1.0 / CUBE)
    wide_0[...] = jnp.zeros_like(wide_0)
    wide_1[...] = jnp.zeros_like(wide_1)

    def listed(n):
        origin = asked_by(head, copy, n // PLANES)
        tile = (n % PLANES * 4 + origin // 8 * 2 + core) * 8 + origin % 8
        cube = cot[tile]
        return [soc[sel[r, cube]] for r in range(TOPK)]

    def beside(ref, lists, c):
        return jnp.concatenate(
            [jnp.concatenate([ref[s] for s in slots[c * 4:c * 4 + 4]], axis=0) for slots in lists],
            axis=1,
        )

    sides = ((prob_0, dsc_0, wide_0), (prob_1, dsc_1, wide_1))

    def advance(old, m_old, new, m_new):
        prob_new, dsc_new, wide_new = sides[new]
        lists_new = [listed(2 * m_new + i) for i in range(2)]
        for i, slots in enumerate(lists_new):
            for r, slot in enumerate(slots):
                held[new, i * TOPK + r] = slot
            rows, lanes = slice(i * CUBE, (i + 1) * CUBE), slice(i * HDIM, (i + 1) * HDIM)
            wide_new[0, rows, lanes] = q[2 * m_new + i]
            wide_new[1, rows, lanes] = fg[2 * m_new + i]
        score, dprob = [], []
        if old is not None:
            prob_old, dsc_old, wide_old = sides[old]
            lists_old = [[held[old, i * TOPK + r] for r in range(TOPK)] for i in range(2)]
            dquery = jnp.zeros((2 * CUBE, 2 * HDIM), F32)
        for c in range(4):
            score.append(nt(beside(k, lists_new, c), wide_new[0]))
            dprob.append(nt(beside(v, lists_new, c), wide_new[1]))
            if old is None:
                continue
            chunk = slice(c * 4 * CUBE, (c + 1) * 4 * CUBE)
            dscore = dsc_old[chunk]
            dquery += tn(dscore, beside(k, lists_old, c))
            key_terms = nn(dscore, wide_old[0])
            value_terms = nn(prob_old[chunk], wide_old[1])
            for i, slots in enumerate(lists_old):
                lanes = slice(i * HDIM, (i + 1) * HDIM)
                for total_of, terms in ((ak, key_terms), (av, value_terms)):
                    before = [total_of[s] for s in slots[c * 4:c * 4 + 4]]
                    for at, s in enumerate(slots[c * 4:c * 4 + 4]):
                        total_of[s] = before[at] + terms[at * CUBE:(at + 1) * CUBE, lanes]
        top = jnp.max(functools.reduce(jnp.maximum, score), axis=0, keepdims=True)
        weight = [jnp.exp2((s - top) * (factor * log2e)) for s in score]
        total = jnp.sum(functools.reduce(jnp.add, weight), axis=0, keepdims=True)
        inverse = 1.0 / total
        mixed = functools.reduce(jnp.add, [w * d for w, d in zip(weight, dprob)])
        center = jnp.sum(mixed, axis=0, keepdims=True) * inverse
        for c in range(4):
            chunk = slice(c * 4 * CUBE, (c + 1) * 4 * CUBE)
            prob = weight[c] * inverse
            prob_new[chunk] = prob.astype(BF16)
            dsc_new[chunk] = (prob * (dprob[c] - center)).astype(BF16)
        if old is not None:
            for i in range(2):
                n = 2 * m_old + i
                mine = dquery[i * CUBE:(i + 1) * CUBE, i * HDIM:(i + 1) * HDIM]
                dq[n] = (mine * factor + cdq[pl.ds(n, 1), :]).astype(BF16)

    advance(None, 0, 0, 0)

    def two_pairs(m, _):
        advance(0, 2 * m, 1, 2 * m + 1)
        advance(1, 2 * m + 1, 0, jnp.minimum(2 * m + 2, UNITS // 2 - 1))
        return 0

    lax.fori_loop(0, units // 4, two_pairs, 0)

    def finish(group, _):
        for i in range(4):
            slot = group * 4 + i
            dk[slot] = (ak[slot] * factor + pk[pl.ds(slot, 1), :]).astype(BF16)
            dv[slot] = (av[slot] + pv[pl.ds(slot, 1), :]).astype(BF16)
        return 0

    lax.fori_loop(0, SLOTS // 4, finish, 0)


def attend(tile_of_cube, select, qh, fh, ph, kh, vh):
    smem = pl.BlockSpec(memory_space=pltpu.SMEM)
    vmem = pl.BlockSpec(memory_space=pltpu.VMEM)
    query_shape = jax.ShapeDtypeStruct((UNITS, CUBE, HDIM), BF16)
    keys_shape = jax.ShapeDtypeStruct((SLOTS, CUBE, HDIM), BF16)
    return pl.pallas_call(
        attend_kernel,
        name="attend",
        out_shape=(query_shape, keys_shape, keys_shape),
        in_specs=[smem] * 2 + [vmem] * 5,
        out_specs=[vmem] * 3,
        scratch_shapes=[
            pltpu.VMEM((SLOTS, CUBE, HDIM), F32),
            pltpu.VMEM((SLOTS, CUBE, HDIM), F32),
            pltpu.VMEM((2, 2 * CUBE, 2 * HDIM), BF16),
            pltpu.VMEM((2, 2 * CUBE, 2 * HDIM), BF16),
            pltpu.VMEM((TOPK * CUBE, 2 * CUBE), BF16),
            pltpu.VMEM((TOPK * CUBE, 2 * CUBE), BF16),
            pltpu.VMEM((TOPK * CUBE, 2 * CUBE), BF16),
            pltpu.VMEM((TOPK * CUBE, 2 * CUBE), BF16),
            pltpu.VMEM((SLOTS, HDIM), F32),
            pltpu.VMEM((SLOTS, HDIM), F32),
            pltpu.VMEM((UNITS, HDIM), F32),
            pltpu.VMEM((UNITS, HDIM), F32),
            pltpu.VMEM((SLOTS * 8, HDIM), F32),
            pltpu.VMEM((SLOTS * 8, HDIM), F32),
            pltpu.SMEM((SLOTS,), jnp.int32),
            pltpu.SMEM((SLOTS,), jnp.int32),
            pltpu.SMEM((2, 2 * TOPK), jnp.int32),
        ],
        compiler_params=pltpu.CompilerParams(vmem_limit_bytes=ATTEND_VMEM),
    )(
        tile_of_cube, select.T,
        qh.reshape(UNITS, CUBE, HDIM), fh.reshape(UNITS, CUBE, HDIM),
        ph.reshape(UNITS, 16, HDIM), kh.reshape(SLOTS, CUBE, HDIM), vh.reshape(SLOTS, CUBE, HDIM),
    )


def home_kernel(
    dq, dk, dv,
    grads,
    own_k, own_v, sib_k, sib_v, land_q, land_k, land_v, sum_k, sum_v, sum_q,
    ssend, srecv, psend, precv, zsend, zrecv,
):
    plane, chip, core = where_am_i()
    works, head, replica = role_of(chip)
    greet(plane, chip, core)
    sibling = device_of(plane, chip, 1 - core)
    oq, ok, ov = grads.at[0], grads.at[1], grads.at[2]
    sources, owns, sibs = (dk, dv), (own_k, own_v), (sib_k, sib_v)
    lands, sums, outs = (land_k, land_v), (sum_k, sum_v), (ok, ov)
    mine = columns(plane)

    @pl.when(works)
    def _():
        for number in range(2):
            def give(d, _, number=number):
                target = (chip + d) % CHIPS
                remote(
                    sources[number].at[(1 - core) * CHIPS + target], sibs[number].at[target],
                    ssend.at[number], srecv.at[number, target], sibling,
                ).start()
                return 0

            lax.fori_loop(0, CHIPS, give, 0)

        def send_query(m, _):
            i = (m + chip) % QGROUPS
            target = asked_by(head, replica, i)

            @pl.when(target != chip)
            def _():
                remote(
                    dq.at[i], land_q.at[head], psend.at[2], precv.at[4],
                    device_of(plane, target, core),
                ).start()

            @pl.when(target == chip)
            def _():
                pltpu.make_async_copy(dq.at[i], land_q.at[head], precv.at[4]).start()

            return 0

        lax.fori_loop(0, QGROUPS, send_query, 0)

    def settle(number, half):
        rows = rows_of(half)
        source, own, sib, land = sources[number], owns[number], sibs[number], lands[number]

        def step(d, _):
            target = (chip + d) % CHIPS
            if half == 0:
                take_bytes(sib.at[target], srecv.at[number, target])
            own[target, :, rows] = (
                source[core * CHIPS + target, :, rows].astype(F32)
                + sib[target, :, rows].astype(F32)
            ).astype(BF16)
            arrived = precv.at[number * 2 + half]

            @pl.when(target != chip)
            def _():
                remote(
                    own.at[target, :, rows], land.at[replica, head, :, rows], psend.at[number],
                    arrived, device_of(plane, target, core),
                ).start()

            @pl.when(target == chip)
            def _():
                pltpu.make_async_copy(
                    own.at[target, :, rows], land.at[replica, head, :, rows], arrived
                ).start()

            return 0

        @pl.when(works)
        def _():
            lax.fori_loop(0, CHIPS, step, 0)

    def send_home(number, block, out, target):
        @pl.when(target != plane)
        def _():
            remote(
                block, out, zsend.at[number], zrecv.at[number], device_of(target, chip, core)
            ).start()

        @pl.when(target == plane)
        def _():
            pltpu.make_async_copy(block, out, zrecv.at[number]).start()

    def queries_home():
        take_bytes(land_q, precv.at[4])

        def step(d, _):
            target = (plane + d) % PLANES
            for j in range(HEADS_PLANE):
                sum_q[target, :, j * HDIM:(j + 1) * HDIM] = land_q[j, target]
            send_home(2, sum_q.at[target], oq.at[:, mine], target)
            return 0

        lax.fori_loop(0, PLANES, step, 0)

    def keys_home(number, half):
        rows = rows_of(half)
        land, total, out = lands[number], sums[number], outs[number]
        take_bytes(land.at[:, :, :, rows], precv.at[number * 2 + half])

        def step(d, _):
            target = (plane + d) % PLANES
            for j in range(HEADS_PLANE):
                summed = land[0, j, target, rows].astype(F32)
                for r in range(1, COPIES):
                    summed += land[r, j, target, rows].astype(F32)
                total[target, rows, j * HDIM:(j + 1) * HDIM] = summed.astype(BF16)
            send_home(number, total.at[target, rows], out.at[rows, mine], target)
            return 0

        lax.fori_loop(0, PLANES, step, 0)

    settle(0, 0)
    settle(0, 1)
    queries_home()
    keys_home(0, 0)
    settle(1, 0)
    keys_home(0, 1)
    settle(1, 1)
    keys_home(1, 0)
    keys_home(1, 1)

    for number, out in enumerate((ok, ov, oq)):
        take_bytes(out, zrecv.at[number])
        take_bytes(sum_q.at[pl.ds(0, PLANES - 1)], zsend.at[number])

    @pl.when(works)
    def _():
        for number in range(2):
            take_bytes(sibs[number], ssend.at[number])
            take_bytes(owns[number].at[pl.ds(0, CHIPS - 1)], psend.at[number])

        take_bytes(dq.at[pl.ds(0, QGROUPS - 1)], psend.at[2])


def home(dq, dk, dv, rows, width):
    anywhere = pl.BlockSpec(memory_space=pl.ANY)
    in_vmem = pl.BlockSpec(memory_space=pltpu.VMEM)
    out_shape = jax.ShapeDtypeStruct((3, rows, width), BF16)
    half = pltpu.VMEM((CHIPS, PLANES, CUBE, HDIM), BF16)
    slab = pltpu.VMEM((PLANES, CUBE, WIDTH), BF16)
    by_head = pltpu.VMEM((HEADS_PLANE, PLANES, CUBE, HDIM), BF16)
    copies = pltpu.VMEM((COPIES, HEADS_PLANE, PLANES, CUBE, HDIM), BF16)
    return pl.pallas_call(
        home_kernel,
        name="home",
        out_shape=out_shape,
        in_specs=[anywhere, in_vmem, in_vmem],
        out_specs=anywhere,
        scratch_shapes=[
            half, half, half, half, by_head, copies, copies, slab, slab, slab,
            pltpu.SemaphoreType.DMA((2,)),
            pltpu.SemaphoreType.DMA((2, CHIPS)),
            pltpu.SemaphoreType.DMA((3,)),
            pltpu.SemaphoreType.DMA((5,)),
            pltpu.SemaphoreType.DMA((3,)),
            pltpu.SemaphoreType.DMA((3,)),
        ],
        compiler_params=pltpu.CompilerParams(
            collective_id=1, has_side_effects=True, vmem_limit_bytes=HOME_VMEM
        ),
    )(
        dq.reshape(QGROUPS, PLANES, CUBE, HDIM),
        dk.reshape(2 * CHIPS, PLANES, CUBE, HDIM),
        dv.reshape(2 * CHIPS, PLANES, CUBE, HDIM),
    )


def on_device(queries, keys_in, values, grad_out, fine_gate, coarse_gate, tile_of_cube, select):
    kh, vh, qh, fh, ph = bring(keys_in, values, queries, grad_out, fine_gate, coarse_gate)
    dq, dk, dv = attend(tile_of_cube, select, qh, fh, ph, kh, vh)
    grads = home(dq, dk, dv, *queries.shape)
    return grads[0], grads[1], grads[2]


def solution(mesh):
    split = P(("tok", "head"), None)
    return jax.shard_map(
        on_device,
        mesh=mesh,
        in_specs=(split,) * 6 + (P(), P()),
        out_specs=(split,) * 3,
        check_vma=False,
    )
```
